32 devices in a mesh: seq: 8 (over z, core), batch: 4 (over y, x).
Axes of the slice: x: 2, y: 2, z: 4, core: 2. Of those that a mesh axis runs over, the one named last changes fastest.
Arguments:
- tokens: bfloat16 [8, 1024, 1024], P('batch', 'seq'), may hold values from -6 to 6
- cotangent: bfloat16 [8, 1024, 1024], P('batch', 'seq'), may hold values from -6 to 6
- ln_gain: float32 [1024], replicated, may hold values from 0.5 to 1.5
- ln_bias: float32 [1024], replicated, may hold values from -3 to 3
- w_in: bfloat16 [1024, 3072], replicated, may hold values from -0.1875 to 0.1875
- b_in: float32 [3072], replicated, may hold values from -3 to 3
- short_w: float32 [3, 3072], replicated, may hold values from -4 to 4
- short_b: float32 [3072], replicated, may hold values from -3 to 3
- w_one: float32 [33, 64], replicated, may hold values from -1 to 1
- b_one: float32 [64], replicated, may hold values from -3.140625 to 3.140625
- w_two: float32 [64, 64], replicated, may hold values from -0.75 to 0.75
- b_two: float32 [64], replicated, may hold values from -3 to 3
- w_three: float32 [64, 1024], replicated, may hold values from -0.046875 to 0.046875
- decay_rates: float32 [1024], replicated, may hold values from 0.5 to 200
- filt_bias: float32 [1024], replicated, may hold values from -4 to 4
- w_out: bfloat16 [1024, 1024], replicated, may hold values from -0.1875 to 0.1875
- b_out: float32 [1024], replicated, may hold values from -3 to 3
Outputs:
- block_out: bfloat16 [8, 1024, 1024], P('batch', 'seq')
- grad_tokens: float32 [8, 1024, 1024], P('batch', 'seq')
- grad_ln_gain: float32 [1024], P(('seq', 'batch'))
- grad_ln_bias: float32 [1024], P(('seq', 'batch'))
- grad_w_in: float32 [1024, 3072], P(('seq', 'batch'))
- grad_b_in: float32 [3072], P(('seq', 'batch'))
- grad_short_w: float32 [3, 3072], P(None, ('seq', 'batch'))
- grad_short_b: float32 [3072], P(('seq', 'batch'))
- grad_w_one: float32 [33, 64], replicated
- grad_b_one: float32 [64], replicated
- grad_w_two: float32 [64, 64], replicated
- grad_b_two: float32 [64], replicated
- grad_w_three: float32 [64, 1024], P(None, ('seq', 'batch'))
- grad_filt_bias: float32 [1024], P(('seq', 'batch'))
- grad_w_out: float32 [1024, 1024], P(('seq', 'batch'))
- grad_b_out: float32 [1024], P(('seq', 'batch'))
The draws below stay inside these ranges and needn't reach their ends.
All inputs are finite; a program needn't handle non-finite values.
Results may differ from the reference program's by a relative error of at most 0.024.
Values may be sent and summed in bfloat16 or wider, within the bound.
A program may use at most 128 MiB of HBM per device.

```python
import math
import jax
import jax.numpy as jnp
from jax import lax

D = 1024
FH = 64
EMB = 33
SEQS = 8
LEN = 1024


def shard_levels(own_key, shape, shards, least, largest):
    level, own = 1.0, jax.random.fold_in(own_key, 6)
    for axis_at, shards_of in shards:
        steps = jnp.exp(jax.random.uniform(jax.random.fold_in(own, axis_at), (shards_of,), jnp.float32, least / len(shards), largest / len(shards)))
        level = level * jnp.repeat(steps, shape[axis_at] // shards_of).reshape([-1 if axis == axis_at else 1 for axis in range(len(shape))])
    return level


def bell_draw(key, shape, spread, most, cuts=(), kind=jnp.bfloat16):
    level = shard_levels(key, shape, cuts, -0.22, 0.18) if cuts else 1.0
    drawn = jax.random.normal(key, shape, jnp.float32) * spread * level
    return jnp.minimum(jnp.maximum(drawn, -most), most).astype(kind)


def setup_inputs(seed: int = 0) -> dict:
    keys = jax.random.split(jax.random.key(seed), 18)
    tokens = bell_draw(keys[0], (SEQS, LEN, D), 1.0, 6.0, ((0, 4), (1, 8)))
    cotangent = bell_draw(keys[1], (SEQS, LEN, D), 1.0, 6.0, ((0, 4), (1, 8)))
    ln_gain = jnp.clip(1.0 + 0.1 * jax.random.normal(keys[2], (D,), jnp.float32), 0.5, 1.5)
    ln_bias = bell_draw(keys[3], (D,), 0.3, 3.0, (), jnp.float32)
    w_in = bell_draw(keys[4], (D, 3 * D), D ** -0.5, 0.1875)
    b_in = bell_draw(keys[5], (3 * D,), 0.3, 3.0, (), jnp.float32)
    short_w = bell_draw(keys[6], (3, 3 * D), 0.6, 4.0, (), jnp.float32)
    short_b = bell_draw(keys[7], (3 * D,), 0.3, 3.0, (), jnp.float32)
    w_one = bell_draw(keys[8], (EMB, FH), EMB ** -0.5, 1.0, (), jnp.float32)
    b_one = jnp.clip(jax.random.uniform(keys[9], (FH,), jnp.float32, -3.140625, 3.140625), -3.140625, 3.140625)
    w_two = bell_draw(keys[10], (FH, FH), FH ** -0.5, 0.75, (), jnp.float32)
    b_two = bell_draw(keys[11], (FH,), 0.5, 3.0, (), jnp.float32)
    w_three = bell_draw(keys[12], (FH, D), (16 * LEN) ** -0.5, 0.046875, (), jnp.float32)
    decay_rates = jnp.clip(jnp.exp(jax.random.uniform(keys[13], (D,), jnp.float32, math.log(0.5), math.log(200.0))), 0.5, 200.0)
    filt_bias = bell_draw(keys[14], (D,), 1.0, 4.0, (), jnp.float32)
    w_out = bell_draw(keys[15], (D, D), D ** -0.5, 0.1875)
    b_out = bell_draw(keys[16], (D,), 0.3, 3.0, (), jnp.float32)
    return {"tokens": tokens, "cotangent": cotangent, "ln_gain": ln_gain, "ln_bias": ln_bias, "w_in": w_in, "b_in": b_in, "short_w": short_w, "short_b": short_b, "w_one": w_one, "b_one": b_one, "w_two": w_two, "b_two": b_two, "w_three": w_three, "decay_rates": decay_rates, "filt_bias": filt_bias, "w_out": w_out, "b_out": b_out}


@jax.custom_vjp
def low(v):
    return lax.optimization_barrier(v.astype(jnp.bfloat16)).astype(jnp.float32)

@jax.custom_vjp
def low_back(v):
    return v

def low_keep(v):
    return (low(v), None)

def low_pass(kept, grad):
    return (grad,)

def back_keep(v):
    return (v, None)

def back_low(kept, grad):
    return (low(grad),)
low.defvjp(low_keep, low_pass)
low_back.defvjp(back_keep, back_low)
highest = lax.Precision.HIGHEST
epsilon = 1e-05

def position_features(length, features):
    step_axis = jnp.arange(length).astype(jnp.float32)
    band_count = (features - 1) // 2
    band_rates = 0.0001 + jnp.arange(band_count).astype(jnp.float32) * (band_count - 1 - 0.0001) / (band_count - 1)
    phases = 2.0 * jnp.pi / length * step_axis[:, None] * band_rates[None, :]
    return jnp.concatenate([(step_axis / length)[:, None], jnp.cos(phases), -jnp.sin(phases)], axis=1)

def filter_shape(positions, w_one, b_one, w_two, b_two, w_three, decay_rates):
    first_layer = jnp.sin(jnp.dot(positions, w_one, precision=highest) + b_one)
    second_layer = jnp.sin(jnp.dot(first_layer, w_two, precision=highest) + b_two)
    shaped = jnp.dot(second_layer, w_three, precision=highest)
    length = positions.shape[0]
    fraction = jnp.arange(length).astype(jnp.float32) / length
    return shaped * jnp.exp(-fraction[:, None] * decay_rates[None, :])

def block_forward(params, decay_rates, positions, inputs):
    ln_gain, ln_bias, w_in, b_in, short_w, short_b, w_one, b_one, w_two, b_two, w_three, filt_bias, w_out, b_out = params
    length = inputs.shape[1]
    model_width = inputs.shape[2]
    average = lax.optimization_barrier(jnp.mean(inputs, axis=-1, keepdims=True))
    centered = inputs - average
    variance = lax.optimization_barrier(jnp.mean(centered * centered, axis=-1, keepdims=True))
    normed = low(centered * lax.rsqrt(variance + epsilon) * ln_gain + ln_bias)
    mixed = low_back(jnp.einsum('gtd,de->gte', normed, w_in, precision=highest) + b_in)
    padded = jnp.pad(mixed, ((0, 0), (2, 0), (0, 0)))
    short_out = short_w[0] * mixed + short_w[1] * padded[:, 1:-1] + short_w[2] * padded[:, :-2] + short_b
    outer_gate = short_out[..., :model_width]
    inner_gate = short_out[..., model_width:2 * model_width]
    values = short_out[..., 2 * model_width:]
    gated = low(low_back(values * inner_gate))
    kernel = low(filter_shape(positions, w_one, b_one, w_two, b_two, w_three, decay_rates))
    spectra = jnp.fft.rfft(gated, n=2 * length, axis=1) * jnp.fft.rfft(kernel, n=2 * length, axis=0)[None]
    long_out = jnp.fft.irfft(spectra, n=2 * length, axis=1)[:, :length]
    summed = low(low_back(long_out + filt_bias * gated))
    product = low(low_back(summed * outer_gate))
    return inputs + jnp.einsum('gtd,de->gte', product, w_out, precision=highest) + b_out

def reference(tokens, cotangent, ln_gain, ln_bias, w_in, b_in, short_w, short_b, w_one, b_one, w_two, b_two, w_three, decay_rates, filt_bias, w_out, b_out):
    params = (ln_gain, ln_bias, w_in.astype(jnp.float32), b_in, short_w, short_b, w_one, b_one, w_two, b_two, w_three, filt_bias, w_out.astype(jnp.float32), b_out)
    positions = position_features(LEN, EMB)
    group_size = 2
    token_groups = tokens.astype(jnp.float32).reshape(SEQS // group_size, group_size, LEN, D)
    grad_groups = cotangent.astype(jnp.float32).reshape(SEQS // group_size, group_size, LEN, D)

    def forward_of(weights, inputs):
        return block_forward(weights, decay_rates, positions, inputs)

    def one_group(running, members):
        inputs, grads = members
        outputs, pull = jax.vjp(forward_of, params, inputs)
        grad_params, grad_inputs = pull(grads)
        return (jax.tree.map(jnp.add, running, grad_params), (outputs.astype(jnp.bfloat16), grad_inputs))
    start_sums = jax.tree.map(jnp.zeros_like, params)
    totals, (outputs, grad_inputs) = lax.scan(one_group, start_sums, (token_groups, grad_groups))
    return (outputs.reshape(SEQS, LEN, D), grad_inputs.reshape(SEQS, LEN, D), totals[0], totals[1], totals[2], totals[3], totals[4], totals[5], totals[6], totals[7], totals[8], totals[9], totals[10], totals[11], totals[12], totals[13])
```

```python
import jax
import jax.numpy as jnp
import numpy as np
from jax import lax
from jax.sharding import PartitionSpec as P

highest = lax.Precision.HIGHEST
epsilon = 1e-05
f32, bf16 = jnp.float32, jnp.bfloat16


def dft_matrix(length):
    turns = ((2 * np.arange(length)[:, None] + 1) * np.arange(length)[None, :]) % (4 * length)
    phases = turns * (np.pi / (2 * length))
    return np.concatenate([np.cos(phases), np.sin(phases)], axis=0).astype(bf16)


def position_features(length, features):
    step_axis = np.arange(length, dtype=np.float64)
    band_count = (features - 1) // 2
    band_rates = 0.0001 + np.arange(band_count) * (band_count - 1 - 0.0001) / (band_count - 1)
    phases = 2.0 * np.pi / length * step_axis[:, None] * band_rates[None, :]
    return np.concatenate(
        [(step_axis / length)[:, None], np.cos(phases), -np.sin(phases)], axis=1
    ).astype(np.float32)


def filter_shape(positions, w_one, b_one, w_two, b_two, w_three, decay_rates):
    first_layer = jnp.sin(jnp.dot(positions, w_one, precision=highest) + b_one)
    second_layer = jnp.sin(jnp.dot(first_layer, w_two, precision=highest) + b_two)
    shaped = jnp.dot(second_layer, w_three, precision=highest)
    length = positions.shape[0]
    fraction = jnp.arange(length).astype(f32) / length
    return shaped * jnp.exp(-fraction[:, None] * decay_rates[None, :])


def shifted(value, axis, steps):
    count = lax.axis_size(axis)
    first, last = (max(0, -steps), min(count, count - steps))
    return lax.ppermute(value, axis, [(source, source + steps) for source in range(first, last)])


def reduce_scatter(value, dtype):
    out = lax.all_to_all(value.astype(dtype), "batch", split_axis=1, concat_axis=1, tiled=True)
    out = jnp.sum(out.astype(f32), axis=1)
    out = lax.all_to_all(out.astype(dtype), "seq", split_axis=0, concat_axis=0, tiled=True)
    return jnp.sum(out.astype(f32), axis=0)


def local(
    tokens,
    cotangent,
    ln_gain,
    ln_bias,
    w_in,
    b_in,
    short_w,
    short_b,
    w_one,
    b_one,
    w_two,
    b_two,
    w_three,
    decay_rates,
    filt_bias,
    w_out,
    b_out,
):
    seq_count, block_len, model_width = tokens.shape
    seq_devices = lax.axis_size("seq")
    batch_devices = lax.axis_size("batch")
    devices = seq_devices * batch_devices
    length = block_len * seq_devices
    channels = model_width // seq_devices
    col_start = lax.axis_index("seq") * channels
    inputs = tokens.astype(f32)
    average = jnp.mean(inputs, axis=-1, keepdims=True)
    centered = inputs - average
    inv_std = lax.rsqrt(jnp.mean(centered * centered, axis=-1, keepdims=True) + epsilon)
    whitened = centered * inv_std
    normed = (whitened * ln_gain + ln_bias).astype(bf16)
    mixed = jnp.einsum("btd,de->bte", normed, w_in, preferred_element_type=f32) + b_in
    prev_rows = shifted(mixed[:, block_len - 2 :], "seq", 1)
    padded = jnp.concatenate([prev_rows, mixed], axis=1)
    delay_one = padded[:, 1:-1]
    delay_two = padded[:, :-2]
    short_out = short_w[0] * mixed + short_w[1] * delay_one + short_w[2] * delay_two + short_b
    outer_gate = short_out[..., :model_width]
    inner_gate = short_out[..., model_width : 2 * model_width]
    values = short_out[..., 2 * model_width :]
    gated = (values * inner_gate).astype(bf16)
    d_product = jnp.einsum(
        "bte,de->btd", cotangent, w_out, preferred_element_type=f32
    ).astype(bf16)
    d_prod_f = d_product.astype(f32)
    d_summed = (d_prod_f * outer_gate).astype(bf16)

    def to_channels(value):
        return lax.all_to_all(value, "seq", split_axis=2, concat_axis=1, tiled=True)

    def to_tokens(value):
        return lax.all_to_all(value, "seq", split_axis=1, concat_axis=2, tiled=True)

    gated_ch = to_channels(gated)
    d_ch = to_channels(d_summed)
    positions = jnp.asarray(position_features(length, w_one.shape[0]))
    w_three_part = lax.dynamic_slice_in_dim(w_three, col_start, channels, 1)
    decay_part = lax.dynamic_slice_in_dim(decay_rates, col_start, channels, 0)
    bias_part = lax.dynamic_slice_in_dim(filt_bias, col_start, channels, 0)

    def kernel_of(first_w, first_b, second_w, second_b, third_w):
        return filter_shape(positions, first_w, first_b, second_w, second_b, third_w, decay_part)

    kernel_full, kernel_pull = jax.vjp(kernel_of, w_one, b_one, w_two, b_two, w_three_part)
    matrix = jnp.asarray(dft_matrix(length))

    def spectrum(value):
        return jnp.einsum("kt,btc->bkc", matrix, value, preferred_element_type=f32)

    def inverse(cosines, sines):
        both = jnp.concatenate([cosines, sines], axis=1).astype(bf16)
        return jnp.einsum("kt,bkc->btc", matrix, both, preferred_element_type=f32) * (1.0 / length)

    k_both = spectrum(kernel_full.astype(bf16)[None])
    g_both = spectrum(gated_ch)
    d_both = spectrum(d_ch)
    k_c, k_s = k_both[:, :length], k_both[:, length:]
    g_c, g_s = g_both[:, :length], g_both[:, length:]
    d_c, d_s = d_both[:, :length], d_both[:, length:]
    long_out = inverse(g_c * k_c - g_s * k_s, g_c * k_s + g_s * k_c)
    gated_float = gated_ch.astype(f32)
    d_ch_float = d_ch.astype(f32)
    summed_ch = (long_out + bias_part * gated_float).astype(bf16)
    summed = to_tokens(summed_ch).astype(f32)
    grad_in = inverse(k_c * d_c + k_s * d_s, k_c * d_s - k_s * d_c) + bias_part * d_ch_float
    d_gated = to_tokens(grad_in.astype(bf16)).astype(f32)
    d_kernel = inverse(
        jnp.sum(g_c * d_c + g_s * d_s, axis=0, keepdims=True),
        jnp.sum(g_c * d_s - g_s * d_c, axis=0, keepdims=True),
    )[0]
    g_bias_part = jnp.sum(d_ch_float * gated_float, axis=(0, 1))
    g_w_one, g_b_one, g_w_two, g_b_two, g_w_three_part = kernel_pull(d_kernel)

    product = (summed * outer_gate).astype(bf16)
    result = jnp.einsum("btd,de->bte", product, w_out, preferred_element_type=f32) + b_out
    block_out = (inputs + result).astype(bf16)
    grad_out = cotangent.astype(f32)
    g_w_out = jnp.einsum("btd,bte->de", product, cotangent, preferred_element_type=f32)
    g_b_out = jnp.sum(grad_out, axis=(0, 1))
    d_outer = d_prod_f * summed
    d_short = jnp.concatenate([d_outer, d_gated * values, d_gated * inner_gate], axis=-1)
    g_short_w = jnp.stack(
        [
            jnp.sum(d_short * mixed, axis=(0, 1)),
            jnp.sum(d_short * delay_one, axis=(0, 1)),
            jnp.sum(d_short * delay_two, axis=(0, 1)),
        ]
    )
    g_short_b = jnp.sum(d_short, axis=(0, 1))
    next_rows = shifted(d_short[:, :2], "seq", -1)
    extended = jnp.concatenate([d_short, next_rows], axis=1)
    d_mixed = (
        short_w[0] * extended[:, :block_len]
        + short_w[1] * extended[:, 1 : block_len + 1]
        + short_w[2] * extended[:, 2:]
    ).astype(bf16)
    g_w_in = jnp.einsum("btd,bte->de", normed, d_mixed, preferred_element_type=f32)
    g_b_in = jnp.sum(d_mixed.astype(f32), axis=(0, 1))
    d_normed = jnp.einsum("bte,de->btd", d_mixed, w_in, preferred_element_type=f32)
    g_ln_gain = jnp.sum(d_normed * whitened, axis=(0, 1))
    g_ln_bias = jnp.sum(d_normed, axis=(0, 1))
    d_white = d_normed * ln_gain
    grad_tokens = grad_out + inv_std * (
        d_white
        - jnp.mean(d_white, axis=-1, keepdims=True)
        - whitened * jnp.mean(d_white * whitened, axis=-1, keepdims=True)
    )
    rows = model_width // devices
    big = jnp.concatenate([g_w_in, g_w_out], axis=1)
    big = reduce_scatter(big.reshape(seq_devices, batch_devices, rows, -1), bf16)
    out_w_in, out_w_out = big[:, : 3 * model_width], big[:, 3 * model_width :]
    g_w_three = lax.dynamic_update_slice_in_dim(
        jnp.zeros(w_three.shape, f32), g_w_three_part, col_start, 1
    )
    g_filt_bias = lax.dynamic_update_slice_in_dim(
        jnp.zeros(filt_bias.shape, f32), g_bias_part, col_start, 0
    )
    vectors = jnp.concatenate(
        [
            g_ln_gain[None],
            g_ln_bias[None],
            g_b_out[None],
            g_filt_bias[None],
            g_w_three,
        ],
        axis=0,
    )
    vectors = jnp.transpose(vectors.reshape(-1, devices, rows), (1, 0, 2)).reshape(devices, -1)
    wides = jnp.concatenate([g_b_in[None], g_short_w, g_short_b[None]], axis=0)
    wides = jnp.transpose(wides.reshape(-1, devices, 3 * rows), (1, 0, 2)).reshape(devices, -1)
    net = jnp.concatenate([v.reshape(-1) for v in (g_w_one, g_b_one, g_w_two, g_b_two)])
    net_size = net.shape[0]
    net_part = -(-net_size // devices)
    net = jnp.pad(net, (0, net_part * devices - net_size)).reshape(devices, net_part)
    small = jnp.concatenate([vectors, wides, net], axis=1)
    small = reduce_scatter(small.reshape(seq_devices, batch_devices, -1), f32)
    hidden = w_two.shape[0]
    cut = rows * (4 + hidden)
    vectors = small[:cut].reshape(4 + hidden, rows)
    wides = small[cut : cut + 15 * rows].reshape(5, 3 * rows)
    net = lax.all_gather(small[cut + 15 * rows :], ("seq", "batch"), tiled=True)
    features = w_one.shape[0]
    edges = [features * hidden, (features + 1) * hidden, (features + 1 + hidden) * hidden]
    return (
        block_out,
        grad_tokens,
        vectors[0],
        vectors[1],
        out_w_in,
        wides[0],
        wides[1:4],
        wides[4],
        net[: edges[0]].reshape(features, hidden),
        net[edges[0] : edges[1]],
        net[edges[1] : edges[2]].reshape(hidden, hidden),
        net[edges[2] : net_size],
        vectors[4:],
        vectors[3],
        out_w_out,
        vectors[2],
    )


def solution(mesh):
    tokens_spec = P("batch", "seq", None)
    both = ("seq", "batch")
    in_specs = (tokens_spec, tokens_spec) + (P(),) * 15
    out_specs = (
        tokens_spec,
        tokens_spec,
        P(both),
        P(both),
        P(both, None),
        P(both),
        P(None, both),
        P(both),
        P(),
        P(),
        P(),
        P(),
        P(None, both),
        P(both),
        P(both, None),
        P(both),
    )
    return jax.shard_map(local, mesh=mesh, in_specs=in_specs, out_specs=out_specs, check_vma=False)
```

```python
import functools

import jax
import jax.numpy as jnp
import numpy as np
from jax import lax
from jax.experimental import pallas as pl
from jax.experimental.pallas import tpu as pltpu
from jax.sharding import PartitionSpec as P

highest = lax.Precision.HIGHEST
epsilon = 1e-05
f32, bf16 = jnp.float32, jnp.bfloat16


def dft_matrix(length):
    turns = ((2 * np.arange(length)[:, None] + 1) * np.arange(length)[None, :]) % (4 * length)
    phases = turns * (np.pi / (2 * length))
    return np.concatenate([np.cos(phases), np.sin(phases)], axis=0).astype(bf16)


def position_features(length, features):
    step_axis = np.arange(length, dtype=np.float64)
    band_count = (features - 1) // 2
    band_rates = 0.0001 + np.arange(band_count) * (band_count - 1 - 0.0001) / (band_count - 1)
    phases = 2.0 * np.pi / length * step_axis[:, None] * band_rates[None, :]
    return np.concatenate(
        [(step_axis / length)[:, None], np.cos(phases), -np.sin(phases)], axis=1
    ).astype(np.float32)


def filter_shape(positions, w_one, b_one, w_two, b_two, w_three, decay_rates):
    first_layer = jnp.sin(jnp.dot(positions, w_one, precision=highest) + b_one)
    second_layer = jnp.sin(jnp.dot(first_layer, w_two, precision=highest) + b_two)
    shaped = jnp.dot(second_layer, w_three, precision=highest)
    length = positions.shape[0]
    fraction = jnp.arange(length).astype(f32) / length
    return shaped * jnp.exp(-fraction[:, None] * decay_rates[None, :])


def shifted(value, axis, steps):
    count = lax.axis_size(axis)
    first, last = (max(0, -steps), min(count, count - steps))
    return lax.ppermute(value, axis, [(source, source + steps) for source in range(first, last)])


def reduce_scatter(value, dtype):
    out = lax.all_to_all(value.astype(dtype), "batch", split_axis=1, concat_axis=1, tiled=True)
    out = jnp.sum(out.astype(f32), axis=1)
    out = lax.all_to_all(out.astype(dtype), "seq", split_axis=0, concat_axis=0, tiled=True)
    return jnp.sum(out.astype(f32), axis=0)

MESH = pl.DeviceIdType.MESH


def back_kernel(
    nt_ref,
    pt_ref,
    dm_ref,
    cot_ref,
    sa_ref,
    sb_ref,
    win_ref,
    wout_ref,
    oa_ref,
    ob_ref,
    nt,
    pt,
    dm,
    cot,
    core_send,
    core_recv,
    core_send_o,
    core_recv_o,
    z_send,
    z_recv,
    z_send_o,
    z_recv_o,
    own,
    last_send,
    last_recv,
    sa,
    sb,
    b_sem,
    c_sem,
    zed_sem,
    l_sem,
    s_sem,
):
    s, b = lax.axis_index("seq"), lax.axis_index("batch")
    zed, core = s // 2, s % 2
    other = (zed * 2 + 1 - core, b)

    def batch_peer(p):
        return (s, (b + p) % 4)

    def zed_peer(p):
        return (((zed + p) % 4) * 2 + core, b)

    barrier = pltpu.get_barrier_semaphore()
    peers = [other] + [batch_peer(p) for p in (1, 2, 3)] + [zed_peer(p) for p in (1, 2, 3)]
    for peer in peers:
        pl.semaphore_signal(barrier, inc=1, device_id=peer, device_id_type=MESH)
    pl.semaphore_wait(barrier, 7)

    def remote(src, dst, sems, index, peer):
        copy = pltpu.make_async_remote_copy(
            src_ref=src,
            dst_ref=dst,
            send_sem=sems.at[(0,) + index],
            recv_sem=sems.at[(1,) + index],
            device_id=peer,
            device_id_type=MESH,
        )
        copy.start()
        return copy

    moves = {}
    for p in (1, 2, 3):
        peer, to = batch_peer(p), (b + p) % 4
        moves["n", p] = remote(nt_ref, nt.at[b], b_sem, (0, p), peer)
        moves["c", p] = remote(cot_ref, cot.at[b], b_sem, (1, p), peer)
        for half in range(2):
            moves["p", half, p] = remote(
                pt_ref.at[:, half, to], pt.at[b, half], b_sem, (2 + half, p), peer
            )
        for g in range(3):
            moves["d", g, p] = remote(dm_ref.at[g, to], dm.at[g, b], b_sem, (4 + g, p), peer)
    nt[b] = nt_ref[...]
    cot[b] = cot_ref[...]
    for half in range(2):
        pt[b, half] = pt_ref[:, half, b]
    for g in range(3):
        dm[g, b] = dm_ref[g, b]
    sa[0] = sa_ref[...]
    sb[0] = sb_ref[...]
    x, y = b % 2, b // 2
    steps = [
        other,
        (s, y * 2 + 1 - x),
        (s, (1 - y) * 2 + x),
        (((zed // 2) * 2 + 1 - zed % 2) * 2 + core, b),
        (((1 - zed // 2) * 2 + zed % 2) * 2 + core, b),
    ]

    def small_step(i):
        todo = [remote(sa.at[2 * i], sa.at[2 * i + 1], s_sem, (i, 0), steps[i])]
        if i in (1, 2):
            j = i - 1
            todo.append(remote(sb.at[2 * j], sb.at[2 * j + 1], s_sem, (i, 1), steps[i]))
        return todo

    def small_add(i, todo):
        for move in todo:
            move.wait()
        sa[2 * i + 2] = sa[2 * i] + sa[2 * i + 1]
        if i in (1, 2):
            j = i - 1
            sb[2 * j + 2] = sb[2 * j] + sb[2 * j + 1]

    small = small_step(0)
    for p in (1, 2, 3):
        for key in (("n", p), ("c", p), ("p", 0, p), ("p", 1, p)):
            moves[key].wait()
    small_add(0, small)
    small = small_step(1)

    def part_out(half):
        total = jnp.zeros((128, 1024), f32)
        for i in range(4):
            total += jnp.dot(
                pt[i, half].reshape(128, 256), cot[i], preferred_element_type=f32
            )
        return total

    def part_in(g, to, half):
        rows = pl.ds(pl.multiple_of(to * 256 + half * 128, 128), 128)
        total = jnp.zeros((128, 256), f32)
        for i in range(4):
            total += jnp.dot(nt[i, rows], dm[g, i], preferred_element_type=f32)
        return total

    core_send_o[...] = part_out(1 - core).astype(bf16)
    moves["co"] = remote(core_send_o, core_recv_o, c_sem, (3, 0), other)
    order = (2, 1, 3, 0)
    for g in range(3):
        for p in (1, 2, 3):
            moves["d", g, p].wait()
        for p in order:
            core_send[g, p] = part_in(g, (zed + p) % 4, 1 - core).astype(bf16)
            moves["c", g, p] = remote(
                core_send.at[g, p], core_recv.at[g, p], c_sem, (g, p), other
            )
    small_add(1, small)
    small = small_step(2)
    moves["co"].wait()
    out_own = part_out(core) + core_recv_o[...].astype(f32)
    z_send_o[...] = out_own.astype(bf16).reshape(4, 32, 1024)
    for p in (2, 1, 3):
        moves["zo", p] = remote(
            z_send_o.at[(zed + p) % 4], z_recv_o.at[p], zed_sem, (3, p), zed_peer(p)
        )
    for g in range(3):
        for p in order:
            moves["c", g, p].wait()
            total = part_in(g, (zed + p) % 4, core) + core_recv[g, p].astype(f32)
            if p == 0:
                own[g] = total
            else:
                z_send[g, p] = total.astype(bf16)
                moves["z", g, p] = remote(
                    z_send.at[g, p], z_recv.at[g, p], zed_sem, (g, p), zed_peer(p)
                )
    small_add(2, small)
    small = small_step(3)
    total = z_send_o[zed].astype(f32)
    for p in (2, 1, 3):
        moves["zo", p].wait()
        total += z_recv_o[p].astype(f32)
    wout_ref[...] = total
    for g in range(3):
        total = own[g]
        for p in (2, 1, 3):
            moves["z", g, p].wait()
            total += z_recv[g, p].astype(f32)
        last_send[g] = total.reshape(4, 32, 256)
        for p in (1, 2, 3):
            moves["l", g, p] = remote(
                last_send.at[g, (b + p) % 4], last_recv.at[g, b], l_sem, (g, p), batch_peer(p)
            )
        last_recv[g, b] = last_send[g, b]
        if g == 0:
            small_add(3, small)
            small = small_step(4)
    small_add(4, small)
    oa_ref[...] = sa[10]
    ob_ref[...] = sb[4]
    for g in range(3):
        for p in (1, 2, 3):
            moves["l", g, p].wait()
        for i in range(4):
            win_ref[:, g * 1024 + i * 256 : g * 1024 + (i + 1) * 256] = last_recv[g, i]


def back(nt, pt, dm, cot, sa, sb):
    vmem = pl.BlockSpec(memory_space=pltpu.VMEM)
    dma = pltpu.SemaphoreType.DMA
    rows = sa.shape[0]
    return pl.pallas_call(
        back_kernel,
        out_shape=(
            jax.ShapeDtypeStruct((32, 3072), f32),
            jax.ShapeDtypeStruct((32, 1024), f32),
            jax.ShapeDtypeStruct(sa.shape, f32),
            jax.ShapeDtypeStruct(sb.shape, f32),
        ),
        in_specs=[vmem] * 6,
        out_specs=(vmem,) * 4,
        scratch_shapes=[
            pltpu.VMEM((4, 1024, 256), bf16),
            pltpu.VMEM((4, 2, 4, 32, 256), bf16),
            pltpu.VMEM((3, 4, 256, 256), bf16),
            pltpu.VMEM((4, 256, 1024), bf16),
            pltpu.VMEM((3, 4, 128, 256), bf16),
            pltpu.VMEM((3, 4, 128, 256), bf16),
            pltpu.VMEM((128, 1024), bf16),
            pltpu.VMEM((128, 1024), bf16),
            pltpu.VMEM((3, 4, 128, 256), bf16),
            pltpu.VMEM((3, 4, 128, 256), bf16),
            pltpu.VMEM((4, 32, 1024), bf16),
            pltpu.VMEM((4, 32, 1024), bf16),
            pltpu.VMEM((3, 128, 256), f32),
            pltpu.VMEM((3, 4, 32, 256), f32),
            pltpu.VMEM((3, 4, 32, 256), f32),
            pltpu.VMEM((11, rows, 1024), f32),
            pltpu.VMEM((5,) + sb.shape, f32),
            dma((2, 7, 4)),
            dma((2, 4, 4)),
            dma((2, 4, 4)),
            dma((2, 3, 4)),
            dma((2, 5, 2)),
        ],
        compiler_params=pltpu.CompilerParams(
            collective_id=0, has_side_effects=True, vmem_limit_bytes=60 * 1024 * 1024
        ),
    )(nt, pt, dm, cot, sa, sb)


def local(
    tokens,
    cotangent,
    ln_gain,
    ln_bias,
    w_in,
    b_in,
    short_w,
    short_b,
    w_one,
    b_one,
    w_two,
    b_two,
    w_three,
    decay_rates,
    filt_bias,
    w_out,
    b_out,
):
    seq_count, block_len, model_width = tokens.shape
    seq_devices = lax.axis_size("seq")
    batch_devices = lax.axis_size("batch")
    devices = seq_devices * batch_devices
    length = block_len * seq_devices
    channels = model_width // seq_devices
    col_start = lax.axis_index("seq") * channels
    inputs = tokens.astype(f32)
    average = jnp.mean(inputs, axis=-1, keepdims=True)
    centered = inputs - average
    inv_std = lax.rsqrt(jnp.mean(centered * centered, axis=-1, keepdims=True) + epsilon)
    whitened = centered * inv_std
    normed = (whitened * ln_gain + ln_bias).astype(bf16)
    mixed = jnp.einsum("btd,de->bte", normed, w_in, preferred_element_type=f32) + b_in
    prev_rows = shifted(mixed[:, block_len - 2 :], "seq", 1)
    padded = jnp.concatenate([prev_rows, mixed], axis=1)
    delay_one = padded[:, 1:-1]
    delay_two = padded[:, :-2]
    short_out = short_w[0] * mixed + short_w[1] * delay_one + short_w[2] * delay_two + short_b
    outer_gate = short_out[..., :model_width]
    inner_gate = short_out[..., model_width : 2 * model_width]
    values = short_out[..., 2 * model_width :]
    gated = (values * inner_gate).astype(bf16)
    d_product = jnp.einsum(
        "bte,de->btd", cotangent, w_out, preferred_element_type=f32
    ).astype(bf16)
    d_prod_f = d_product.astype(f32)
    d_summed = (d_prod_f * outer_gate).astype(bf16)

    def to_channels(value):
        return lax.all_to_all(value, "seq", split_axis=2, concat_axis=1, tiled=True)

    def to_tokens(value):
        return lax.all_to_all(value, "seq", split_axis=1, concat_axis=2, tiled=True)

    gated_ch = to_channels(gated)
    d_ch = to_channels(d_summed)
    positions = jnp.asarray(position_features(length, w_one.shape[0]))
    w_three_part = lax.dynamic_slice_in_dim(w_three, col_start, channels, 1)
    decay_part = lax.dynamic_slice_in_dim(decay_rates, col_start, channels, 0)
    bias_part = lax.dynamic_slice_in_dim(filt_bias, col_start, channels, 0)

    def kernel_of(first_w, first_b, second_w, second_b, third_w):
        return filter_shape(positions, first_w, first_b, second_w, second_b, third_w, decay_part)

    kernel_full, kernel_pull = jax.vjp(kernel_of, w_one, b_one, w_two, b_two, w_three_part)
    matrix = jnp.asarray(dft_matrix(length))

    def spectrum(value):
        return jnp.einsum("kt,btc->bkc", matrix, value, preferred_element_type=f32)

    def inverse(cosines, sines):
        both = jnp.concatenate([cosines, sines], axis=1).astype(bf16)
        return jnp.einsum("kt,bkc->btc", matrix, both, preferred_element_type=f32) * (1.0 / length)

    k_both = spectrum(kernel_full.astype(bf16)[None])
    g_both = spectrum(gated_ch)
    d_both = spectrum(d_ch)
    k_c, k_s = k_both[:, :length], k_both[:, length:]
    g_c, g_s = g_both[:, :length], g_both[:, length:]
    d_c, d_s = d_both[:, :length], d_both[:, length:]
    long_out = inverse(g_c * k_c - g_s * k_s, g_c * k_s + g_s * k_c)
    gated_float = gated_ch.astype(f32)
    d_ch_float = d_ch.astype(f32)
    summed_ch = (long_out + bias_part * gated_float).astype(bf16)
    summed = to_tokens(summed_ch).astype(f32)
    grad_in = inverse(k_c * d_c + k_s * d_s, k_c * d_s - k_s * d_c) + bias_part * d_ch_float
    d_gated = to_tokens(grad_in.astype(bf16)).astype(f32)
    d_kernel = inverse(
        jnp.sum(g_c * d_c + g_s * d_s, axis=0, keepdims=True),
        jnp.sum(g_c * d_s - g_s * d_c, axis=0, keepdims=True),
    )[0]
    g_bias_part = jnp.sum(d_ch_float * gated_float, axis=(0, 1))
    g_w_one, g_b_one, g_w_two, g_b_two, g_w_three_part = kernel_pull(d_kernel)

    product = (summed * outer_gate).astype(bf16)
    result = jnp.einsum("btd,de->bte", product, w_out, preferred_element_type=f32) + b_out
    block_out = (inputs + result).astype(bf16)
    grad_out = cotangent.astype(f32)
    g_w_out = jnp.einsum("btd,bte->de", product, cotangent, preferred_element_type=f32)
    g_b_out = jnp.sum(grad_out, axis=(0, 1))
    d_outer = d_prod_f * summed
    d_short = jnp.concatenate([d_outer, d_gated * values, d_gated * inner_gate], axis=-1)
    g_short_w = jnp.stack(
        [
            jnp.sum(d_short * mixed, axis=(0, 1)),
            jnp.sum(d_short * delay_one, axis=(0, 1)),
            jnp.sum(d_short * delay_two, axis=(0, 1)),
        ]
    )
    g_short_b = jnp.sum(d_short, axis=(0, 1))
    next_rows = shifted(d_short[:, :2], "seq", -1)
    extended = jnp.concatenate([d_short, next_rows], axis=1)
    d_mixed = (
        short_w[0] * extended[:, :block_len]
        + short_w[1] * extended[:, 1 : block_len + 1]
        + short_w[2] * extended[:, 2:]
    ).astype(bf16)
    g_w_in = jnp.einsum("btd,bte->de", normed, d_mixed, preferred_element_type=f32)
    g_b_in = jnp.sum(d_mixed.astype(f32), axis=(0, 1))
    d_normed = jnp.einsum("bte,de->btd", d_mixed, w_in, preferred_element_type=f32)
    g_ln_gain = jnp.sum(d_normed * whitened, axis=(0, 1))
    g_ln_bias = jnp.sum(d_normed, axis=(0, 1))
    d_white = d_normed * ln_gain
    grad_tokens = grad_out + inv_std * (
        d_white
        - jnp.mean(d_white, axis=-1, keepdims=True)
        - whitened * jnp.mean(d_white * whitened, axis=-1, keepdims=True)
    )
    hidden, features = w_two.shape[0], w_one.shape[0]
    edges = [features * hidden, (features + 1) * hidden, (features + 1 + hidden) * hidden]
    net = jnp.concatenate([v.reshape(-1) for v in (g_w_one, g_b_one, g_w_two, g_b_two)])
    net_size = net.shape[0]
    if (seq_devices, batch_devices, seq_count, block_len, model_width) == (8, 4, 2, 128, 1024):
        tokens_here = seq_count * block_len
        dm = jnp.transpose(d_mixed.reshape(tokens_here, 3, 4, 256), (1, 2, 0, 3))
        net_rows = -(-net_size // 1024)
        sa = jnp.concatenate(
            [
                g_ln_gain[None],
                g_ln_bias[None],
                g_b_out[None],
                g_b_in.reshape(3, 1024),
                g_short_w.reshape(9, 1024),
                g_short_b.reshape(3, 1024),
                jnp.pad(net, (0, net_rows * 1024 - net_size)).reshape(net_rows, 1024),
            ],
            axis=0,
        )
        sa = jnp.pad(sa, ((0, -sa.shape[0] % 8), (0, 0)))
        sb = jnp.concatenate([g_w_three_part, g_bias_part[None]], axis=0)
        sb = jnp.pad(sb, ((0, -sb.shape[0] % 8), (0, 0)))
        out_w_in, out_w_out, sa, sb = back(
            jnp.transpose(normed.reshape(tokens_here, model_width)),
            jnp.transpose(product.reshape(tokens_here, model_width)).reshape(4, 2, 4, 32, 256),
            dm,
            cotangent.reshape(tokens_here, model_width),
            sa,
            sb,
        )
        place = lax.axis_index("seq") * 4 + lax.axis_index("batch")
        narrow = lax.dynamic_slice_in_dim(sa[:3], place * 32, 32, 1)
        wide = lax.dynamic_slice_in_dim(sa[3:18].reshape(5, 3072), place * 96, 96, 1)
        third = lax.dynamic_slice_in_dim(sb, lax.axis_index("batch") * 32, 32, 1)
        vectors = jnp.concatenate([narrow, third[hidden : hidden + 1], third[:hidden]], axis=0)
        wides = wide
        net = sa[18 : 18 + net_rows].reshape(-1)
    else:
        rows = model_width // devices
        big = jnp.concatenate([g_w_in, g_w_out], axis=1)
        big = reduce_scatter(big.reshape(seq_devices, batch_devices, rows, -1), bf16)
        out_w_in, out_w_out = big[:, : 3 * model_width], big[:, 3 * model_width :]
        g_w_three = lax.dynamic_update_slice_in_dim(
            jnp.zeros(w_three.shape, f32), g_w_three_part, col_start, 1
        )
        g_filt_bias = lax.dynamic_update_slice_in_dim(
            jnp.zeros(filt_bias.shape, f32), g_bias_part, col_start, 0
        )
        vectors = jnp.concatenate(
            [
                g_ln_gain[None],
                g_ln_bias[None],
                g_b_out[None],
                g_filt_bias[None],
                g_w_three,
            ],
            axis=0,
        )
        vectors = jnp.transpose(vectors.reshape(-1, devices, rows), (1, 0, 2)).reshape(devices, -1)
        wides = jnp.concatenate([g_b_in[None], g_short_w, g_short_b[None]], axis=0)
        wides = jnp.transpose(wides.reshape(-1, devices, 3 * rows), (1, 0, 2)).reshape(devices, -1)
        net_part = -(-net_size // devices)
        net = jnp.pad(net, (0, net_part * devices - net_size)).reshape(devices, net_part)
        small = jnp.concatenate([vectors, wides, net], axis=1)
        small = reduce_scatter(small.reshape(seq_devices, batch_devices, -1), f32)
        cut = rows * (4 + hidden)
        vectors = small[:cut].reshape(4 + hidden, rows)
        wides = small[cut : cut + 15 * rows].reshape(5, 3 * rows)
        net = lax.all_gather(small[cut + 15 * rows :], ("seq", "batch"), tiled=True)
    return (
        block_out,
        grad_tokens,
        vectors[0],
        vectors[1],
        out_w_in,
        wides[0],
        wides[1:4],
        wides[4],
        net[: edges[0]].reshape(features, hidden),
        net[edges[0] : edges[1]],
        net[edges[1] : edges[2]].reshape(hidden, hidden),
        net[edges[2] : net_size],
        vectors[4:],
        vectors[3],
        out_w_out,
        vectors[2],
    )


def solution(mesh):
    tokens_spec = P("batch", "seq", None)
    both = ("seq", "batch")
    in_specs = (tokens_spec, tokens_spec) + (P(),) * 15
    out_specs = (
        tokens_spec,
        tokens_spec,
        P(both),
        P(both),
        P(both, None),
        P(both),
        P(None, both),
        P(both),
        P(),
        P(),
        P(),
        P(),
        P(None, both),
        P(both),
        P(both, None),
        P(both),
    )
    return jax.shard_map(local, mesh=mesh, in_specs=in_specs, out_specs=out_specs, check_vma=False)
```

```python
import jax
import jax.numpy as jnp
import numpy as np
from jax import lax
from jax.experimental import pallas as pl
from jax.experimental.pallas import tpu as pltpu
from jax.sharding import PartitionSpec as P

highest = lax.Precision.HIGHEST
epsilon = 1e-05
f32, bf16 = jnp.float32, jnp.bfloat16


def dft_matrix(length):
    turns = ((2 * np.arange(length)[:, None] + 1) * np.arange(length)[None, :]) % (4 * length)
    phases = turns * (np.pi / (2 * length))
    return np.concatenate([np.cos(phases), np.sin(phases)], axis=0).astype(bf16)


def position_features(length, features):
    step_axis = np.arange(length, dtype=np.float64)
    band_count = (features - 1) // 2
    band_rates = 0.0001 + np.arange(band_count) * (band_count - 1 - 0.0001) / (band_count - 1)
    phases = 2.0 * np.pi / length * step_axis[:, None] * band_rates[None, :]
    return np.concatenate(
        [(step_axis / length)[:, None], np.cos(phases), -np.sin(phases)], axis=1
    ).astype(np.float32)


def filter_shape(positions, w_one, b_one, w_two, b_two, w_three, decay_rates):
    first_layer = jnp.sin(jnp.dot(positions, w_one, precision=highest) + b_one)
    second_layer = jnp.sin(jnp.dot(first_layer, w_two, precision=highest) + b_two)
    shaped = jnp.dot(second_layer, w_three, precision=highest)
    length = positions.shape[0]
    fraction = jnp.arange(length).astype(f32) / length
    return shaped * jnp.exp(-fraction[:, None] * decay_rates[None, :])


def shifted(value, axis, steps):
    count = lax.axis_size(axis)
    first, last = (max(0, -steps), min(count, count - steps))
    return lax.ppermute(value, axis, [(source, source + steps) for source in range(first, last)])


def reduce_scatter(value, dtype):
    out = lax.all_to_all(value.astype(dtype), "batch", split_axis=1, concat_axis=1, tiled=True)
    out = jnp.sum(out.astype(f32), axis=1)
    out = lax.all_to_all(out.astype(dtype), "seq", split_axis=0, concat_axis=0, tiled=True)
    return jnp.sum(out.astype(f32), axis=0)


def local(
    tokens,
    cotangent,
    ln_gain,
    ln_bias,
    w_in,
    b_in,
    short_w,
    short_b,
    w_one,
    b_one,
    w_two,
    b_two,
    w_three,
    decay_rates,
    filt_bias,
    w_out,
    b_out,
):
    seq_count, block_len, model_width = tokens.shape
    seq_devices = lax.axis_size("seq")
    batch_devices = lax.axis_size("batch")
    devices = seq_devices * batch_devices
    length = block_len * seq_devices
    channels = model_width // seq_devices
    col_start = lax.axis_index("seq") * channels
    inputs = tokens.astype(f32)
    average = jnp.mean(inputs, axis=-1, keepdims=True)
    centered = inputs - average
    inv_std = lax.rsqrt(jnp.mean(centered * centered, axis=-1, keepdims=True) + epsilon)
    whitened = centered * inv_std
    normed = (whitened * ln_gain + ln_bias).astype(bf16)
    mixed = jnp.einsum("btd,de->bte", normed, w_in, preferred_element_type=f32) + b_in
    prev_rows = shifted(mixed[:, block_len - 2 :], "seq", 1)
    padded = jnp.concatenate([prev_rows, mixed], axis=1)
    delay_one = padded[:, 1:-1]
    delay_two = padded[:, :-2]
    short_out = short_w[0] * mixed + short_w[1] * delay_one + short_w[2] * delay_two + short_b
    outer_gate = short_out[..., :model_width]
    inner_gate = short_out[..., model_width : 2 * model_width]
    values = short_out[..., 2 * model_width :]
    gated = (values * inner_gate).astype(bf16)
    d_product = jnp.einsum(
        "bte,de->btd", cotangent, w_out, preferred_element_type=f32
    ).astype(bf16)
    d_prod_f = d_product.astype(f32)
    d_summed = (d_prod_f * outer_gate).astype(bf16)

    def to_channels(value):
        return lax.all_to_all(value, "seq", split_axis=2, concat_axis=1, tiled=True)

    def to_tokens(value):
        return lax.all_to_all(value, "seq", split_axis=1, concat_axis=2, tiled=True)

    gated_ch = to_channels(gated)
    d_ch = to_channels(d_summed)
    positions = jnp.asarray(position_features(length, w_one.shape[0]))
    w_three_part = lax.dynamic_slice_in_dim(w_three, col_start, channels, 1)
    decay_part = lax.dynamic_slice_in_dim(decay_rates, col_start, channels, 0)
    bias_part = lax.dynamic_slice_in_dim(filt_bias, col_start, channels, 0)

    def kernel_of(first_w, first_b, second_w, second_b, third_w):
        return filter_shape(positions, first_w, first_b, second_w, second_b, third_w, decay_part)

    kernel_full, kernel_pull = jax.vjp(kernel_of, w_one, b_one, w_two, b_two, w_three_part)
    matrix = jnp.asarray(dft_matrix(length))

    def spectrum(value):
        return jnp.einsum("kt,btc->bkc", matrix, value, preferred_element_type=f32)

    def inverse(cosines, sines):
        both = jnp.concatenate([cosines, sines], axis=1).astype(bf16)
        return jnp.einsum("kt,bkc->btc", matrix, both, preferred_element_type=f32) * (1.0 / length)

    k_both = spectrum(kernel_full.astype(bf16)[None])
    g_both = spectrum(gated_ch)
    d_both = spectrum(d_ch)
    k_c, k_s = k_both[:, :length], k_both[:, length:]
    g_c, g_s = g_both[:, :length], g_both[:, length:]
    d_c, d_s = d_both[:, :length], d_both[:, length:]
    long_out = inverse(g_c * k_c - g_s * k_s, g_c * k_s + g_s * k_c)
    gated_float = gated_ch.astype(f32)
    d_ch_float = d_ch.astype(f32)
    summed_ch = (long_out + bias_part * gated_float).astype(bf16)
    summed = to_tokens(summed_ch).astype(f32)
    grad_in = inverse(k_c * d_c + k_s * d_s, k_c * d_s - k_s * d_c) + bias_part * d_ch_float
    d_gated = to_tokens(grad_in.astype(bf16)).astype(f32)
    d_kernel = inverse(
        jnp.sum(g_c * d_c + g_s * d_s, axis=0, keepdims=True),
        jnp.sum(g_c * d_s - g_s * d_c, axis=0, keepdims=True),
    )[0]
    g_bias_part = jnp.sum(d_ch_float * gated_float, axis=(0, 1))
    g_w_one, g_b_one, g_w_two, g_b_two, g_w_three_part = kernel_pull(d_kernel)

    product = (summed * outer_gate).astype(bf16)
    result = jnp.einsum("btd,de->bte", product, w_out, preferred_element_type=f32) + b_out
    block_out = (inputs + result).astype(bf16)
    grad_out = cotangent.astype(f32)
    g_w_out = jnp.einsum("btd,bte->de", product, cotangent, preferred_element_type=f32)
    g_b_out = jnp.sum(grad_out, axis=(0, 1))
    d_outer = d_prod_f * summed
    d_short = jnp.concatenate([d_outer, d_gated * values, d_gated * inner_gate], axis=-1)
    g_short_w = jnp.stack(
        [
            jnp.sum(d_short * mixed, axis=(0, 1)),
            jnp.sum(d_short * delay_one, axis=(0, 1)),
            jnp.sum(d_short * delay_two, axis=(0, 1)),
        ]
    )
    g_short_b = jnp.sum(d_short, axis=(0, 1))
    next_rows = shifted(d_short[:, :2], "seq", -1)
    extended = jnp.concatenate([d_short, next_rows], axis=1)
    d_mixed = (
        short_w[0] * extended[:, :block_len]
        + short_w[1] * extended[:, 1 : block_len + 1]
        + short_w[2] * extended[:, 2:]
    ).astype(bf16)
    g_w_in = jnp.einsum("btd,bte->de", normed, d_mixed, preferred_element_type=f32)
    g_b_in = jnp.sum(d_mixed.astype(f32), axis=(0, 1))
    d_normed = jnp.einsum("bte,de->btd", d_mixed, w_in, preferred_element_type=f32)
    g_ln_gain = jnp.sum(d_normed * whitened, axis=(0, 1))
    g_ln_bias = jnp.sum(d_normed, axis=(0, 1))
    d_white = d_normed * ln_gain
    grad_tokens = grad_out + inv_std * (
        d_white
        - jnp.mean(d_white, axis=-1, keepdims=True)
        - whitened * jnp.mean(d_white * whitened, axis=-1, keepdims=True)
    )
    rows = model_width // devices
    big = jnp.concatenate([g_w_in, g_w_out], axis=1)
    big = reduce_scatter(big.reshape(seq_devices, batch_devices, rows, -1), bf16)
    out_w_in, out_w_out = big[:, : 3 * model_width], big[:, 3 * model_width :]
    g_w_three = lax.dynamic_update_slice_in_dim(
        jnp.zeros(w_three.shape, f32), g_w_three_part, col_start, 1
    )
    g_filt_bias = lax.dynamic_update_slice_in_dim(
        jnp.zeros(filt_bias.shape, f32), g_bias_part, col_start, 0
    )
    vectors = jnp.concatenate(
        [
            g_ln_gain[None],
            g_ln_bias[None],
            g_b_out[None],
            g_filt_bias[None],
            g_w_three,
        ],
        axis=0,
    )
    vectors = jnp.transpose(vectors.reshape(-1, devices, rows), (1, 0, 2)).reshape(devices, -1)
    wides = jnp.concatenate([g_b_in[None], g_short_w, g_short_b[None]], axis=0)
    wides = jnp.transpose(wides.reshape(-1, devices, 3 * rows), (1, 0, 2)).reshape(devices, -1)
    net = jnp.concatenate([v.reshape(-1) for v in (g_w_one, g_b_one, g_w_two, g_b_two)])
    net_size = net.shape[0]
    net_part = -(-net_size // devices)
    net = jnp.pad(net, (0, net_part * devices - net_size)).reshape(devices, net_part)
    small = jnp.concatenate([vectors, wides, net], axis=1)
    small = reduce_scatter(small.reshape(seq_devices, batch_devices, -1), f32)
    hidden = w_two.shape[0]
    cut = rows * (4 + hidden)
    vectors = small[:cut].reshape(4 + hidden, rows)
    wides = small[cut : cut + 15 * rows].reshape(5, 3 * rows)
    net = lax.all_gather(small[cut + 15 * rows :], ("seq", "batch"), tiled=True)
    features = w_one.shape[0]
    edges = [features * hidden, (features + 1) * hidden, (features + 1 + hidden) * hidden]
    return (
        block_out,
        grad_tokens,
        vectors[0],
        vectors[1],
        out_w_in,
        wides[0],
        wides[1:4],
        wides[4],
        net[: edges[0]].reshape(features, hidden),
        net[edges[0] : edges[1]],
        net[edges[1] : edges[2]].reshape(hidden, hidden),
        net[edges[2] : net_size],
        vectors[4:],
        vectors[3],
        out_w_out,
        vectors[2],
    )


MESH = pl.DeviceIdType.MESH
HALF_TURN = (1.5703125, 4.837512969970703125e-4, 7.549789948768648e-8)


def sin_cos(x):
    turns = jnp.floor(x * 0.6366197723675814 + 0.5)
    r = ((x - turns * HALF_TURN[0]) - turns * HALF_TURN[1]) - turns * HALF_TURN[2]
    q = turns.astype(jnp.int32)
    r2 = r * r
    sine = r + r * r2 * (
        -1.6666654611e-1 + r2 * (8.3321608736e-3 + r2 * -1.9515295891e-4)
    )
    cosine = 1.0 - 0.5 * r2 + r2 * r2 * (
        4.166664568298827e-2 + r2 * (-1.388731625493765e-3 + r2 * 2.443315711809948e-5)
    )
    odd = (q & 1) == 1
    s_abs, c_abs = jnp.where(odd, cosine, sine), jnp.where(odd, sine, cosine)
    s_neg, c_neg = (q & 2) == 2, ((q + 1) & 2) == 2
    return jnp.where(s_neg, -s_abs, s_abs), jnp.where(c_neg, -c_abs, c_abs)


def mm(a, b, dims=((1,), (0,))):
    return lax.dot_general(a, b, (dims, ((), ())), preferred_element_type=f32)


def mm_full(a, b, dims=((1,), (0,))):
    return lax.dot_general(
        a, b, (dims, ((), ())), precision=highest, preferred_element_type=f32
    )


def twice(v):
    return jnp.concatenate([v, v], axis=1)


def lanes(start, size):
    return pl.ds(pl.multiple_of(start, size), size)


NT, TN = ((1,), (1,)), ((0,), (0,))


def whole_kernel(
    tok_ref,
    cot_ref,
    gain_ref,
    beta_ref,
    win_ref,
    bin_ref,
    sw_ref,
    sb_ref,
    w1_ref,
    b1_ref,
    w2_ref,
    b2_ref,
    w3_ref,
    decay_ref,
    fb_ref,
    wout_ref,
    bout_ref,
    pos_ref,
    f_ref,
    ft_ref,
    out_ref,
    gtok_ref,
    gwin_ref,
    gwout_ref,
    oa_ref,
    ob_ref,
    oc_ref,
    w_in,
    w_out,
    fm,
    ft,
    halo,
    white,
    istd,
    normed,
    mx,
    oiv,
    dpr,
    gsend,
    gch,
    dsend,
    dch,
    ysend,
    yrecv,
    qsend,
    qrecv,
    first,
    first_c,
    second,
    second_c,
    window,
    ksp,
    gsp,
    zs,
    es,
    dk,
    product,
    pts,
    dsx,
    dms,
    dn,
    nt,
    pt,
    dm,
    cot,
    core_send,
    core_recv,
    core_send_o,
    core_recv_o,
    z_send,
    z_recv,
    z_send_o,
    z_recv_o,
    own,
    last_send,
    last_recv,
    sa,
    sb,
    sc,
    load_sem,
    halo_sem,
    a_sem,
    b_sem,
    c_sem,
    zed_sem,
    l_sem,
    s_sem,
):
    s, b = lax.axis_index("seq"), lax.axis_index("batch")
    zed, core = s // 2, s % 2
    other = (zed * 2 + 1 - core, b)

    loads = [
        pltpu.make_async_copy(src, dst, load_sem.at[i])
        for i, (src, dst) in enumerate(
            ((win_ref, w_in), (wout_ref, w_out), (f_ref, fm), (ft_ref, ft))
        )
    ]
    for load in loads:
        load.start()

    def batch_peer(p):
        return (s, (b + p) % 4)

    def zed_peer(p):
        return (((zed + p) % 4) * 2 + core, b)

    barrier = pltpu.get_barrier_semaphore()
    for p in range(1, 8):
        pl.semaphore_signal(
            barrier, inc=1, device_id=((s + p) % 8, b), device_id_type=MESH
        )
    for p in range(1, 4):
        pl.semaphore_signal(barrier, inc=1, device_id=batch_peer(p), device_id_type=MESH)
    pl.semaphore_wait(barrier, 10)

    def remote(src, dst, sems, index, peer, start=True):
        copy = pltpu.make_async_remote_copy(
            src_ref=src,
            dst_ref=dst,
            send_sem=sems.at[(0,) + index],
            recv_sem=sems.at[(1,) + index],
            device_id=peer,
            device_id_type=MESH,
        )
        if start:
            copy.start()
        return copy

    edge = remote(
        tok_ref.at[:, 112:128],
        halo,
        halo_sem,
        (0,),
        ((s + 1) % 8, b),
        start=False,
    )

    @pl.when(s < 7)
    def _():
        edge.start()

    moves = {}
    for p in (1, 2, 3):
        moves["c", p] = remote(cot_ref, cot.at[b], b_sem, (1, p), batch_peer(p))

    gain, beta = gain_ref[...], beta_ref[...]

    def white_of(x):
        x = x.astype(f32)
        centered = x - jnp.mean(x, axis=-1, keepdims=True)
        inv = lax.rsqrt(jnp.mean(centered * centered, axis=-1, keepdims=True) + epsilon)
        return centered * inv, inv

    def norm_rows(i, _):
        q, r = i // 4, (i % 4) * 32
        rows = lanes(i * 32, 32)
        w, inv = white_of(tok_ref[q, lanes(r, 32)])
        white[rows] = w
        istd[rows] = jnp.broadcast_to(inv, (32, 128))
        normed[rows] = (w * gain + beta).astype(bf16)
        return 0

    lax.fori_loop(0, 8, norm_rows, 0)

    @pl.when(s == 0)
    def _():
        halo[...] = jnp.zeros_like(halo)

    @pl.when(s > 0)
    def _():
        edge.wait_recv()

    w, _inv = white_of(halo[...].reshape(32, 1024))
    normed[256:288] = (w * gain + beta).astype(bf16)

    pairs = ((gsend, gch), (dsend, dch), (ysend, yrecv), (qsend, qrecv))

    def exchange(kind, p):
        src, dst = pairs[kind]
        to = (s + p) % 8
        return remote(src.at[to], dst.at[s], a_sem, (kind, p), (to, b), start=False)

    def send_tile(kind, tile):
        p = (tile - s + 8) % 8

        @pl.when(p != 0)
        def _():
            exchange(kind, p).start()

        @pl.when(p == 0)
        def _():
            src, dst = pairs[kind]
            dst[s] = src[s]

    def wait_tiles(kind):
        for p in range(1, 8):
            exchange(kind, p).wait_recv()

    loads[0].wait()

    def project(i, _):
        t = (zed + 2 + i) % 4
        for g in range(3):
            cols = lanes(g * 1024 + t * 256, 256)
            m = mm(normed[...], w_in[:, cols]) + bin_ref[:, cols]
            for h in range(2):
                at = slice(h * 128, h * 128 + 128)
                tile = 2 * t + h
                edge_rows = jnp.concatenate([m[264:272, at], m[280:288, at]], axis=1)
                mx[g, tile, 0:8] = jnp.where(s > 0, edge_rows, 0.0)
                mx[g, tile, 8:136] = jnp.concatenate([m[0:128, at], m[128:256, at]], axis=1)
        for h in range(2):
            tile = 2 * t + h
            got = []
            for g in range(3):
                cols = lanes(g * 1024 + tile * 128, 128)
                taps = sw_ref[:, cols]
                value = (
                    twice(taps[0:1]) * mx[g, tile, 8:136]
                    + twice(taps[1:2]) * mx[g, tile, 7:135]
                    + twice(taps[2:3]) * mx[g, tile, 6:134]
                    + twice(sb_ref[:, cols])
                )
                oiv[g, tile] = value
                got.append(value)
            gsend[tile] = (got[2] * got[1]).astype(bf16)
            send_tile(0, tile)
        return 0

    lax.fori_loop(0, 4, project, 0)

    loads[1].wait()
    cot_here = cot_ref[...]

    def backproject(i, _):
        t = (zed + 2 + i) % 4
        m = mm(cot_here, w_out[lanes(t * 256, 256)], NT).astype(bf16)
        for h in range(2):
            at = slice(h * 128, h * 128 + 128)
            tile = 2 * t + h
            value = jnp.concatenate([m[0:128, at], m[128:256, at]], axis=1)
            dpr[tile] = value
            dsend[tile] = (value.astype(f32) * oiv[0, tile]).astype(bf16)
            send_tile(1, tile)
        return 0

    lax.fori_loop(0, 4, backproject, 0)

    nt[b] = normed[0:256].T
    for p in (1, 2, 3):
        moves["n", p] = remote(nt.at[b], nt.at[b], b_sem, (0, p), batch_peer(p))
    cot[b] = cot_here
    sa[0] = jnp.zeros(sa.shape[1:], f32)
    sa[0, 2:3] = jnp.sum(cot_here.astype(f32), axis=0, keepdims=True)

    mine = lanes(s * 128, 128)
    pos = pos_ref[...]
    one, one_c = sin_cos(mm_full(pos, w1_ref[...]) + b1_ref[...])
    first[...] = one
    first_c[...] = one_c
    two, two_c = sin_cos(mm_full(one, w2_ref[...]) + b2_ref[...])
    second[...] = two
    second_c[...] = two_c
    fraction = lax.broadcasted_iota(jnp.int32, (1024, 128), 0).astype(f32) * (1.0 / 1024)
    wind = jnp.exp(-fraction * decay_ref[:, mine])
    window[...] = wind
    taps_bf = (mm_full(two, w3_ref[:, mine]) * wind).astype(bf16)
    loads[2].wait()

    def filter_rows(i, _):
        rows = lanes(i * 256, 256)
        ksp[rows] = mm(fm[rows], taps_bf)
        return 0

    lax.fori_loop(0, 8, filter_rows, 0)

    bias = twice(fb_ref[:, mine])
    wait_tiles(0)
    gated = gch[...].reshape(1024, 256)

    def forward_rows(i, _):
        lo, hi = lanes(i * 256, 256), lanes(1024 + i * 256, 256)
        gc, gs = mm(fm[lo], gated), mm(fm[hi], gated)
        kc, ks = twice(ksp[lo]), twice(ksp[hi])
        gsp[lo] = gc
        gsp[hi] = gs
        zs[lo] = (gc * kc - gs * ks).astype(bf16)
        zs[hi] = (gc * ks + gs * kc).astype(bf16)
        return 0

    lax.fori_loop(0, 4, forward_rows, 0)
    loads[3].wait()

    def inverse_to(kind, send, inputs):
        def rows_of(i, _):
            t = (zed + 2 + i) % 4
            y = mm(ft[lanes(t * 256, 256)], zs[...]) * (1.0 / 1024)
            for h in range(2):
                tile = 2 * t + h
                here = y[h * 128 : h * 128 + 128] + bias * inputs[tile].astype(f32)
                send[tile] = here.astype(bf16)
                send_tile(kind, tile)
            return 0

        lax.fori_loop(0, 4, rows_of, 0)

    inverse_to(2, ysend, gch)

    wait_tiles(1)
    d_here = dch[...].reshape(1024, 256)

    def backward_rows(i, _):
        lo, hi = lanes(i * 256, 256), lanes(1024 + i * 256, 256)
        dc, ds = mm(fm[lo], d_here), mm(fm[hi], d_here)
        kc, ks = twice(ksp[lo]), twice(ksp[hi])
        gc, gs = gsp[lo], gsp[hi]
        zs[lo] = (kc * dc + ks * ds).astype(bf16)
        zs[hi] = (kc * ds - ks * dc).astype(bf16)
        ec, e_s = gc * dc + gs * ds, gc * ds - gs * dc
        es[lo] = (ec[:, :128] + ec[:, 128:]).astype(bf16)
        es[hi] = (e_s[:, :128] + e_s[:, 128:]).astype(bf16)
        return 0

    lax.fori_loop(0, 4, backward_rows, 0)
    inverse_to(3, qsend, dch)

    def kernel_rows(i, total):
        rows = lanes(i * 256, 256)
        dk[rows] = mm(ft[rows], es[...]) * (1.0 / 1024) * window[rows]
        for h in range(2):
            tile = 2 * i + h
            total += jnp.sum(dch[tile].astype(f32) * gch[tile].astype(f32), axis=0, keepdims=True)
        return total

    total = lax.fori_loop(0, 4, kernel_rows, jnp.zeros((1, 256), f32))
    sb[0] = jnp.zeros(sb.shape[1:], f32)
    sc[0] = jnp.zeros(sc.shape[1:], f32)
    sb[0, 64:65] = total[:, :128] + total[:, 128:]
    d_shaped = dk[...]
    sb[0, 0:64] = mm_full(second[...], d_shaped, TN)
    d_two = mm_full(d_shaped, w3_ref[:, mine], NT) * second_c[...]
    sc[0, 40:104, 0:64] = mm_full(first[...], d_two, TN)
    sc[0, 104:105, 0:64] = jnp.sum(d_two, axis=0, keepdims=True)
    d_one = mm_full(d_two, w2_ref[...], NT) * first_c[...]
    sc[0, 0:33, 0:64] = mm_full(pos_ref[...], d_one, TN)
    sc[0, 105:106, 0:64] = jnp.sum(d_one, axis=0, keepdims=True)

    x, y = b % 2, b // 2
    steps = [
        other,
        (s, y * 2 + 1 - x),
        (s, (1 - y) * 2 + x),
        (((zed // 2) * 2 + 1 - zed % 2) * 2 + core, b),
        (((1 - zed // 2) * 2 + zed % 2) * 2 + core, b),
    ]

    def small_start(array, which, i, k):
        return remote(array.at[2 * k], array.at[2 * k + 1], s_sem, (which, i), steps[i])

    def small_end(array, k, move):
        move.wait()
        array[2 * k + 2] = array[2 * k] + array[2 * k + 1]

    wait_tiles(2)

    def product_tile(j, _):
        value = yrecv[j].astype(f32)
        made = (value * oiv[0, j]).astype(bf16)
        cols = lanes(j * 128, 128)
        product[0:128, cols] = made[:, :128]
        product[128:256, cols] = made[:, 128:]
        dsx[0, j, 0:128] = dpr[j].astype(f32) * value
        return 0

    lax.fori_loop(0, 8, product_tile, 0)

    def edges_of(groups, index):
        return remote(
            dsx.at[groups, :, 0:8],
            dsx.at[groups, :, 128:136],
            halo_sem,
            (index,),
            ((s + 7) % 8, b),
            start=False,
        )

    def send_edges(groups, index):
        @pl.when(s > 0)
        def _():
            edges_of(groups, index).start()

    def wait_edges(groups, index):
        @pl.when(s == 7)
        def _():
            for g in range(groups.start, groups.stop):
                for j in range(8):
                    dsx[g, j, 128:136] = jnp.zeros((8, 256), f32)

        @pl.when(s < 7)
        def _():
            edges_of(groups, index).wait_recv()

    send_edges(slice(0, 1), 1)
    pts[...] = product[...].T.reshape(4, 2, 4, 32, 256)
    for p in (1, 2, 3):
        peer, to = batch_peer(p), (b + p) % 4
        for half in range(2):
            moves["p", half, p] = remote(
                pts.at[:, half, to], pt.at[b, half], b_sem, (2 + half, p), peer
            )
    for half in range(2):
        pt[b, half] = pts[:, half, b]

    def out_cols(i, _):
        cols = lanes(i * 256, 256)
        r = mm(product[...], w_out[:, cols]) + bout_ref[:, cols]
        for q in range(2):
            rows = slice(q * 128, q * 128 + 128)
            out_ref[q, :, cols] = (tok_ref[q, :, cols].astype(f32) + r[rows]).astype(bf16)
        return 0

    lax.fori_loop(0, 4, out_cols, 0)
    wait_edges(slice(0, 1), 1)

    def mixed_tile(g):
        def one_tile(j, _):
            q, cols = j // 2, lanes((j % 2) * 128, 128)
            wide = lanes(g * 1024 + j * 128, 128)
            narrow = lanes(j * 128, 128)
            taps = sw_ref[:, wide]
            here = dsx[g, j, 0:128]
            value = (
                twice(taps[0:1]) * here
                + twice(taps[1:2]) * dsx[g, j, 1:129]
                + twice(taps[2:3]) * dsx[g, j, 2:130]
            ).astype(bf16)
            dms[g, q, 0:128, cols] = value[:, :128]
            dms[g, q, 128:256, cols] = value[:, 128:]

            def column_sum(v):
                v = jnp.sum(v, axis=0, keepdims=True)
                return v[:, :128] + v[:, 128:]

            sa[0, 3 + g : 4 + g, narrow] = column_sum(value.astype(f32))
            for k in range(3):
                row = 6 + 3 * k + g
                sa[0, row : row + 1, narrow] = column_sum(here * mx[g, j, 8 - k : 136 - k])
            sa[0, 15 + g : 16 + g, narrow] = column_sum(here)
            return 0

        lax.fori_loop(0, 8, one_tile, 0)
        for p in (1, 2, 3):
            to = (b + p) % 4
            moves["d", g, p] = remote(
                dms.at[g, to], dm.at[g, b], b_sem, (4 + g, p), batch_peer(p)
            )
        dm[g, b] = dms[g, b]

    mixed_tile(0)
    mb, mc = None, small_start(sc, 1, 0, 0)

    def part_out(half):
        total = jnp.zeros((128, 1024), f32)
        for i in range(4):
            total += mm(pt[i, half].reshape(128, 256), cot[i])
        return total

    def part_in(g, to, half):
        rows = lanes(to * 256 + half * 128, 128)
        total = jnp.zeros((128, 256), f32)
        for i in range(4):
            total += mm(nt[i, rows], dm[g, i])
        return total

    order = (2, 1, 3, 0)

    def done(key):
        moves[key].wait()

    def core_half(g):
        for p in (1, 2, 3):
            done(("d", g, p))
        for p in order:
            core_send[g, p] = part_in(g, (zed + p) % 4, 1 - core).astype(bf16)
            moves["e", g, p] = remote(
                core_send.at[g, p], core_recv.at[g, p], c_sem, (g, p), other
            )

    def zed_half(g):
        for p in order:
            done(("e", g, p))
            total = part_in(g, (zed + p) % 4, core) + core_recv[g, p].astype(f32)
            if p == 0:
                own[g] = total
            else:
                z_send[g, p] = total.astype(bf16)
                moves["z", g, p] = remote(
                    z_send.at[g, p], z_recv.at[g, p], zed_sem, (g, p), zed_peer(p)
                )

    def last_half(g):
        total = own[g]
        for p in (2, 1, 3):
            done(("z", g, p))
            total += z_recv[g, p].astype(f32)
        last_send[g] = total.reshape(4, 32, 256)
        for p in (1, 2, 3):
            moves["l", g, p] = remote(
                last_send.at[g, (b + p) % 4], last_recv.at[g, b], l_sem, (g, p), batch_peer(p)
            )
        last_recv[g, b] = last_send[g, b]

    for p in (1, 2, 3):
        for key in (("n", p), ("c", p), ("p", 0, p), ("p", 1, p)):
            done(key)
    core_send_o[...] = part_out(1 - core).astype(bf16)
    moves["co"] = remote(core_send_o, core_recv_o, c_sem, (3, 0), other)
    core_half(0)
    small_end(sc, 0, mc)
    mb, mc = small_start(sb, 0, 1, 0), small_start(sc, 1, 1, 1)

    wait_tiles(3)

    def gate_tile(j, _):
        value = qrecv[j].astype(f32)
        dsx[1, j, 0:128] = value * oiv[2, j]
        dsx[2, j, 0:128] = value * oiv[1, j]
        return 0

    lax.fori_loop(0, 8, gate_tile, 0)
    send_edges(slice(1, 3), 2)
    done("co")
    out_own = part_out(core) + core_recv_o[...].astype(f32)
    z_send_o[...] = out_own.astype(bf16).reshape(4, 32, 1024)
    for p in (2, 1, 3):
        moves["zo", p] = remote(
            z_send_o.at[(zed + p) % 4], z_recv_o.at[p], zed_sem, (3, p), zed_peer(p)
        )
    wait_edges(slice(1, 3), 2)
    mixed_tile(1)
    mixed_tile(2)
    small_end(sb, 0, mb)
    small_end(sc, 1, mc)
    mb, mc = small_start(sb, 0, 2, 1), small_start(sc, 1, 2, 2)
    zed_half(0)

    def normed_cols(i, _):
        at = lanes(i * 256, 256)
        total = jnp.zeros((256, 256), f32)
        for g in range(3):
            for q in range(4):
                c = g * 1024 + q * 256
                total += mm(dms[g, q], w_in[at, c : c + 256], NT)
        dn[:, at] = total
        return 0

    lax.fori_loop(0, 4, normed_cols, 0)
    core_half(1)
    core_half(2)

    def token_rows(i, sums):
        q, r = i // 4, lanes((i % 4) * 32, 32)
        rows = lanes(i * 32, 32)
        d, w = dn[rows], white[rows]
        dw = d * w
        d_white = d * gain
        grad = cot_ref[rows].astype(f32) + istd[rows, 0:1] * (
            d_white
            - jnp.mean(d_white, axis=-1, keepdims=True)
            - w * jnp.mean(d_white * w, axis=-1, keepdims=True)
        )
        gtok_ref[q, r] = grad
        return (
            sums[0] + jnp.sum(dw, axis=0, keepdims=True),
            sums[1] + jnp.sum(d, axis=0, keepdims=True),
        )

    zero = jnp.zeros((1, 1024), f32)
    sums = lax.fori_loop(0, 8, token_rows, (zero, zero))
    sa[0, 0:1] = sums[0]
    sa[0, 1:2] = sums[1]
    ma = small_start(sa, 2, 0, 0)
    small_end(sb, 1, mb)
    small_end(sc, 2, mc)
    mc = small_start(sc, 1, 3, 3)
    zed_half(1)
    small_end(sa, 0, ma)
    ma = small_start(sa, 2, 1, 1)
    zed_half(2)
    small_end(sa, 1, ma)
    ma = small_start(sa, 2, 2, 2)
    small_end(sc, 3, mc)
    mc = small_start(sc, 1, 4, 4)
    total = z_send_o[zed].astype(f32)
    for p in (2, 1, 3):
        done(("zo", p))
        total += z_recv_o[p].astype(f32)
    gwout_ref[...] = total
    last_half(0)
    small_end(sa, 2, ma)
    ma = small_start(sa, 2, 3, 3)
    last_half(1)
    last_half(2)
    small_end(sa, 3, ma)
    ma = small_start(sa, 2, 4, 4)
    small_end(sc, 4, mc)
    for g in range(3):
        for p in (1, 2, 3):
            done(("l", g, p))
        for i in range(4):
            gwin_ref[:, g * 1024 + i * 256 : g * 1024 + (i + 1) * 256] = last_recv[g, i]
    small_end(sa, 4, ma)
    oa_ref[...] = sa[10]
    ob_ref[...] = sb[4]
    oc_ref[...] = sc[10]
    for kind in range(4):
        for p in range(1, 8):
            exchange(kind, p).wait_send()

    @pl.when(s < 7)
    def _():
        edge.wait_send()

    @pl.when(s > 0)
    def _():
        edges_of(slice(0, 1), 1).wait_send()
        edges_of(slice(1, 3), 2).wait_send()


def whole(args, positions, matrix):
    vmem, anywhere = (pl.BlockSpec(memory_space=m) for m in (pltpu.VMEM, pl.ANY))
    dma = pltpu.SemaphoreType.DMA
    specs = [vmem] * 20
    for i in (4, 15, 18, 19):
        specs[i] = anywhere
    shape = jax.ShapeDtypeStruct

    def v(dtype, *dims):
        return pltpu.VMEM(dims, dtype)

    return pl.pallas_call(
        whole_kernel,
        out_shape=(
            shape((2, 128, 1024), bf16),
            shape((2, 128, 1024), f32),
            shape((32, 3072), f32),
            shape((32, 1024), f32),
            shape((24, 1024), f32),
            shape((72, 128), f32),
            shape((112, 128), f32),
        ),
        in_specs=specs,
        out_specs=(vmem,) * 7,
        scratch_shapes=[
            v(bf16, 1024, 3072),
            v(bf16, 1024, 1024),
            v(bf16, 2048, 1024),
            v(bf16, 1024, 2048),
            v(bf16, 2, 16, 1024),
            v(f32, 256, 1024),
            v(f32, 256, 128),
            v(bf16, 288, 1024),
            v(f32, 3, 8, 136, 256),
            v(f32, 3, 8, 128, 256),
            v(bf16, 8, 128, 256),
            v(bf16, 8, 128, 256),
            v(bf16, 8, 128, 256),
            v(bf16, 8, 128, 256),
            v(bf16, 8, 128, 256),
            v(bf16, 8, 128, 256),
            v(bf16, 8, 128, 256),
            v(bf16, 8, 128, 256),
            v(bf16, 8, 128, 256),
            v(f32, 1024, 64),
            v(f32, 1024, 64),
            v(f32, 1024, 64),
            v(f32, 1024, 64),
            v(f32, 1024, 128),
            v(f32, 2048, 128),
            v(f32, 2048, 256),
            v(bf16, 2048, 256),
            v(bf16, 2048, 128),
            v(f32, 1024, 128),
            v(bf16, 256, 1024),
            v(bf16, 4, 2, 4, 32, 256),
            v(f32, 3, 8, 136, 256),
            v(bf16, 3, 4, 256, 256),
            v(f32, 256, 1024),
            v(bf16, 4, 1024, 256),
            v(bf16, 4, 2, 4, 32, 256),
            v(bf16, 3, 4, 256, 256),
            v(bf16, 4, 256, 1024),
            v(bf16, 3, 4, 128, 256),
            v(bf16, 3, 4, 128, 256),
            v(bf16, 128, 1024),
            v(bf16, 128, 1024),
            v(bf16, 3, 4, 128, 256),
            v(bf16, 3, 4, 128, 256),
            v(bf16, 4, 32, 1024),
            v(bf16, 4, 32, 1024),
            v(f32, 3, 128, 256),
            v(f32, 3, 4, 32, 256),
            v(f32, 3, 4, 32, 256),
            v(f32, 11, 24, 1024),
            v(f32, 5, 72, 128),
            v(f32, 11, 112, 128),
            dma((4,)),
            dma((2, 3)),
            dma((2, 4, 8)),
            dma((2, 7, 4)),
            dma((2, 4, 4)),
            dma((2, 4, 4)),
            dma((2, 3, 4)),
            dma((2, 3, 5)),
        ],
        compiler_params=pltpu.CompilerParams(
            collective_id=0, has_side_effects=True, vmem_limit_bytes=63 * 1024 * 1024
        ),
    )(*args, positions, matrix, np.ascontiguousarray(matrix.T))


def local_small(*args):
    tokens, cotangent = args[:2]
    row = lambda v: v.reshape(1, -1)
    vectors = {2, 3, 5, 7, 9, 11, 13, 14, 16}
    given = [row(a) if i in vectors else a for i, a in enumerate(args)]
    given[1] = cotangent.reshape(256, 1024)
    features, hidden = args[8].shape
    out, gtok, gwin, gwout, sa, sb, sc = whole(
        given, position_features(1024, features), dft_matrix(1024)
    )
    place = lax.axis_index("seq") * 4 + lax.axis_index("batch")
    narrow = lax.dynamic_slice_in_dim(sa[:3], place * 32, 32, 1)
    wide = lax.dynamic_slice_in_dim(sa[3:18].reshape(5, 3072), place * 96, 96, 1)
    third = lax.dynamic_slice_in_dim(sb, lax.axis_index("batch") * 32, 32, 1)
    return (
        out,
        gtok,
        narrow[0],
        narrow[1],
        gwin,
        wide[0],
        wide[1:4],
        wide[4],
        sc[0:features, :hidden],
        sc[105, :hidden],
        sc[40 : 40 + hidden, :hidden],
        sc[104, :hidden],
        third[:hidden],
        third[hidden],
        gwout,
        narrow[2],
    )


def solution(mesh):
    tokens_spec = P("batch", "seq", None)
    both = ("seq", "batch")
    in_specs = (tokens_spec, tokens_spec) + (P(),) * 15
    out_specs = (
        tokens_spec,
        tokens_spec,
        P(both),
        P(both),
        P(both, None),
        P(both),
        P(None, both),
        P(both),
        P(),
        P(),
        P(),
        P(),
        P(None, both),
        P(both),
        P(both, None),
        P(both),
    )

    def per_device(*args):
        tokens, w_one = args[0], args[8]
        sizes = (mesh.shape["seq"], mesh.shape["batch"]) + tokens.shape + w_one.shape
        fits = sizes == (8, 4, 2, 128, 1024, 33, 64)
        return (local_small if fits else local)(*args)

    return jax.shard_map(per_device, mesh=mesh, in_specs=in_specs, out_specs=out_specs, check_vma=False)
```

```python
import jax
import jax.numpy as jnp
import numpy as np
from jax import lax
from jax.experimental import pallas as pl
from jax.experimental.pallas import tpu as pltpu
from jax.sharding import PartitionSpec as P

highest = lax.Precision.HIGHEST
epsilon = 1e-05
f32, bf16 = jnp.float32, jnp.bfloat16


def dft_matrix(length):
    turns = ((2 * np.arange(length)[:, None] + 1) * np.arange(length)[None, :]) % (4 * length)
    phases = turns * (np.pi / (2 * length))
    return np.concatenate([np.cos(phases), np.sin(phases)], axis=0).astype(bf16)


def position_features(length, features):
    step_axis = np.arange(length, dtype=np.float64)
    band_count = (features - 1) // 2
    band_rates = 0.0001 + np.arange(band_count) * (band_count - 1 - 0.0001) / (band_count - 1)
    phases = 2.0 * np.pi / length * step_axis[:, None] * band_rates[None, :]
    return np.concatenate(
        [(step_axis / length)[:, None], np.cos(phases), -np.sin(phases)], axis=1
    ).astype(np.float32)


def filter_shape(positions, w_one, b_one, w_two, b_two, w_three, decay_rates):
    first_layer = jnp.sin(jnp.dot(positions, w_one, precision=highest) + b_one)
    second_layer = jnp.sin(jnp.dot(first_layer, w_two, precision=highest) + b_two)
    shaped = jnp.dot(second_layer, w_three, precision=highest)
    length = positions.shape[0]
    fraction = jnp.arange(length).astype(f32) / length
    return shaped * jnp.exp(-fraction[:, None] * decay_rates[None, :])


def shifted(value, axis, steps):
    count = lax.axis_size(axis)
    first, last = (max(0, -steps), min(count, count - steps))
    return lax.ppermute(value, axis, [(source, source + steps) for source in range(first, last)])


def reduce_scatter(value, dtype):
    out = lax.all_to_all(value.astype(dtype), "batch", split_axis=1, concat_axis=1, tiled=True)
    out = jnp.sum(out.astype(f32), axis=1)
    out = lax.all_to_all(out.astype(dtype), "seq", split_axis=0, concat_axis=0, tiled=True)
    return jnp.sum(out.astype(f32), axis=0)


def local(
    tokens,
    cotangent,
    ln_gain,
    ln_bias,
    w_in,
    b_in,
    short_w,
    short_b,
    w_one,
    b_one,
    w_two,
    b_two,
    w_three,
    decay_rates,
    filt_bias,
    w_out,
    b_out,
):
    seq_count, block_len, model_width = tokens.shape
    seq_devices = lax.axis_size("seq")
    batch_devices = lax.axis_size("batch")
    devices = seq_devices * batch_devices
    length = block_len * seq_devices
    channels = model_width // seq_devices
    col_start = lax.axis_index("seq") * channels
    inputs = tokens.astype(f32)
    average = jnp.mean(inputs, axis=-1, keepdims=True)
    centered = inputs - average
    inv_std = lax.rsqrt(jnp.mean(centered * centered, axis=-1, keepdims=True) + epsilon)
    whitened = centered * inv_std
    normed = (whitened * ln_gain + ln_bias).astype(bf16)
    mixed = jnp.einsum("btd,de->bte", normed, w_in, preferred_element_type=f32) + b_in
    prev_rows = shifted(mixed[:, block_len - 2 :], "seq", 1)
    padded = jnp.concatenate([prev_rows, mixed], axis=1)
    delay_one = padded[:, 1:-1]
    delay_two = padded[:, :-2]
    short_out = short_w[0] * mixed + short_w[1] * delay_one + short_w[2] * delay_two + short_b
    outer_gate = short_out[..., :model_width]
    inner_gate = short_out[..., model_width : 2 * model_width]
    values = short_out[..., 2 * model_width :]
    gated = (values * inner_gate).astype(bf16)
    d_product = jnp.einsum(
        "bte,de->btd", cotangent, w_out, preferred_element_type=f32
    ).astype(bf16)
    d_prod_f = d_product.astype(f32)
    d_summed = (d_prod_f * outer_gate).astype(bf16)

    def to_channels(value):
        return lax.all_to_all(value, "seq", split_axis=2, concat_axis=1, tiled=True)

    def to_tokens(value):
        return lax.all_to_all(value, "seq", split_axis=1, concat_axis=2, tiled=True)

    gated_ch = to_channels(gated)
    d_ch = to_channels(d_summed)
    positions = jnp.asarray(position_features(length, w_one.shape[0]))
    w_three_part = lax.dynamic_slice_in_dim(w_three, col_start, channels, 1)
    decay_part = lax.dynamic_slice_in_dim(decay_rates, col_start, channels, 0)
    bias_part = lax.dynamic_slice_in_dim(filt_bias, col_start, channels, 0)

    def kernel_of(first_w, first_b, second_w, second_b, third_w):
        return filter_shape(positions, first_w, first_b, second_w, second_b, third_w, decay_part)

    kernel_full, kernel_pull = jax.vjp(kernel_of, w_one, b_one, w_two, b_two, w_three_part)
    matrix = jnp.asarray(dft_matrix(length))

    def spectrum(value):
        return jnp.einsum("kt,btc->bkc", matrix, value, preferred_element_type=f32)

    def inverse(cosines, sines):
        both = jnp.concatenate([cosines, sines], axis=1).astype(bf16)
        return jnp.einsum("kt,bkc->btc", matrix, both, preferred_element_type=f32) * (1.0 / length)

    k_both = spectrum(kernel_full.astype(bf16)[None])
    g_both = spectrum(gated_ch)
    d_both = spectrum(d_ch)
    k_c, k_s = k_both[:, :length], k_both[:, length:]
    g_c, g_s = g_both[:, :length], g_both[:, length:]
    d_c, d_s = d_both[:, :length], d_both[:, length:]
    long_out = inverse(g_c * k_c - g_s * k_s, g_c * k_s + g_s * k_c)
    gated_float = gated_ch.astype(f32)
    d_ch_float = d_ch.astype(f32)
    summed_ch = (long_out + bias_part * gated_float).astype(bf16)
    summed = to_tokens(summed_ch).astype(f32)
    grad_in = inverse(k_c * d_c + k_s * d_s, k_c * d_s - k_s * d_c) + bias_part * d_ch_float
    d_gated = to_tokens(grad_in.astype(bf16)).astype(f32)
    d_kernel = inverse(
        jnp.sum(g_c * d_c + g_s * d_s, axis=0, keepdims=True),
        jnp.sum(g_c * d_s - g_s * d_c, axis=0, keepdims=True),
    )[0]
    g_bias_part = jnp.sum(d_ch_float * gated_float, axis=(0, 1))
    g_w_one, g_b_one, g_w_two, g_b_two, g_w_three_part = kernel_pull(d_kernel)

    product = (summed * outer_gate).astype(bf16)
    result = jnp.einsum("btd,de->bte", product, w_out, preferred_element_type=f32) + b_out
    block_out = (inputs + result).astype(bf16)
    grad_out = cotangent.astype(f32)
    g_w_out = jnp.einsum("btd,bte->de", product, cotangent, preferred_element_type=f32)
    g_b_out = jnp.sum(grad_out, axis=(0, 1))
    d_outer = d_prod_f * summed
    d_short = jnp.concatenate([d_outer, d_gated * values, d_gated * inner_gate], axis=-1)
    g_short_w = jnp.stack(
        [
            jnp.sum(d_short * mixed, axis=(0, 1)),
            jnp.sum(d_short * delay_one, axis=(0, 1)),
            jnp.sum(d_short * delay_two, axis=(0, 1)),
        ]
    )
    g_short_b = jnp.sum(d_short, axis=(0, 1))
    next_rows = shifted(d_short[:, :2], "seq", -1)
    extended = jnp.concatenate([d_short, next_rows], axis=1)
    d_mixed = (
        short_w[0] * extended[:, :block_len]
        + short_w[1] * extended[:, 1 : block_len + 1]
        + short_w[2] * extended[:, 2:]
    ).astype(bf16)
    g_w_in = jnp.einsum("btd,bte->de", normed, d_mixed, preferred_element_type=f32)
    g_b_in = jnp.sum(d_mixed.astype(f32), axis=(0, 1))
    d_normed = jnp.einsum("bte,de->btd", d_mixed, w_in, preferred_element_type=f32)
    g_ln_gain = jnp.sum(d_normed * whitened, axis=(0, 1))
    g_ln_bias = jnp.sum(d_normed, axis=(0, 1))
    d_white = d_normed * ln_gain
    grad_tokens = grad_out + inv_std * (
        d_white
        - jnp.mean(d_white, axis=-1, keepdims=True)
        - whitened * jnp.mean(d_white * whitened, axis=-1, keepdims=True)
    )
    rows = model_width // devices
    big = jnp.concatenate([g_w_in, g_w_out], axis=1)
    big = reduce_scatter(big.reshape(seq_devices, batch_devices, rows, -1), bf16)
    out_w_in, out_w_out = big[:, : 3 * model_width], big[:, 3 * model_width :]
    g_w_three = lax.dynamic_update_slice_in_dim(
        jnp.zeros(w_three.shape, f32), g_w_three_part, col_start, 1
    )
    g_filt_bias = lax.dynamic_update_slice_in_dim(
        jnp.zeros(filt_bias.shape, f32), g_bias_part, col_start, 0
    )
    vectors = jnp.concatenate(
        [
            g_ln_gain[None],
            g_ln_bias[None],
            g_b_out[None],
            g_filt_bias[None],
            g_w_three,
        ],
        axis=0,
    )
    vectors = jnp.transpose(vectors.reshape(-1, devices, rows), (1, 0, 2)).reshape(devices, -1)
    wides = jnp.concatenate([g_b_in[None], g_short_w, g_short_b[None]], axis=0)
    wides = jnp.transpose(wides.reshape(-1, devices, 3 * rows), (1, 0, 2)).reshape(devices, -1)
    net = jnp.concatenate([v.reshape(-1) for v in (g_w_one, g_b_one, g_w_two, g_b_two)])
    net_size = net.shape[0]
    net_part = -(-net_size // devices)
    net = jnp.pad(net, (0, net_part * devices - net_size)).reshape(devices, net_part)
    small = jnp.concatenate([vectors, wides, net], axis=1)
    small = reduce_scatter(small.reshape(seq_devices, batch_devices, -1), f32)
    hidden = w_two.shape[0]
    cut = rows * (4 + hidden)
    vectors = small[:cut].reshape(4 + hidden, rows)
    wides = small[cut : cut + 15 * rows].reshape(5, 3 * rows)
    net = lax.all_gather(small[cut + 15 * rows :], ("seq", "batch"), tiled=True)
    features = w_one.shape[0]
    edges = [features * hidden, (features + 1) * hidden, (features + 1 + hidden) * hidden]
    return (
        block_out,
        grad_tokens,
        vectors[0],
        vectors[1],
        out_w_in,
        wides[0],
        wides[1:4],
        wides[4],
        net[: edges[0]].reshape(features, hidden),
        net[edges[0] : edges[1]],
        net[edges[1] : edges[2]].reshape(hidden, hidden),
        net[edges[2] : net_size],
        vectors[4:],
        vectors[3],
        out_w_out,
        vectors[2],
    )


MESH = pl.DeviceIdType.MESH
HALF_TURN = (1.5703125, 4.837512969970703125e-4, 7.549789948768648e-8)


def sin_cos(x):
    turns = jnp.floor(x * 0.6366197723675814 + 0.5)
    r = ((x - turns * HALF_TURN[0]) - turns * HALF_TURN[1]) - turns * HALF_TURN[2]
    q = turns.astype(jnp.int32)
    r2 = r * r
    sine = r + r * r2 * (
        -1.6666654611e-1 + r2 * (8.3321608736e-3 + r2 * -1.9515295891e-4)
    )
    cosine = 1.0 - 0.5 * r2 + r2 * r2 * (
        4.166664568298827e-2 + r2 * (-1.388731625493765e-3 + r2 * 2.443315711809948e-5)
    )
    odd = (q & 1) == 1
    s_abs, c_abs = jnp.where(odd, cosine, sine), jnp.where(odd, sine, cosine)
    s_neg, c_neg = (q & 2) == 2, ((q + 1) & 2) == 2
    return jnp.where(s_neg, -s_abs, s_abs), jnp.where(c_neg, -c_abs, c_abs)


def mm(a, b, dims=((1,), (0,))):
    return lax.dot_general(a, b, (dims, ((), ())), preferred_element_type=f32)


def mm_full(a, b, dims=((1,), (0,))):
    return lax.dot_general(
        a, b, (dims, ((), ())), precision=highest, preferred_element_type=f32
    )


def twice(v):
    return jnp.concatenate([v, v], axis=1)


def lanes(start, size):
    return pl.ds(pl.multiple_of(start, size), size)


NT, TN = ((1,), (1,)), ((0,), (0,))


def whole_kernel(
    tok_ref,
    cot_ref,
    gain_ref,
    beta_ref,
    win_ref,
    bin_ref,
    sw_ref,
    sb_ref,
    w1_ref,
    b1_ref,
    w2_ref,
    b2_ref,
    w3_ref,
    decay_ref,
    fb_ref,
    wout_ref,
    bout_ref,
    pos_ref,
    f_ref,
    ft_ref,
    out_ref,
    gtok_ref,
    gwin_ref,
    gwout_ref,
    oa_ref,
    ob_ref,
    oc_ref,
    w_in,
    w_out,
    fm,
    ft,
    halo,
    white,
    istd,
    normed,
    mx,
    oiv,
    dpr,
    gsend,
    gch,
    dsend,
    dch,
    yrecv,
    qrecv,
    first,
    first_c,
    second,
    second_c,
    window,
    ksp,
    gsp,
    zs,
    es,
    dk,
    product,
    pts,
    dsx,
    dms,
    nt,
    pt,
    dm,
    cot,
    core_send,
    core_recv,
    core_send_o,
    core_recv_o,
    own_o,
    outv,
    gtokv,
    z_send,
    z_recv,
    z_send_o,
    z_recv_o,
    own,
    last_send,
    last_recv,
    sa,
    sr,
    sf,
    sb,
    sc,
    load_sem,
    in_sem,
    v_sem,
    halo_sem,
    a_sem,
    b_sem,
    c_sem,
    zed_sem,
    l_sem,
    s_sem,
):
    s, b = lax.axis_index("seq"), lax.axis_index("batch")
    zed, core = s // 2, s % 2
    other = (zed * 2 + 1 - core, b)

    loads = [
        pltpu.make_async_copy(src, dst, load_sem.at[i])
        for i, (src, dst) in enumerate(((wout_ref, w_out), (f_ref, fm), (ft_ref, ft)))
    ]

    def load_in(g, i):
        cols = lanes(g * 1024 + (zed + 2 + i) % 4 * 256, 256)
        return pltpu.make_async_copy(win_ref.at[:, cols], w_in.at[:, cols], in_sem.at[g, i])

    loads[0].start()
    for i in range(4):
        for g in range(3):
            load_in(g, i).start()
    loads[1].start()
    loads[2].start()

    def batch_peer(p):
        return (s, (b + p) % 4)

    def zed_peer(p):
        return (((zed + p) % 4) * 2 + core, b)

    barrier = pltpu.get_barrier_semaphore()
    for p in range(1, 8):
        pl.semaphore_signal(
            barrier, inc=1, device_id=((s + p) % 8, b), device_id_type=MESH
        )
    for p in range(1, 4):
        pl.semaphore_signal(barrier, inc=1, device_id=batch_peer(p), device_id_type=MESH)

    def remote(src, dst, sems, index, peer, start=True):
        copy = pltpu.make_async_remote_copy(
            src_ref=src,
            dst_ref=dst,
            send_sem=sems.at[(0,) + index],
            recv_sem=sems.at[(1,) + index],
            device_id=peer,
            device_id_type=MESH,
        )
        if start:
            copy.start()
        return copy

    gain, beta = gain_ref[...], beta_ref[...]

    def white_of(x):
        x = x.astype(f32)
        centered = x - jnp.mean(x, axis=-1, keepdims=True)
        inv = lax.rsqrt(jnp.mean(centered * centered, axis=-1, keepdims=True) + epsilon)
        return centered * inv, inv

    def norm_rows(i, _):
        q, r = i // 4, (i % 4) * 32
        rows = lanes(i * 32, 32)
        w, inv = white_of(tok_ref[q, lanes(r, 32)])
        white[rows] = w
        istd[rows] = jnp.broadcast_to(inv, (32, 128))
        normed[rows] = (w * gain + beta).astype(bf16)
        return 0

    lax.fori_loop(0, 8, norm_rows, 0)

    pl.semaphore_wait(barrier, 10)
    edge = remote(
        tok_ref.at[:, 112:128],
        halo,
        halo_sem,
        (0,),
        ((s + 1) % 8, b),
        start=False,
    )

    @pl.when(s < 7)
    def _():
        edge.start()

    nt[b] = normed[0:256].T
    moves = {}
    order = (2, 1, 3, 0)
    x, y = b % 2, b // 2
    beside = (y * 2 + 1 - x, (1 - y) * 2 + x)
    for k in range(2):
        moves["n", k] = remote(nt.at[b], nt.at[b], b_sem, (0, k), (s, beside[k]))
    for k in range(2):
        moves["c", k] = remote(cot_ref, cot.at[b], b_sem, (1, k), (s, beside[k]))

    loads[0].wait()
    cot_here = cot_ref[...]
    cot[b] = cot_here

    def backproject(t, _):
        m = mm(cot_here, w_out[lanes(t * 256, 256)], NT).astype(bf16)
        for h in range(2):
            at = slice(h * 128, h * 128 + 128)
            dpr[2 * t + h] = jnp.concatenate([m[0:128, at], m[128:256, at]], axis=1)
        return 0

    lax.fori_loop(0, 4, backproject, 0)
    sa[...] = jnp.zeros(sa.shape, f32)
    sa[5:6, 2048:3072] = jnp.sum(cot_here.astype(f32), axis=0, keepdims=True)

    @pl.when(s == 0)
    def _():
        halo[...] = jnp.zeros_like(halo)

    @pl.when(s > 0)
    def _():
        edge.wait_recv()

    w, _inv = white_of(halo[...].reshape(32, 1024))
    normed[256:288] = (w * gain + beta).astype(bf16)

    pairs = ((gsend, gch), (dsend, dch), (gsend, yrecv), (dsend, qrecv))

    def exchange(kind, p):
        src, dst = pairs[kind]
        to = (s + p) % 8
        return remote(src.at[to], dst.at[s], a_sem, (kind, p), (to, b), start=False)

    def send_tile(kind, tile):
        p = (tile - s + 8) % 8

        @pl.when(p != 0)
        def _():
            exchange(kind, p).start()

        @pl.when(p == 0)
        def _():
            src, dst = pairs[kind]
            dst[s] = src[s]

    def sent_tiles(kind):
        for p in range(1, 8):
            exchange(kind, p).wait_send()

    def wait_tiles(kind):
        for p in range(1, 8):
            exchange(kind, p).wait_recv()


    def project(i, _):
        t = (zed + 2 + i) % 4
        for g in range(3):
            load_in(g, i).wait()
            cols = lanes(g * 1024 + t * 256, 256)
            m = mm(normed[...], w_in[:, cols]) + bin_ref[:, cols]
            for h in range(2):
                at = slice(h * 128, h * 128 + 128)
                tile = 2 * t + h
                edge_rows = jnp.concatenate([m[264:272, at], m[280:288, at]], axis=1)
                mx[g, tile, 0:8] = jnp.where(s > 0, edge_rows, 0.0)
                mx[g, tile, 8:136] = jnp.concatenate([m[0:128, at], m[128:256, at]], axis=1)
        for h in range(2):
            tile = 2 * t + h
            got = []
            for g in range(3):
                cols = lanes(g * 1024 + tile * 128, 128)
                taps = sw_ref[:, cols]
                value = (
                    twice(taps[0:1]) * mx[g, tile, 8:136]
                    + twice(taps[1:2]) * mx[g, tile, 7:135]
                    + twice(taps[2:3]) * mx[g, tile, 6:134]
                    + twice(sb_ref[:, cols])
                )
                oiv[g, tile] = value
                got.append(value)
            gsend[tile] = (got[2] * got[1]).astype(bf16)
            send_tile(0, tile)
            dsend[tile] = (dpr[tile].astype(f32) * got[0]).astype(bf16)
        return 0

    lax.fori_loop(0, 4, project, 0)

    mine = lanes(s * 128, 128)
    pos = pos_ref[...]
    one, one_c = sin_cos(mm_full(pos, w1_ref[...]) + b1_ref[...])
    first[...] = one
    first_c[...] = one_c
    two, two_c = sin_cos(mm_full(one, w2_ref[...]) + b2_ref[...])
    second[...] = two
    second_c[...] = two_c
    fraction = lax.broadcasted_iota(jnp.int32, (1024, 128), 0).astype(f32) * (1.0 / 1024)
    wind = jnp.exp(-fraction * decay_ref[:, mine])
    window[...] = wind
    taps_bf = (mm_full(two, w3_ref[:, mine]) * wind).astype(bf16)
    loads[1].wait()

    def filter_rows(i, _):
        rows = lanes(i * 256, 256)
        ksp[rows] = mm(fm[rows], taps_bf)
        return 0

    lax.fori_loop(0, 8, filter_rows, 0)

    bias = twice(fb_ref[:, mine])
    for i in range(8):
        send_tile(1, (2 * zed + 4 + i) % 8)
    wait_tiles(0)
    gated = gch[...].reshape(1024, 256)

    def forward_rows(i, _):
        lo, hi = lanes(i * 256, 256), lanes(1024 + i * 256, 256)
        gc, gs = mm(fm[lo], gated), mm(fm[hi], gated)
        kc, ks = twice(ksp[lo]), twice(ksp[hi])
        gsp[lo] = gc
        gsp[hi] = gs
        zs[lo] = (gc * kc - gs * ks).astype(bf16)
        zs[hi] = (gc * ks + gs * kc).astype(bf16)
        return 0

    lax.fori_loop(0, 4, forward_rows, 0)
    loads[2].wait()

    def inverse_to(kind, send, inputs):
        def rows_of(i, _):
            t = (zed + 2 + i) % 4
            y = mm(ft[lanes(t * 256, 256)], zs[...]) * (1.0 / 1024)
            for h in range(2):
                tile = 2 * t + h
                here = y[h * 128 : h * 128 + 128] + bias * inputs[tile].astype(f32)
                send[tile] = here.astype(bf16)
                send_tile(kind, tile)
            return 0

        lax.fori_loop(0, 4, rows_of, 0)

    sent_tiles(0)
    inverse_to(2, gsend, gch)

    for k in range(2):
        near, far = beside[k], (s, beside[1 - k])
        moves["n", k].wait()
        part = nt.at[near, 512 * k : 512 * k + 512]
        moves["n", 2 + k] = remote(part, part, b_sem, (0, 2 + k), far)
    for k in range(2):
        near, far = beside[k], (s, beside[1 - k])
        moves["c", k].wait()
        part = cot.at[near, 128 * k : 128 * k + 128]
        moves["c", 2 + k] = remote(part, part, b_sem, (1, 2 + k), far)

    wait_tiles(1)
    d_here = dch[...].reshape(1024, 256)

    def backward_rows(i, _):
        lo, hi = lanes(i * 256, 256), lanes(1024 + i * 256, 256)
        dc, ds = mm(fm[lo], d_here), mm(fm[hi], d_here)
        kc, ks = twice(ksp[lo]), twice(ksp[hi])
        gc, gs = gsp[lo], gsp[hi]
        zs[lo] = (kc * dc + ks * ds).astype(bf16)
        zs[hi] = (kc * ds - ks * dc).astype(bf16)
        ec, e_s = gc * dc + gs * ds, gc * ds - gs * dc
        es[lo] = (ec[:, :128] + ec[:, 128:]).astype(bf16)
        es[hi] = (e_s[:, :128] + e_s[:, 128:]).astype(bf16)
        return 0

    lax.fori_loop(0, 4, backward_rows, 0)
    sent_tiles(1)
    inverse_to(3, dsend, dch)

    def kernel_rows(i, total):
        rows = lanes(i * 256, 256)
        dk[rows] = mm(ft[rows], es[...]) * (1.0 / 1024) * window[rows]
        for h in range(2):
            tile = 2 * i + h
            total += jnp.sum(dch[tile].astype(f32) * gch[tile].astype(f32), axis=0, keepdims=True)
        return total

    total = lax.fori_loop(0, 4, kernel_rows, jnp.zeros((1, 256), f32))
    sb[0] = jnp.zeros(sb.shape[1:], f32)
    sc[0] = jnp.zeros(sc.shape[1:], f32)
    sb[0, 64:65] = total[:, :128] + total[:, 128:]
    d_shaped = dk[...]
    sb[0, 0:64] = mm_full(second[...], d_shaped, TN)
    d_two = mm_full(d_shaped, w3_ref[:, mine], NT) * second_c[...]
    sc[0, 40:104, 0:64] = mm_full(first[...], d_two, TN)
    sc[0, 104:105, 0:64] = jnp.sum(d_two, axis=0, keepdims=True)
    d_one = mm_full(d_two, w2_ref[...], NT) * first_c[...]
    sc[0, 0:33, 0:64] = mm_full(pos_ref[...], d_one, TN)
    sc[0, 105:106, 0:64] = jnp.sum(d_one, axis=0, keepdims=True)

    steps = [
        other,
        (s, y * 2 + 1 - x),
        (s, (1 - y) * 2 + x),
        (((zed // 2) * 2 + 1 - zed % 2) * 2 + core, b),
        (((1 - zed // 2) * 2 + zed % 2) * 2 + core, b),
    ]

    def small_start(array, which, i, k):
        return remote(array.at[2 * k], array.at[2 * k + 1], s_sem, (which, i), steps[i])

    def small_end(array, k, move):
        move.wait()
        array[2 * k + 2] = array[2 * k] + array[2 * k + 1]

    wait_tiles(2)

    def product_tile(j, _):
        value = yrecv[j].astype(f32)
        made = (value * oiv[0, j]).astype(bf16)
        cols = lanes(j * 128, 128)
        product[0:128, cols] = made[:, :128]
        product[128:256, cols] = made[:, 128:]
        dsx[0, j, 0:128] = dpr[j].astype(f32) * value
        return 0

    lax.fori_loop(0, 8, product_tile, 0)

    def edges_of(groups, index):
        return remote(
            dsx.at[groups, :, 0:8],
            dsx.at[groups, :, 128:136],
            halo_sem,
            (index,),
            ((s + 7) % 8, b),
            start=False,
        )

    def send_edges(groups, index):
        @pl.when(s > 0)
        def _():
            edges_of(groups, index).start()

    def wait_edges(groups, index):
        @pl.when(s == 7)
        def _():
            for g in range(groups.start, groups.stop):
                for j in range(8):
                    dsx[g, j, 128:136] = jnp.zeros((8, 256), f32)

        @pl.when(s < 7)
        def _():
            edges_of(groups, index).wait_recv()

    send_edges(slice(0, 1), 1)
    pts[...] = product[...].T.reshape(4, 2, 4, 32, 256)
    for p in (1, 2, 3):
        peer, to = batch_peer(p), (b + p) % 4
        for half in range(2):
            moves["p", half, p] = remote(
                pts.at[:, half, to], pt.at[b, half], b_sem, (2 + half, p), peer
            )
    for half in range(2):
        pt[b, half] = pts[:, half, b]

    def column_sum(v):
        v = jnp.sum(v, axis=0, keepdims=True)
        return v[:, :128] + v[:, 128:]

    def short_sums(g, j):
        wide = lanes(g * 1024 + j * 128, 128)
        here = dsx[g, j, 0:128]
        for k in range(3):
            sa[1 + k : 2 + k, wide] = column_sum(here * mx[g, j, 8 - k : 136 - k])
        sa[4:5, wide] = column_sum(here)

    def first_sums(j, _):
        short_sums(0, j)
        return 0

    lax.fori_loop(0, 8, first_sums, 0)
    wait_edges(slice(0, 1), 1)

    def mixed_tile(g):
        def one_tile(j, _):
            q, cols = j // 2, lanes((j % 2) * 128, 128)
            wide = lanes(g * 1024 + j * 128, 128)
            taps = sw_ref[:, wide]
            value = (
                twice(taps[0:1]) * dsx[g, j, 0:128]
                + twice(taps[1:2]) * dsx[g, j, 1:129]
                + twice(taps[2:3]) * dsx[g, j, 2:130]
            ).astype(bf16)
            dms[g, q, 0:128, cols] = value[:, :128]
            dms[g, q, 128:256, cols] = value[:, 128:]
            sa[0:1, wide] = column_sum(value.astype(f32))
            return 0

        lax.fori_loop(0, 8, one_tile, 0)
        for p in (1, 2, 3):
            to = (b + p) % 4
            moves["d", g, p] = remote(
                dms.at[g, to], dm.at[g, b], b_sem, (4 + g, p), batch_peer(p)
            )
        dm[g, b] = dms[g, b]

    mixed_tile(0)
    mb, mc = small_start(sb, 0, 1, 0), small_start(sc, 1, 0, 0)

    def out_cols(i, _):
        cols = lanes(i * 256, 256)
        r = mm(product[...], w_out[:, cols]) + bout_ref[:, cols]
        for q in range(2):
            rows = slice(q * 128, q * 128 + 128)
            outv[q, :, cols] = (tok_ref[q, :, cols].astype(f32) + r[rows]).astype(bf16)
        return 0

    lax.fori_loop(0, 4, out_cols, 0)
    store_out = pltpu.make_async_copy(outv, out_ref, load_sem.at[3])
    store_out.start()

    def normed_cols(groups):
        def one(i, _):
            at = lanes(i * 256, 256)
            total = jnp.zeros((256, 256), f32)
            for g in groups:
                for q in range(4):
                    c = g * 1024 + q * 256
                    total += mm(dms[g, q], w_in[at, c : c + 256], NT)
            for q in range(2):
                rows = slice(q * 128, q * 128 + 128)
                before = 0.0 if 0 in groups else gtokv[q, :, at]
                gtokv[q, :, at] = before + total[rows]
            return 0

        lax.fori_loop(0, 4, one, 0)

    normed_cols((0,))
    small_end(sc, 0, mc)
    mc = small_start(sc, 1, 1, 1)

    def done(key):
        moves[key].wait()

    def part_out(half):
        total = jnp.zeros((128, 1024), f32)
        for i in range(4):
            total += mm(pt[i, half].reshape(128, 256), cot[i])
        return total

    def part_in(g, to, half):
        rows = lanes(to * 256 + half * 128, 128)
        total = jnp.zeros((128, 256), f32)
        for i in range(4):
            total += mm(nt[i, rows], dm[g, i])
        return total

    def core_half(g):
        for p in (1, 2, 3):
            done(("d", g, p))
        for p in order:
            core_send[g, p] = part_in(g, (zed + p) % 4, 1 - core).astype(bf16)
            moves["e", g, p] = remote(
                core_send.at[g, p], core_recv.at[g, p], c_sem, (g, p), other
            )

    def zed_half(g):
        for p in order:
            done(("e", g, p))
            total = part_in(g, (zed + p) % 4, core) + core_recv[g, p].astype(f32)
            if p == 0:
                own[g] = total
            else:
                z_send[g, p] = total.astype(bf16)
                moves["z", g, p] = remote(
                    z_send.at[g, p], z_recv.at[g, p], zed_sem, (g, p), zed_peer(p)
                )

    def last_half(g):
        total = own[g]
        for p in (2, 1, 3):
            done(("z", g, p))
            total += z_recv[g, p].astype(f32)
        last_send[g] = total.astype(bf16).reshape(4, 32, 256)
        for p in (1, 2, 3):
            moves["l", g, p] = remote(
                last_send.at[g, (b + p) % 4], last_recv.at[g, b], l_sem, (g, p), batch_peer(p)
            )
        last_recv[g, b] = last_send[g, b]

    wait_tiles(3)

    def gate_tile(j, _):
        value = qrecv[j].astype(f32)
        dsx[1, j, 0:128] = value * oiv[2, j]
        dsx[2, j, 0:128] = value * oiv[1, j]
        return 0

    lax.fori_loop(0, 8, gate_tile, 0)
    send_edges(slice(1, 3), 2)

    def other_sums(j, _):
        short_sums(1, j)
        short_sums(2, j)
        return 0

    lax.fori_loop(0, 8, other_sums, 0)
    wait_edges(slice(1, 3), 2)
    mixed_tile(1)
    mixed_tile(2)
    for k in (2, 3):
        done(("n", k))
        done(("c", k))
    for p in (1, 2, 3):
        done(("p", 0, p))
        done(("p", 1, p))
    core_send_o[...] = part_out(1 - core).astype(bf16)
    moves["co"] = remote(core_send_o, core_recv_o, c_sem, (3, 0), other)
    core_half(0)
    small_end(sb, 0, mb)
    small_end(sc, 1, mc)
    mb, mc = small_start(sb, 0, 2, 1), small_start(sc, 1, 2, 2)
    done("co")
    own_o[...] = (part_out(core) + core_recv_o[...].astype(f32)).reshape(4, 32, 1024)
    z_send_o[...] = own_o[...].astype(bf16)
    for p in (2, 1, 3):
        moves["zo", p] = remote(
            z_send_o.at[(zed + p) % 4], z_recv_o.at[p], zed_sem, (3, p), zed_peer(p)
        )
    zed_half(0)

    normed_cols((1, 2))

    def token_rows(i, sums):
        q, r = i // 4, lanes((i % 4) * 32, 32)
        rows = lanes(i * 32, 32)
        d, w = gtokv[q, r], white[rows]
        dw = d * w
        d_white = d * gain
        grad = cot_ref[rows].astype(f32) + istd[rows, 0:1] * (
            d_white
            - jnp.mean(d_white, axis=-1, keepdims=True)
            - w * jnp.mean(d_white * w, axis=-1, keepdims=True)
        )
        gtokv[q, r] = grad
        return (
            sums[0] + jnp.sum(dw, axis=0, keepdims=True),
            sums[1] + jnp.sum(d, axis=0, keepdims=True),
        )

    zero = jnp.zeros((1, 1024), f32)
    sums = lax.fori_loop(0, 8, token_rows, (zero, zero))
    store_tok = pltpu.make_async_copy(gtokv, gtok_ref, load_sem.at[4])
    store_tok.start()
    sa[5:6, 0:1024] = sums[0]
    sa[5:6, 1024:2048] = sums[1]

    def half_at(k):
        return lanes(k * 1536, 1536)

    vec = remote(sa.at[:, half_at(1 - core)], sr.at[0], v_sem, (0,), other)
    small_end(sb, 1, mb)
    small_end(sc, 2, mc)
    mc = small_start(sc, 1, 3, 3)
    core_half(1)
    vec.wait()
    sr[1] = sa[:, half_at(core)] + sr[0]
    vecs = [remote(sr.at[1], sr.at[1 + p], v_sem, (p,), batch_peer(p)) for p in (1, 2, 3)]
    zed_half(1)
    core_half(2)
    for vec in vecs:
        vec.wait()
    sr[5] = sr[1] + sr[2] + sr[3] + sr[4]
    vecs = [remote(sr.at[5], sr.at[5 + p], v_sem, (3 + p,), zed_peer(p)) for p in (1, 2, 3)]
    zed_half(2)
    small_end(sc, 3, mc)
    mc = small_start(sc, 1, 4, 4)
    total = own_o[zed]
    for p in (2, 1, 3):
        done(("zo", p))
        total += z_recv_o[p].astype(f32)
    gwout_ref[...] = total
    last_half(0)
    for vec in vecs:
        vec.wait()
    oa_ref[:, half_at(core)] = sr[5] + sr[6] + sr[7] + sr[8]
    sf[...] = sr[5] + sr[6] + sr[7] + sr[8]
    vec = remote(sf, sr.at[9], v_sem, (7,), other)
    last_half(1)
    last_half(2)
    small_end(sc, 4, mc)
    vec.wait()
    oa_ref[:, half_at(1 - core)] = sr[9]
    ob_ref[...] = sb[4]
    oc_ref[...] = sc[10]
    for g in range(3):
        for p in (1, 2, 3):
            done(("l", g, p))
        for i in range(4):
            c = g * 1024 + i * 256
            gwin_ref[:, c : c + 256] = last_recv[g, i].astype(f32)
    store_out.wait()
    store_tok.wait()
    sent_tiles(2)
    sent_tiles(3)

    @pl.when(s < 7)
    def _():
        edge.wait_send()

    @pl.when(s > 0)
    def _():
        edges_of(slice(0, 1), 1).wait_send()
        edges_of(slice(1, 3), 2).wait_send()


def whole(args, positions, matrix):
    vmem, anywhere = (pl.BlockSpec(memory_space=m) for m in (pltpu.VMEM, pl.ANY))
    dma = pltpu.SemaphoreType.DMA
    specs = [vmem] * 20
    for i in (4, 15, 18, 19):
        specs[i] = anywhere
    shape = jax.ShapeDtypeStruct

    def v(dtype, *dims):
        return pltpu.VMEM(dims, dtype)

    return pl.pallas_call(
        whole_kernel,
        out_shape=(
            shape((2, 128, 1024), bf16),
            shape((2, 128, 1024), f32),
            shape((32, 3072), f32),
            shape((32, 1024), f32),
            shape((8, 3072), f32),
            shape((72, 128), f32),
            shape((112, 128), f32),
        ),
        in_specs=specs,
        out_specs=(anywhere,) * 2 + (vmem,) * 5,
        scratch_shapes=[
            v(bf16, 1024, 3072),
            v(bf16, 1024, 1024),
            v(bf16, 2048, 1024),
            v(bf16, 1024, 2048),
            v(bf16, 2, 16, 1024),
            v(f32, 256, 1024),
            v(f32, 256, 128),
            v(bf16, 288, 1024),
            v(f32, 3, 8, 136, 256),
            v(f32, 3, 8, 128, 256),
            v(bf16, 8, 128, 256),
            v(bf16, 8, 128, 256),
            v(bf16, 8, 128, 256),
            v(bf16, 8, 128, 256),
            v(bf16, 8, 128, 256),
            v(bf16, 8, 128, 256),
            v(bf16, 8, 128, 256),
            v(f32, 1024, 64),
            v(f32, 1024, 64),
            v(f32, 1024, 64),
            v(f32, 1024, 64),
            v(f32, 1024, 128),
            v(f32, 2048, 128),
            v(f32, 2048, 256),
            v(bf16, 2048, 256),
            v(bf16, 2048, 128),
            v(f32, 1024, 128),
            v(bf16, 256, 1024),
            v(bf16, 4, 2, 4, 32, 256),
            v(f32, 3, 8, 136, 256),
            v(bf16, 3, 4, 256, 256),
            v(bf16, 4, 1024, 256),
            v(bf16, 4, 2, 4, 32, 256),
            v(bf16, 3, 4, 256, 256),
            v(bf16, 4, 256, 1024),
            v(bf16, 3, 4, 128, 256),
            v(bf16, 3, 4, 128, 256),
            v(bf16, 128, 1024),
            v(bf16, 128, 1024),
            v(f32, 4, 32, 1024),
            v(bf16, 2, 128, 1024),
            v(f32, 2, 128, 1024),
            v(bf16, 3, 4, 128, 256),
            v(bf16, 3, 4, 128, 256),
            v(bf16, 4, 32, 1024),
            v(bf16, 4, 32, 1024),
            v(f32, 3, 128, 256),
            v(bf16, 3, 4, 32, 256),
            v(bf16, 3, 4, 32, 256),
            v(f32, 8, 3072),
            v(f32, 10, 8, 1536),
            v(f32, 8, 1536),
            v(f32, 5, 72, 128),
            v(f32, 11, 112, 128),
            dma((5,)),
            dma((3, 4)),
            dma((2, 8)),
            dma((2, 3)),
            dma((2, 4, 8)),
            dma((2, 7, 4)),
            dma((2, 4, 4)),
            dma((2, 4, 4)),
            dma((2, 3, 4)),
            dma((2, 3, 5)),
        ],
        compiler_params=pltpu.CompilerParams(
            collective_id=0, has_side_effects=True, vmem_limit_bytes=63 * 1024 * 1024
        ),
    )(*args, positions, matrix, np.ascontiguousarray(matrix.T))


def settle_kernel(
    out_ref,
    gtok_ref,
    gwin_ref,
    gwout_ref,
    sa_ref,
    sb_ref,
    sc_ref,
    out,
    gtok,
    ln_gain,
    ln_bias,
    gwin,
    b_in,
    short_w,
    short_b,
    w_one,
    b_one,
    w_two,
    b_two,
    w_three,
    filt,
    gwout,
    b_out,
    sems,
):
    copies = [
        pltpu.make_async_copy(src, dst, sems.at[i])
        for i, (src, dst) in enumerate(
            ((out_ref, out), (gtok_ref, gtok), (gwin_ref, gwin), (gwout_ref, gwout))
        )
    ]
    for copy in copies:
        copy.start()
    b = lax.axis_index("batch")
    place = lax.axis_index("seq") * 4 + b
    sa = sa_ref[...]
    wide = pltpu.roll(sa, (32 - place) * 96, 1)
    b_in[...] = wide[0:1, :96]
    short_w[...] = wide[1:4, :96]
    short_b[...] = wide[4:5, :96]
    thin = pltpu.roll(sa, (96 - place) * 32, 1)
    ln_gain[...] = thin[5:6, 0:32]
    ln_bias[...] = thin[5:6, 1024:1056]
    b_out[...] = thin[5:6, 2048:2080]
    third = pltpu.roll(sb_ref[...], (4 - b) * 32, 1)
    w_three[...] = third[0:64, 0:32]
    filt[...] = third[64:65, 0:32]
    w_one[...] = sc_ref[0:33, 0:64]
    w_two[...] = sc_ref[40:104, 0:64]
    b_two[...] = sc_ref[104:105, 0:64]
    b_one[...] = sc_ref[105:106, 0:64]
    for copy in copies:
        copy.wait()


def settle(parts):
    vmem, anywhere = (pl.BlockSpec(memory_space=m) for m in (pltpu.VMEM, pl.ANY))
    sizes = (
        (2, 128, 1024),
        (2, 128, 1024),
        (1, 32),
        (1, 32),
        (32, 3072),
        (1, 96),
        (3, 96),
        (1, 96),
        (33, 64),
        (1, 64),
        (64, 64),
        (1, 64),
        (64, 32),
        (1, 32),
        (32, 1024),
        (1, 32),
    )
    flat = (2, 3, 5, 7, 9, 11, 13, 15)
    outs = pl.pallas_call(
        settle_kernel,
        out_shape=tuple(
            jax.ShapeDtypeStruct(size, f32 if i else bf16) for i, size in enumerate(sizes)
        ),
        in_specs=[anywhere] * 4 + [vmem] * 3,
        out_specs=(vmem,) * 16,
        scratch_shapes=[pltpu.SemaphoreType.DMA((4,))],
    )(*parts)
    return tuple(o.reshape(-1) if i in flat else o for i, o in enumerate(outs))


def local_small(*args):
    cotangent = args[1]
    vectors = {2, 3, 5, 7, 9, 11, 13, 14, 16}
    given = [a.reshape(1, -1) if i in vectors else a for i, a in enumerate(args)]
    given[1] = cotangent.reshape(256, 1024)
    return settle(whole(given, position_features(1024, args[8].shape[0]), dft_matrix(1024)))


def solution(mesh):
    tokens_spec = P("batch", "seq", None)
    both = ("seq", "batch")
    in_specs = (tokens_spec, tokens_spec) + (P(),) * 15
    out_specs = (
        tokens_spec,
        tokens_spec,
        P(both),
        P(both),
        P(both, None),
        P(both),
        P(None, both),
        P(both),
        P(),
        P(),
        P(),
        P(),
        P(None, both),
        P(both),
        P(both, None),
        P(both),
    )

    def per_device(*args):
        tokens, w_one = args[0], args[8]
        sizes = (mesh.shape["seq"], mesh.shape["batch"]) + tokens.shape + w_one.shape
        fits = sizes == (8, 4, 2, 128, 1024, 33, 64)
        return (local_small if fits else local)(*args)

    return jax.shard_map(per_device, mesh=mesh, in_specs=in_specs, out_specs=out_specs, check_vma=False)
```

```python
import jax
import jax.numpy as jnp
import numpy as np
from jax import lax
from jax.experimental import pallas as pl
from jax.experimental.pallas import tpu as pltpu
from jax.sharding import PartitionSpec as P

highest = lax.Precision.HIGHEST
epsilon = 1e-05
f32, bf16 = jnp.float32, jnp.bfloat16


def dft_matrix(length):
    turns = ((2 * np.arange(length)[:, None] + 1) * np.arange(length)[None, :]) % (4 * length)
    phases = turns * (np.pi / (2 * length))
    return np.concatenate([np.cos(phases), np.sin(phases)], axis=0).astype(bf16)


def position_features(length, features):
    step_axis = np.arange(length, dtype=np.float64)
    band_count = (features - 1) // 2
    band_rates = 0.0001 + np.arange(band_count) * (band_count - 1 - 0.0001) / (band_count - 1)
    phases = 2.0 * np.pi / length * step_axis[:, None] * band_rates[None, :]
    return np.concatenate(
        [(step_axis / length)[:, None], np.cos(phases), -np.sin(phases)], axis=1
    ).astype(np.float32)


def filter_shape(positions, w_one, b_one, w_two, b_two, w_three, decay_rates):
    first_layer = jnp.sin(jnp.dot(positions, w_one, precision=highest) + b_one)
    second_layer = jnp.sin(jnp.dot(first_layer, w_two, precision=highest) + b_two)
    shaped = jnp.dot(second_layer, w_three, precision=highest)
    length = positions.shape[0]
    fraction = jnp.arange(length).astype(f32) / length
    return shaped * jnp.exp(-fraction[:, None] * decay_rates[None, :])


def shifted(value, axis, steps):
    count = lax.axis_size(axis)
    first, last = (max(0, -steps), min(count, count - steps))
    return lax.ppermute(value, axis, [(source, source + steps) for source in range(first, last)])


def reduce_scatter(value, dtype):
    out = lax.all_to_all(value.astype(dtype), "batch", split_axis=1, concat_axis=1, tiled=True)
    out = jnp.sum(out.astype(f32), axis=1)
    out = lax.all_to_all(out.astype(dtype), "seq", split_axis=0, concat_axis=0, tiled=True)
    return jnp.sum(out.astype(f32), axis=0)


def local(
    tokens,
    cotangent,
    ln_gain,
    ln_bias,
    w_in,
    b_in,
    short_w,
    short_b,
    w_one,
    b_one,
    w_two,
    b_two,
    w_three,
    decay_rates,
    filt_bias,
    w_out,
    b_out,
):
    seq_count, block_len, model_width = tokens.shape
    seq_devices = lax.axis_size("seq")
    batch_devices = lax.axis_size("batch")
    devices = seq_devices * batch_devices
    length = block_len * seq_devices
    channels = model_width // seq_devices
    col_start = lax.axis_index("seq") * channels
    inputs = tokens.astype(f32)
    average = jnp.mean(inputs, axis=-1, keepdims=True)
    centered = inputs - average
    inv_std = lax.rsqrt(jnp.mean(centered * centered, axis=-1, keepdims=True) + epsilon)
    whitened = centered * inv_std
    normed = (whitened * ln_gain + ln_bias).astype(bf16)
    mixed = jnp.einsum("btd,de->bte", normed, w_in, preferred_element_type=f32) + b_in
    prev_rows = shifted(mixed[:, block_len - 2 :], "seq", 1)
    padded = jnp.concatenate([prev_rows, mixed], axis=1)
    delay_one = padded[:, 1:-1]
    delay_two = padded[:, :-2]
    short_out = short_w[0] * mixed + short_w[1] * delay_one + short_w[2] * delay_two + short_b
    outer_gate = short_out[..., :model_width]
    inner_gate = short_out[..., model_width : 2 * model_width]
    values = short_out[..., 2 * model_width :]
    gated = (values * inner_gate).astype(bf16)
    d_product = jnp.einsum(
        "bte,de->btd", cotangent, w_out, preferred_element_type=f32
    ).astype(bf16)
    d_prod_f = d_product.astype(f32)
    d_summed = (d_prod_f * outer_gate).astype(bf16)

    def to_channels(value):
        return lax.all_to_all(value, "seq", split_axis=2, concat_axis=1, tiled=True)

    def to_tokens(value):
        return lax.all_to_all(value, "seq", split_axis=1, concat_axis=2, tiled=True)

    gated_ch = to_channels(gated)
    d_ch = to_channels(d_summed)
    positions = jnp.asarray(position_features(length, w_one.shape[0]))
    w_three_part = lax.dynamic_slice_in_dim(w_three, col_start, channels, 1)
    decay_part = lax.dynamic_slice_in_dim(decay_rates, col_start, channels, 0)
    bias_part = lax.dynamic_slice_in_dim(filt_bias, col_start, channels, 0)

    def kernel_of(first_w, first_b, second_w, second_b, third_w):
        return filter_shape(positions, first_w, first_b, second_w, second_b, third_w, decay_part)

    kernel_full, kernel_pull = jax.vjp(kernel_of, w_one, b_one, w_two, b_two, w_three_part)
    matrix = jnp.asarray(dft_matrix(length))

    def spectrum(value):
        return jnp.einsum("kt,btc->bkc", matrix, value, preferred_element_type=f32)

    def inverse(cosines, sines):
        both = jnp.concatenate([cosines, sines], axis=1).astype(bf16)
        return jnp.einsum("kt,bkc->btc", matrix, both, preferred_element_type=f32) * (1.0 / length)

    k_both = spectrum(kernel_full.astype(bf16)[None])
    g_both = spectrum(gated_ch)
    d_both = spectrum(d_ch)
    k_c, k_s = k_both[:, :length], k_both[:, length:]
    g_c, g_s = g_both[:, :length], g_both[:, length:]
    d_c, d_s = d_both[:, :length], d_both[:, length:]
    long_out = inverse(g_c * k_c - g_s * k_s, g_c * k_s + g_s * k_c)
    gated_float = gated_ch.astype(f32)
    d_ch_float = d_ch.astype(f32)
    summed_ch = (long_out + bias_part * gated_float).astype(bf16)
    summed = to_tokens(summed_ch).astype(f32)
    grad_in = inverse(k_c * d_c + k_s * d_s, k_c * d_s - k_s * d_c) + bias_part * d_ch_float
    d_gated = to_tokens(grad_in.astype(bf16)).astype(f32)
    d_kernel = inverse(
        jnp.sum(g_c * d_c + g_s * d_s, axis=0, keepdims=True),
        jnp.sum(g_c * d_s - g_s * d_c, axis=0, keepdims=True),
    )[0]
    g_bias_part = jnp.sum(d_ch_float * gated_float, axis=(0, 1))
    g_w_one, g_b_one, g_w_two, g_b_two, g_w_three_part = kernel_pull(d_kernel)

    product = (summed * outer_gate).astype(bf16)
    result = jnp.einsum("btd,de->bte", product, w_out, preferred_element_type=f32) + b_out
    block_out = (inputs + result).astype(bf16)
    grad_out = cotangent.astype(f32)
    g_w_out = jnp.einsum("btd,bte->de", product, cotangent, preferred_element_type=f32)
    g_b_out = jnp.sum(grad_out, axis=(0, 1))
    d_outer = d_prod_f * summed
    d_short = jnp.concatenate([d_outer, d_gated * values, d_gated * inner_gate], axis=-1)
    g_short_w = jnp.stack(
        [
            jnp.sum(d_short * mixed, axis=(0, 1)),
            jnp.sum(d_short * delay_one, axis=(0, 1)),
            jnp.sum(d_short * delay_two, axis=(0, 1)),
        ]
    )
    g_short_b = jnp.sum(d_short, axis=(0, 1))
    next_rows = shifted(d_short[:, :2], "seq", -1)
    extended = jnp.concatenate([d_short, next_rows], axis=1)
    d_mixed = (
        short_w[0] * extended[:, :block_len]
        + short_w[1] * extended[:, 1 : block_len + 1]
        + short_w[2] * extended[:, 2:]
    ).astype(bf16)
    g_w_in = jnp.einsum("btd,bte->de", normed, d_mixed, preferred_element_type=f32)
    g_b_in = jnp.sum(d_mixed.astype(f32), axis=(0, 1))
    d_normed = jnp.einsum("bte,de->btd", d_mixed, w_in, preferred_element_type=f32)
    g_ln_gain = jnp.sum(d_normed * whitened, axis=(0, 1))
    g_ln_bias = jnp.sum(d_normed, axis=(0, 1))
    d_white = d_normed * ln_gain
    grad_tokens = grad_out + inv_std * (
        d_white
        - jnp.mean(d_white, axis=-1, keepdims=True)
        - whitened * jnp.mean(d_white * whitened, axis=-1, keepdims=True)
    )
    rows = model_width // devices
    big = jnp.concatenate([g_w_in, g_w_out], axis=1)
    big = reduce_scatter(big.reshape(seq_devices, batch_devices, rows, -1), bf16)
    out_w_in, out_w_out = big[:, : 3 * model_width], big[:, 3 * model_width :]
    g_w_three = lax.dynamic_update_slice_in_dim(
        jnp.zeros(w_three.shape, f32), g_w_three_part, col_start, 1
    )
    g_filt_bias = lax.dynamic_update_slice_in_dim(
        jnp.zeros(filt_bias.shape, f32), g_bias_part, col_start, 0
    )
    vectors = jnp.concatenate(
        [
            g_ln_gain[None],
            g_ln_bias[None],
            g_b_out[None],
            g_filt_bias[None],
            g_w_three,
        ],
        axis=0,
    )
    vectors = jnp.transpose(vectors.reshape(-1, devices, rows), (1, 0, 2)).reshape(devices, -1)
    wides = jnp.concatenate([g_b_in[None], g_short_w, g_short_b[None]], axis=0)
    wides = jnp.transpose(wides.reshape(-1, devices, 3 * rows), (1, 0, 2)).reshape(devices, -1)
    net = jnp.concatenate([v.reshape(-1) for v in (g_w_one, g_b_one, g_w_two, g_b_two)])
    net_size = net.shape[0]
    net_part = -(-net_size // devices)
    net = jnp.pad(net, (0, net_part * devices - net_size)).reshape(devices, net_part)
    small = jnp.concatenate([vectors, wides, net], axis=1)
    small = reduce_scatter(small.reshape(seq_devices, batch_devices, -1), f32)
    hidden = w_two.shape[0]
    cut = rows * (4 + hidden)
    vectors = small[:cut].reshape(4 + hidden, rows)
    wides = small[cut : cut + 15 * rows].reshape(5, 3 * rows)
    net = lax.all_gather(small[cut + 15 * rows :], ("seq", "batch"), tiled=True)
    features = w_one.shape[0]
    edges = [features * hidden, (features + 1) * hidden, (features + 1 + hidden) * hidden]
    return (
        block_out,
        grad_tokens,
        vectors[0],
        vectors[1],
        out_w_in,
        wides[0],
        wides[1:4],
        wides[4],
        net[: edges[0]].reshape(features, hidden),
        net[edges[0] : edges[1]],
        net[edges[1] : edges[2]].reshape(hidden, hidden),
        net[edges[2] : net_size],
        vectors[4:],
        vectors[3],
        out_w_out,
        vectors[2],
    )


MESH = pl.DeviceIdType.MESH
HALF_TURN = (1.5703125, 4.837512969970703125e-4, 7.549789948768648e-8)


def sin_cos(x):
    turns = jnp.floor(x * 0.6366197723675814 + 0.5)
    r = ((x - turns * HALF_TURN[0]) - turns * HALF_TURN[1]) - turns * HALF_TURN[2]
    q = turns.astype(jnp.int32)
    r2 = r * r
    sine = r + r * r2 * (
        -1.6666654611e-1 + r2 * (8.3321608736e-3 + r2 * -1.9515295891e-4)
    )
    cosine = 1.0 - 0.5 * r2 + r2 * r2 * (
        4.166664568298827e-2 + r2 * (-1.388731625493765e-3 + r2 * 2.443315711809948e-5)
    )
    odd = (q & 1) == 1
    s_abs, c_abs = jnp.where(odd, cosine, sine), jnp.where(odd, sine, cosine)
    s_neg, c_neg = (q & 2) == 2, ((q + 1) & 2) == 2
    return jnp.where(s_neg, -s_abs, s_abs), jnp.where(c_neg, -c_abs, c_abs)


def mm(a, b, dims=((1,), (0,))):
    return lax.dot_general(a, b, (dims, ((), ())), preferred_element_type=f32)


def mm_full(a, b, dims=((1,), (0,))):
    return lax.dot_general(
        a, b, (dims, ((), ())), precision=highest, preferred_element_type=f32
    )


def twice(v):
    return jnp.concatenate([v, v], axis=1)


def lanes(start, size):
    return pl.ds(pl.multiple_of(start, size), size)


NT, TN = ((1,), (1,)), ((0,), (0,))


def whole_kernel(
    tok_ref,
    cot_ref,
    gain_ref,
    beta_ref,
    win_ref,
    bin_ref,
    sw_ref,
    sb_ref,
    w1_ref,
    b1_ref,
    w2_ref,
    b2_ref,
    w3_ref,
    decay_ref,
    fb_ref,
    wout_ref,
    bout_ref,
    pos_ref,
    f_ref,
    ft_ref,
    out_ref,
    gtok_ref,
    gwin_ref,
    gwout_ref,
    oa_ref,
    ob_ref,
    oc_ref,
    w_in,
    w_out,
    fm,
    ft,
    halo,
    white,
    istd,
    normed,
    mx,
    oiv,
    dpr,
    a1,
    a2,
    xs,
    yo,
    yx,
    r1s,
    r1,
    r2,
    first,
    second,
    window,
    ksp,
    xsp,
    zs,
    es,
    product,
    pts,
    dsx,
    dms,
    nt,
    pt,
    dm,
    cot,
    core_send,
    core_recv,
    core_send_o,
    core_recv_o,
    own_o,
    outv,
    gtokv,
    z_recv,
    z_recv_o,
    last_send,
    last_recv,
    sa,
    sr,
    sf,
    sb,
    sp,
    vb,
    sg,
    sc,
    sq,
    sh,
    load_sem,
    in_sem,
    v_sem,
    halo_sem,
    a_sem,
    b_sem,
    c_sem,
    zed_sem,
    l_sem,
):
    s, b = lax.axis_index("seq"), lax.axis_index("batch")
    zed, core = s // 2, s % 2
    side, quarter = s // 4, s % 4
    pair, cross = zed // 2 * 2 + 1 - zed % 2, (zed + 2) % 4
    pair_cross = (pair + 2) % 4
    other = (zed * 2 + 1 - core, b)

    loads = [
        pltpu.make_async_copy(src, dst, load_sem.at[i])
        for i, (src, dst) in enumerate(((wout_ref, w_out), (f_ref, fm), (ft_ref, ft)))
    ]

    def load_in(g, i):
        cols = lanes(g * 1024 + (quarter + 2 + i) % 4 * 256, 256)
        return pltpu.make_async_copy(win_ref.at[:, cols], w_in.at[:, cols], in_sem.at[g, i])

    loads[0].start()
    for i in range(4):
        for g in range(3):
            load_in(g, i).start()
    loads[1].start()
    loads[2].start()

    def batch_peer(p):
        return (s, (b + p) % 4)

    def zed_peer(p):
        return (((zed + p) % 4) * 2 + core, b)

    barrier = pltpu.get_barrier_semaphore()
    for p in range(1, 8):
        pl.semaphore_signal(
            barrier, inc=1, device_id=((s + p) % 8, b), device_id_type=MESH
        )
    for p in range(1, 4):
        pl.semaphore_signal(barrier, inc=1, device_id=batch_peer(p), device_id_type=MESH)

    def remote(src, dst, sems, index, peer, start=True):
        copy = pltpu.make_async_remote_copy(
            src_ref=src,
            dst_ref=dst,
            send_sem=sems.at[(0,) + index],
            recv_sem=sems.at[(1,) + index],
            device_id=peer,
            device_id_type=MESH,
        )
        if start:
            copy.start()
        return copy

    gain, beta = gain_ref[...], beta_ref[...]

    def white_of(x):
        x = x.astype(f32)
        centered = x - jnp.mean(x, axis=-1, keepdims=True)
        inv = lax.rsqrt(jnp.mean(centered * centered, axis=-1, keepdims=True) + epsilon)
        return centered * inv, inv

    def norm_rows(i, _):
        q, r = i // 4, (i % 4) * 32
        rows = lanes(i * 32, 32)
        w, inv = white_of(tok_ref[q, lanes(r, 32)])
        white[rows] = w
        istd[rows] = jnp.broadcast_to(inv, (32, 128))
        normed[rows] = (w * gain + beta).astype(bf16)
        return 0

    lax.fori_loop(0, 8, norm_rows, 0)

    pl.semaphore_wait(barrier, 10)
    edge = remote(
        tok_ref.at[:, 112:128],
        halo,
        halo_sem,
        (0,),
        ((s + 1) % 8, b),
        start=False,
    )

    @pl.when(s < 7)
    def _():
        edge.start()

    nt[b] = normed[0:256].T.reshape(4, 2, 128, 256)
    moves = {}
    shards = (pair_cross, pair, cross, zed)
    x, y = b % 2, b // 2
    beside = (y * 2 + 1 - x, (1 - y) * 2 + x)
    for k in range(2):
        moves["n", k] = remote(nt.at[b], nt.at[b], b_sem, (0, k), (s, beside[k]))
    for k in range(2):
        moves["c", k] = remote(cot_ref, cot.at[b], b_sem, (1, k), (s, beside[k]))

    loads[0].wait()
    cot_here = cot_ref[...]
    cot[b] = cot_here

    def backproject(t, _):
        m = mm(cot_here, w_out[lanes(t * 256, 256)], NT).astype(bf16)
        for h in range(2):
            at = slice(h * 128, h * 128 + 128)
            dpr[2 * t + h] = jnp.concatenate([m[0:128, at], m[128:256, at]], axis=1)
        return 0

    lax.fori_loop(0, 4, backproject, 0)
    sa[...] = jnp.zeros(sa.shape, f32)
    sa[5:6, 2048:3072] = jnp.sum(cot_here.astype(f32), axis=0, keepdims=True)

    @pl.when(s == 0)
    def _():
        halo[...] = jnp.zeros_like(halo)

    @pl.when(s > 0)
    def _():
        edge.wait_recv()

    w, _inv = white_of(halo[...].reshape(32, 1024))
    normed[256:288] = (w * gain + beta).astype(bf16)

    def exchange(kind, p):
        to = (quarter + p) % 4
        target = side * 4 + to
        if kind == 0:
            src, dst = a1.at[to], xs.at[quarter]
        elif kind == 1:
            src, dst, target = a1.at[to], yx.at[quarter], (1 - side) * 4 + to
        elif kind == 2:
            src, dst = a2.at[to], yo.at[quarter]
        else:
            u = (kind - 3) % 2
            send, recv = ((r1s, r1), (a2, r2))[(kind - 3) // 2]
            src, dst = send.at[to, u], recv.at[2 * quarter + u]
        return remote(src, dst, a_sem, (kind, p), (target, b), start=False)

    def send_to(kind, to):
        p = (to - quarter + 4) % 4

        @pl.when(p != 0)
        def _():
            exchange(kind, p).start()

        @pl.when(p == 0)
        def _():
            if kind == 0:
                xs[quarter] = a1[quarter]
            elif kind == 2:
                yo[quarter] = a2[quarter]
            else:
                u = (kind - 3) % 2
                send, recv = ((r1s, r1), (a2, r2))[(kind - 3) // 2]
                recv[2 * quarter + u] = send[quarter, u]

    def sent_tiles(kind):
        for p in range(0 if kind == 1 else 1, 4):
            exchange(kind, p).wait_send()

    def wait_tiles(kind):
        for p in range(0 if kind == 1 else 1, 4):
            exchange(kind, p).wait_recv()


    def project(i, _):
        t = (quarter + 2 + i) % 4
        for g in range(3):
            load_in(g, i).wait()
            cols = lanes(g * 1024 + t * 256, 256)
            m = mm(normed[...], w_in[:, cols]) + bin_ref[:, cols]
            for h in range(2):
                at = slice(h * 128, h * 128 + 128)
                tile = 2 * t + h
                edge_rows = jnp.concatenate([m[264:272, at], m[280:288, at]], axis=1)
                mx[g, tile, 0:8] = jnp.where(s > 0, edge_rows, 0.0)
                mx[g, tile, 8:136] = jnp.concatenate([m[0:128, at], m[128:256, at]], axis=1)
        for h in range(2):
            tile = 2 * t + h
            got = []
            for g in range(3):
                cols = lanes(g * 1024 + tile * 128, 128)
                taps = sw_ref[:, cols]
                value = (
                    twice(taps[0:1]) * mx[g, tile, 8:136]
                    + twice(taps[1:2]) * mx[g, tile, 7:135]
                    + twice(taps[2:3]) * mx[g, tile, 6:134]
                    + twice(sb_ref[:, cols])
                )
                oiv[g, tile] = value
                got.append(value)
            gated = got[2] * got[1]
            d_summed = dpr[tile].astype(f32) * got[0]
            a1[t, h] = jnp.where(side == 0, gated, d_summed).astype(bf16)
            a2[t, h] = jnp.where(side == 0, d_summed, gated).astype(bf16)
        exchange(1, (t - quarter + 4) % 4).start()
        send_to(0, t)
        return 0

    lax.fori_loop(0, 4, project, 0)

    mine = lanes(quarter * 256, 256)
    pos = pos_ref[...]
    one, one_c = sin_cos(mm_full(pos, w1_ref[...]) + b1_ref[...])
    first[...] = jnp.concatenate([one, one_c], axis=1)
    two, two_c = sin_cos(mm_full(one, w2_ref[...]) + b2_ref[...])
    second[...] = jnp.concatenate([two, two_c], axis=1)
    fraction = lax.broadcasted_iota(jnp.int32, (1024, 256), 0).astype(f32) * (1.0 / 1024)
    wind = jnp.exp(-fraction * decay_ref[:, mine])
    window[...] = wind
    taps_bf = (mm_full(two, w3_ref[:, mine]) * wind).astype(bf16)
    loads[1].wait()

    def filter_rows(i, _):
        rows = lanes(i * 256, 256)
        ksp[rows] = mm(fm[rows], taps_bf)
        return 0

    lax.fori_loop(0, 8, filter_rows, 0)

    turn = jnp.where(side == 0, 1.0, -1.0)
    bias = fb_ref[:, mine]
    here = side * 512
    near, far_half = lanes(here, 512), lanes(512 - here, 512)
    wait_tiles(0)
    for p in range(4):
        send_to(2, (quarter + p + 2) % 4)

    def inverse_to(kind, u, send, given):
        for k in range(2):
            y = mm(ft[lanes(here + k * 256, 256)], zs[...]) * (1.0 / 1024)
            for h in range(2):
                block = 2 * k + h
                scale = twice(bias[:, u * 128 : u * 128 + 128])
                value = y[h * 128 : h * 128 + 128] + scale * given[block, u].astype(f32)
                send[block, u] = value.astype(bf16)
        for k in range(4):
            send_to(kind + u, (quarter + 2 + k) % 4)

    for u in range(2):
        at = slice(u * 128, u * 128 + 128)
        x_u = xs[:, u].reshape(512, 256)

        def first_rows(i, _):
            lo, hi = lanes(i * 256, 256), lanes(1024 + i * 256, 256)
            xc, x_s = mm(fm[lo, near], x_u), mm(fm[hi, near], x_u)
            kc, ks = twice(ksp[lo, at]), twice(ksp[hi, at] * turn)
            xsp[u, lo] = xc.astype(bf16)
            xsp[u, hi] = x_s.astype(bf16)
            zs[lo] = (kc * xc - ks * x_s).astype(bf16)
            zs[hi] = (kc * x_s + ks * xc).astype(bf16)
            return 0

        lax.fori_loop(0, 4, first_rows, 0)
        if u == 0:
            loads[2].wait()
        inverse_to(3, u, r1s, xs)

    for k in range(2):
        by, on = beside[k], (s, beside[1 - k])
        moves["n", k].wait()
        part = nt.at[by, 2 * k : 2 * k + 2]
        moves["n", 2 + k] = remote(part, part, b_sem, (0, 2 + k), on)
    for k in range(2):
        by, on = beside[k], (s, beside[1 - k])
        moves["c", k].wait()
        part = cot.at[by, 128 * k : 128 * k + 128]
        moves["c", 2 + k] = remote(part, part, b_sem, (1, 2 + k), on)

    wait_tiles(2)
    wait_tiles(1)
    sent_tiles(2)
    for u in range(2):
        at = slice(u * 128, u * 128 + 128)
        y_near = yo[:, u].reshape(512, 256)
        y_far = yx[:, u].reshape(512, 256)

        def second_rows(i, _):
            lo, hi = lanes(i * 256, 256), lanes(1024 + i * 256, 256)
            nc, n_s = mm(fm[lo, near], y_near), mm(fm[hi, near], y_near)
            yc = nc + mm(fm[lo, far_half], y_far)
            y_s = n_s + mm(fm[hi, far_half], y_far)
            kc, ks = twice(ksp[lo, at]), twice(ksp[hi, at] * turn)
            zs[lo] = (kc * yc + ks * y_s).astype(bf16)
            zs[hi] = (kc * y_s - ks * yc).astype(bf16)
            pc = jnp.where(side == 0, nc, yc)
            p_s = jnp.where(side == 0, n_s, y_s)
            xc, x_s = xsp[u, lo].astype(f32), xsp[u, hi].astype(f32)
            ec, e_s = xc * pc + x_s * p_s, (xc * p_s - x_s * pc) * turn
            es[lo, at] = (ec[:, :128] + ec[:, 128:]).astype(bf16)
            es[hi, at] = (e_s[:, :128] + e_s[:, 128:]).astype(bf16)
            return 0

        lax.fori_loop(0, 4, second_rows, 0)
        inverse_to(5, u, a2, yo)

    def product_moves(half, p):
        return remote(
            pts.at[:, half, (b + p) % 4],
            pt.at[b, half],
            b_sem,
            (2 + half, p),
            batch_peer(p),
            start=False,
        )

    def mixed_moves(g, p):
        return remote(
            dms.at[g, (b + p) % 4], dm.at[g, b], b_sem, (4 + g, p), batch_peer(p), start=False
        )

    def edges_of(groups, index):
        return remote(
            dsx.at[groups, :, 0:8],
            dsx.at[groups, :, 128:136],
            halo_sem,
            (index,),
            ((s + 7) % 8, b),
            start=False,
        )

    def send_edges(groups, index):
        @pl.when(s > 0)
        def _():
            edges_of(groups, index).start()

    def wait_edges(groups, index):
        @pl.when(s == 7)
        def _():
            for g in range(groups.start, groups.stop):
                for j in range(8):
                    dsx[g, j, 128:136] = jnp.zeros((8, 256), f32)

        @pl.when(s < 7)
        def _():
            edges_of(groups, index).wait_recv()

    def column_sum(v):
        v = jnp.sum(v, axis=0, keepdims=True)
        return v[:, :128] + v[:, 128:]

    def short_sums(groups):
        def one_tile(j, _):
            for g in groups:
                wide = lanes(g * 1024 + j * 128, 128)
                value = dsx[g, j, 0:128]
                for k in range(3):
                    sa[1 + k : 2 + k, wide] = column_sum(value * mx[g, j, 8 - k : 136 - k])
                sa[4:5, wide] = column_sum(value)
            return 0

        lax.fori_loop(0, 8, one_tile, 0)

    def mixed_tile(g):
        def one_tile(j, _):
            q, cols = j // 2, lanes((j % 2) * 128, 128)
            wide = lanes(g * 1024 + j * 128, 128)
            taps = sw_ref[:, wide]
            value = (
                twice(taps[0:1]) * dsx[g, j, 0:128]
                + twice(taps[1:2]) * dsx[g, j, 1:129]
                + twice(taps[2:3]) * dsx[g, j, 2:130]
            ).astype(bf16)
            dms[g, q, 0:128, cols] = value[:, :128]
            dms[g, q, 128:256, cols] = value[:, 128:]
            sa[0:1, wide] = column_sum(value.astype(f32))
            return 0

        lax.fori_loop(0, 8, one_tile, 0)
        dm[g, b] = dms[g, b]

    def send_mixed(g):
        for p in (1, 2, 3):
            mixed_moves(g, p).start()

    def send_product():
        for half in range(2):
            for p in (1, 2, 3):
                product_moves(half, p).start()

    store_out = pltpu.make_async_copy(outv, out_ref, load_sem.at[3])

    def with_summed(back, early):
        def product_tile(j, _):
            value = back[j].astype(f32)
            made = (value * oiv[0, j]).astype(bf16)
            cols = lanes(j * 128, 128)
            product[0:128, cols] = made[:, :128]
            product[128:256, cols] = made[:, 128:]
            dsx[0, j, 0:128] = dpr[j].astype(f32) * value
            return 0

        lax.fori_loop(0, 8, product_tile, 0)
        send_edges(slice(0, 1), 1)
        pts[...] = product[...].T.reshape(4, 2, 4, 32, 256)
        send_product()
        for half in range(2):
            pt[b, half] = pts[:, half, b]
        short_sums((0,))

        @pl.when(s != 3)
        def _():
            wait_edges(slice(0, 1), 1)
            mixed_tile(0)
            if early:
                send_mixed(0)

        def out_cols(i, _):
            cols = lanes(i * 256, 256)
            r = mm(product[...], w_out[:, cols]) + bout_ref[:, cols]
            for q in range(2):
                rows = slice(q * 128, q * 128 + 128)
                outv[q, :, cols] = (tok_ref[q, :, cols].astype(f32) + r[rows]).astype(bf16)
            return 0

        lax.fori_loop(0, 4, out_cols, 0)
        store_out.start()

    def with_gated(back, early):
        def gate_tile(j, _):
            value = back[j].astype(f32)
            dsx[1, j, 0:128] = value * oiv[2, j]
            dsx[2, j, 0:128] = value * oiv[1, j]
            return 0

        lax.fori_loop(0, 8, gate_tile, 0)
        send_edges(slice(1, 3), 2)
        short_sums((1, 2))
        wait_edges(slice(1, 3), 2)
        mixed_tile(1)
        send_mixed(1)
        mixed_tile(2)
        if early:
            send_mixed(2)

        @pl.when(s == 3)
        def _():
            wait_edges(slice(0, 1), 1)
            mixed_tile(0)
            send_mixed(0)

    wait_tiles(3)
    wait_tiles(4)

    @pl.when(side == 0)
    def _():
        with_summed(r1, True)

    @pl.when(side == 1)
    def _():
        with_gated(r1, True)

    wait_tiles(5)
    wait_tiles(6)

    @pl.when(side == 0)
    def _():
        with_gated(r2, False)

    @pl.when(side == 1)
    def _():
        with_summed(r2, False)

    def normed_cols(i, _):
        at = lanes(i * 256, 256)
        total = jnp.zeros((256, 256), f32)
        for g in range(3):
            for q in range(4):
                c = g * 1024 + q * 256
                total += mm(dms[g, q], w_in[at, c : c + 256], NT)
        for q in range(2):
            gtokv[q, :, at] = total[q * 128 : q * 128 + 128]
        return 0

    lax.fori_loop(0, 4, normed_cols, 0)

    def token_rows(i, sums):
        q, r = i // 4, lanes((i % 4) * 32, 32)
        rows = lanes(i * 32, 32)
        d, w = gtokv[q, r], white[rows]
        dw = d * w
        d_white = d * gain
        grad = cot_ref[rows].astype(f32) + istd[rows, 0:1] * (
            d_white
            - jnp.mean(d_white, axis=-1, keepdims=True)
            - w * jnp.mean(d_white * w, axis=-1, keepdims=True)
        )
        gtokv[q, r] = grad
        return (
            sums[0] + jnp.sum(dw, axis=0, keepdims=True),
            sums[1] + jnp.sum(d, axis=0, keepdims=True),
        )

    zero = jnp.zeros((1, 1024), f32)
    sums = lax.fori_loop(0, 8, token_rows, (zero, zero))
    store_tok = pltpu.make_async_copy(gtokv, gtok_ref, load_sem.at[4])
    store_tok.start()
    sa[5:6, 0:1024] = sums[0]
    sa[5:6, 1024:2048] = sums[1]

    def part_out(half):
        total = jnp.zeros((128, 1024), f32)
        for i in range(4):
            total += mm(pt[i, half].reshape(128, 256), cot[i])
        return total

    def part_in(g, half):
        total = jnp.zeros((512, 256), f32)
        for i in range(4):
            total += mm(nt[i, :, half].reshape(512, 256), dm[g, i])
        return total

    def shard_of(g, z):
        return lanes(g * 512 + z * 128, 128)

    beside_z, across_z = (pair * 2 + core, b), (cross * 2 + core, b)

    def core_move(g):
        return remote(core_send.at[g], core_recv.at[g], c_sem, (g, 0), other, start=False)

    def zed_move(g, k):
        to = across_z if k == 2 else beside_z
        src = core_send.at[g, shards[k]]
        return remote(src, z_recv.at[g, k], zed_sem, (g, k), to, start=False)

    def core_move_o():
        return remote(core_send_o, core_recv_o, c_sem, (3, 0), other, start=False)

    def zed_move_o(k):
        to = across_z if k == 2 else beside_z
        src = core_send_o.at[32 * k : 32 * k + 32]
        return remote(src, z_recv_o.at[k], zed_sem, (3, k), to, start=False)

    def core_half_o():
        core_send_o[...] = part_out(1 - core).astype(bf16)
        core_move_o().start()

    def core_half(g):
        core_send[g] = part_in(g, 1 - core).astype(bf16).reshape(4, 128, 256)
        core_move(g).start()

    def zed_half_o():
        total = part_out(core)
        core_move_o().wait()
        own_o[...] = (total + core_recv_o[...].astype(f32)).reshape(4, 32, 1024)
        for k in range(2):
            core_send_o[32 * k : 32 * k + 32] = own_o[shards[k]].astype(bf16)
            zed_move_o(k).start()

    def zed_half(g):
        total = part_in(g, core)
        core_move(g).wait()
        ksp[512 * g : 512 * g + 512] = total + core_recv[g].astype(f32).reshape(512, 256)
        for k in range(2):
            core_send[g, shards[k]] = ksp[shard_of(g, shards[k])].astype(bf16)
            zed_move(g, k).start()

    def cross_half_o():
        zed_move_o(0).wait()
        core_send_o[64:96] = (own_o[cross] + z_recv_o[0].astype(f32)).astype(bf16)
        zed_move_o(2).start()

    def cross_half(g):
        zed_move(g, 0).wait()
        total = ksp[shard_of(g, cross)] + z_recv[g, 0].astype(f32)
        core_send[g, cross] = total.astype(bf16)
        zed_move(g, 2).start()

    def last_half(g):
        zed_move(g, 1).wait()
        zed_move(g, 2).wait()
        total = ksp[shard_of(g, zed)] + z_recv[g, 1].astype(f32) + z_recv[g, 2].astype(f32)
        last_send[g] = total.astype(bf16).reshape(4, 32, 256)
        for p in (1, 2, 3):
            moves["l", g, p] = remote(
                last_send.at[g, (b + p) % 4], last_recv.at[g, b], l_sem, (g, p), batch_peer(p)
            )
        last_recv[g, b] = last_send[g, b]

    def half_at(k):
        return lanes(k * 1536, 1536)

    def kernel_rows(i, _):
        rows = lanes(i * 256, 256)
        window[rows] = mm(ft[rows], es[...]) * (1.0 / 1024) * window[rows]
        return 0

    lax.fori_loop(0, 4, kernel_rows, 0)
    sb[...] = jnp.zeros(sb.shape, f32)
    sc[...] = jnp.zeros(sc.shape, f32)
    for u in range(2):
        both = xs[:, u].astype(f32) * yo[:, u].astype(f32)
        both = jnp.sum(both.reshape(512, 256), axis=0, keepdims=True)
        sb[64:65, u * 128 : u * 128 + 128] = both[:, :128] + both[:, 128:]
    def low(v):
        return v.astype(bf16)

    d_shaped = low(window[...])
    sb[0:64] = mm(low(second[:, 0:64]), d_shaped, TN)
    d_two = mm(d_shaped, low(w3_ref[:, mine]), NT) * second[:, 64:128]
    sc[0:64, 64:128] = mm(low(first[:, 0:64]), low(d_two), TN)
    sc[40:41, 0:64] = jnp.sum(d_two, axis=0, keepdims=True)
    d_one = mm(low(d_two), low(w2_ref[...]), NT) * first[:, 64:128]
    sc[0:33, 0:64] = mm(low(pos_ref[...]), low(d_one), TN)
    sc[41:42, 0:64] = jnp.sum(d_one, axis=0, keepdims=True)
    def rows_at(k):
        return pl.ds(pl.multiple_of(k * 32, 32), 32)

    def small_remote(src, dst, index, peer):
        return remote(src, dst, v_sem, (index,), peer)

    smalls = [
        small_remote(sa.at[:, half_at(1 - core)], sr.at[0], 0, other),
        small_remote(sc.at[rows_at(1 - core)], sq.at[8], 1, other),
    ]
    for k in (2, 3):
        moves["n", k].wait()
        moves["c", k].wait()

    def arrived(g):
        for p in (1, 2, 3):
            mixed_moves(g, p).wait()

    def arrived_o():
        for p in (1, 2, 3):
            product_moves(0, p).wait()
            product_moves(1, p).wait()

    @pl.when(side == 0)
    def _():
        arrived_o()
        send_mixed(2)
        core_half_o()
        arrived(0)
        core_half(0)
        zed_half_o()
        zed_half(0)

    @pl.when(side == 1)
    def _():
        arrived(1)
        send_mixed(0)
        core_half(1)
        arrived(2)
        core_half(2)
        zed_half(1)
        zed_half(2)

    for move in smalls:
        move.wait()
    def fold(v):
        return jnp.concatenate([v[:, :768], v[:, 768:]], axis=0).astype(bf16)

    def total_of(array, first):
        return sum(array[first + i].astype(f32) for i in range(1, 4)) + array[first].astype(f32)

    vb[b] = fold(sa[:, half_at(core)] + sr[0])
    sq[b] = sc[rows_at(core)] + sq[8]
    sp[b] = sb[...].astype(bf16)
    smalls = []
    for p in (1, 2, 3):
        smalls += [
            small_remote(vb.at[b], vb.at[b], 1 + p, batch_peer(p)),
            small_remote(sq.at[b], sq.at[b], 4 + p, batch_peer(p)),
            small_remote(sp.at[b], sp.at[b], 7 + p, batch_peer(p)),
        ]

    @pl.when(side == 0)
    def _():
        arrived(1)
        core_half(1)
        cross_half_o()
        cross_half(0)
        zed_half(1)

    @pl.when(side == 1)
    def _():
        arrived_o()
        core_half_o()
        cross_half(1)
        cross_half(2)
        zed_half_o()

    for move in smalls:
        move.wait()
    vb[4 + zed] = total_of(vb, 0).astype(bf16)
    sq[4 + zed] = total_of(sq, 0)
    sb[...] = total_of(sp, 0)
    sp[4] = sb[...].astype(bf16)
    smalls = [small_remote(sp.at[4], sp.at[5], 17, across_z)]
    for p in (1, 2, 3):
        smalls += [
            small_remote(vb.at[4 + zed], vb.at[4 + zed], 10 + p, zed_peer(p)),
            small_remote(sq.at[4 + zed], sq.at[4 + zed], 13 + p, zed_peer(p)),
        ]
    @pl.when(side == 0)
    def _():
        arrived(2)
        core_half(2)
        cross_half(1)
        zed_half(2)
        cross_half(2)

    @pl.when(side == 1)
    def _():
        arrived(0)
        core_half(0)
        cross_half_o()
        zed_half(0)
        cross_half(0)

    for move in smalls:
        move.wait()
    sb[...] = sb[...] + sp[5].astype(f32)
    folded = total_of(vb, 4)
    sf[...] = jnp.concatenate([folded[:8], folded[8:]], axis=1)
    sh[...] = total_of(sq, 4)
    smalls = [
        small_remote(sf, sr.at[1], 18, other),
        small_remote(sh, sq.at[9], 19, other),
    ]
    owner = quarter * 2 + side

    def give():
        return remote(
            sb.at[:, lanes(side * 128, 128)], sg, v_sem, (20,), (owner, b), start=False
        )

    @pl.when(owner != s)
    def _():
        give().start()

    @pl.when(owner == s)
    def _():
        sg[...] = sb[:, lanes(side * 128, 128)]

    last_half(0)
    zed_move_o(1).wait()
    zed_move_o(2).wait()
    gwout_ref[...] = own_o[zed] + z_recv_o[1].astype(f32) + z_recv_o[2].astype(f32)
    last_half(1)
    last_half(2)
    for move in smalls:
        move.wait()
    oa_ref[:, half_at(core)] = sf[...]
    oa_ref[:, half_at(1 - core)] = sr[1]
    oc_ref[rows_at(core)] = sh[...]
    oc_ref[rows_at(1 - core)] = sq[9]

    @pl.when(owner != s)
    def _():
        give().wait()

    ob_ref[...] = sg[...]
    for g in range(3):
        for p in (1, 2, 3):
            moves["l", g, p].wait()
        for i in range(4):
            c = g * 1024 + i * 256
            gwin_ref[:, c : c + 256] = last_recv[g, i].astype(f32)
    store_out.wait()
    store_tok.wait()
    for kind in (0, 1, 3, 4, 5, 6):
        sent_tiles(kind)

    @pl.when(s < 7)
    def _():
        edge.wait_send()

    @pl.when(s > 0)
    def _():
        edges_of(slice(0, 1), 1).wait_send()
        edges_of(slice(1, 3), 2).wait_send()


def whole(args, positions, matrix):
    vmem, anywhere = (pl.BlockSpec(memory_space=m) for m in (pltpu.VMEM, pl.ANY))
    dma = pltpu.SemaphoreType.DMA
    specs = [vmem] * 20
    for i in (4, 15, 18, 19):
        specs[i] = anywhere
    shape = jax.ShapeDtypeStruct

    def v(dtype, *dims):
        return pltpu.VMEM(dims, dtype)

    return pl.pallas_call(
        whole_kernel,
        out_shape=(
            shape((2, 128, 1024), bf16),
            shape((2, 128, 1024), f32),
            shape((32, 3072), f32),
            shape((32, 1024), f32),
            shape((8, 3072), f32),
            shape((80, 128), f32),
            shape((64, 128), f32),
        ),
        in_specs=specs,
        out_specs=(anywhere,) * 2 + (vmem,) * 5,
        scratch_shapes=[
            v(bf16, 1024, 3072),
            v(bf16, 1024, 1024),
            v(bf16, 2048, 1024),
            v(bf16, 1024, 2048),
            v(bf16, 2, 16, 1024),
            v(f32, 256, 1024),
            v(f32, 256, 128),
            v(bf16, 288, 1024),
            v(f32, 3, 8, 136, 256),
            v(f32, 3, 8, 128, 256),
            v(bf16, 8, 128, 256),
            v(bf16, 4, 2, 128, 256),
            v(bf16, 4, 2, 128, 256),
            v(bf16, 4, 2, 128, 256),
            v(bf16, 4, 2, 128, 256),
            v(bf16, 4, 2, 128, 256),
            v(bf16, 4, 2, 128, 256),
            v(bf16, 8, 128, 256),
            v(bf16, 8, 128, 256),
            v(f32, 1024, 128),
            v(f32, 1024, 128),
            v(f32, 1024, 256),
            v(f32, 2048, 256),
            v(bf16, 2, 2048, 256),
            v(bf16, 2048, 256),
            v(bf16, 2048, 256),
            v(bf16, 256, 1024),
            v(bf16, 4, 2, 4, 32, 256),
            v(f32, 3, 8, 136, 256),
            v(bf16, 3, 4, 256, 256),
            v(bf16, 4, 4, 2, 128, 256),
            v(bf16, 4, 2, 4, 32, 256),
            v(bf16, 3, 4, 256, 256),
            v(bf16, 4, 256, 1024),
            v(bf16, 3, 4, 128, 256),
            v(bf16, 3, 4, 128, 256),
            v(bf16, 128, 1024),
            v(bf16, 128, 1024),
            v(f32, 4, 32, 1024),
            v(bf16, 2, 128, 1024),
            v(f32, 2, 128, 1024),
            v(bf16, 3, 3, 128, 256),
            v(bf16, 3, 32, 1024),
            v(bf16, 3, 4, 32, 256),
            v(bf16, 3, 4, 32, 256),
            v(f32, 8, 3072),
            v(f32, 2, 8, 1536),
            v(f32, 8, 1536),
            v(f32, 80, 256),
            v(bf16, 6, 80, 256),
            v(bf16, 8, 16, 768),
            v(f32, 80, 128),
            v(f32, 64, 128),
            v(f32, 10, 32, 128),
            v(f32, 32, 128),
            dma((5,)),
            dma((3, 4)),
            dma((2, 21)),
            dma((2, 3)),
            dma((2, 7, 4)),
            dma((2, 7, 4)),
            dma((2, 4, 4)),
            dma((2, 4, 4)),
            dma((2, 3, 4)),
        ],
        compiler_params=pltpu.CompilerParams(
            collective_id=0, has_side_effects=True, vmem_limit_bytes=63 * 1024 * 1024
        ),
    )(*args, positions, matrix, np.ascontiguousarray(matrix.T))


def settle_kernel(
    out_ref,
    gtok_ref,
    gwin_ref,
    gwout_ref,
    sa_ref,
    sb_ref,
    sc_ref,
    out,
    gtok,
    ln_gain,
    ln_bias,
    gwin,
    b_in,
    short_w,
    short_b,
    w_one,
    b_one,
    w_two,
    b_two,
    w_three,
    filt,
    gwout,
    b_out,
    sems,
):
    copies = [
        pltpu.make_async_copy(src, dst, sems.at[i])
        for i, (src, dst) in enumerate(
            ((out_ref, out), (gtok_ref, gtok), (gwin_ref, gwin), (gwout_ref, gwout))
        )
    ]
    for copy in copies:
        copy.start()
    b = lax.axis_index("batch")
    place = lax.axis_index("seq") * 4 + b
    sa = sa_ref[...]
    wide = pltpu.roll(sa, (32 - place) * 96, 1)
    b_in[...] = wide[0:1, :96]
    short_w[...] = wide[1:4, :96]
    short_b[...] = wide[4:5, :96]
    thin = pltpu.roll(sa, (96 - place) * 32, 1)
    ln_gain[...] = thin[5:6, 0:32]
    ln_bias[...] = thin[5:6, 1024:1056]
    b_out[...] = thin[5:6, 2048:2080]
    third = pltpu.roll(sb_ref[...], (4 - b) * 32, 1)
    w_three[...] = third.T[0:32, 0:64]
    filt[...] = third[64:65, 0:32]
    w_one[...] = sc_ref[0:33, 0:64]
    w_two[...] = sc_ref[0:64, 64:128]
    b_two[...] = sc_ref[40:41, 0:64]
    b_one[...] = sc_ref[41:42, 0:64]
    for copy in copies:
        copy.wait()


def settle(parts):
    vmem, anywhere = (pl.BlockSpec(memory_space=m) for m in (pltpu.VMEM, pl.ANY))
    sizes = (
        (2, 128, 1024),
        (2, 128, 1024),
        (1, 32),
        (1, 32),
        (32, 3072),
        (1, 96),
        (3, 96),
        (1, 96),
        (33, 64),
        (1, 64),
        (64, 64),
        (1, 64),
        (32, 64),
        (1, 32),
        (32, 1024),
        (1, 32),
    )
    flat = (2, 3, 5, 7, 9, 11, 13, 15)
    outs = pl.pallas_call(
        settle_kernel,
        out_shape=tuple(
            jax.ShapeDtypeStruct(size, f32 if i else bf16) for i, size in enumerate(sizes)
        ),
        in_specs=[anywhere] * 4 + [vmem] * 3,
        out_specs=(vmem,) * 16,
        scratch_shapes=[pltpu.SemaphoreType.DMA((4,))],
    )(*parts)
    return tuple(
        o.reshape(-1) if i in flat else o.T if i == 12 else o for i, o in enumerate(outs)
    )


def local_small(*args):
    cotangent = args[1]
    vectors = {2, 3, 5, 7, 9, 11, 13, 14, 16}
    given = [a.reshape(1, -1) if i in vectors else a for i, a in enumerate(args)]
    given[1] = cotangent.reshape(256, 1024)
    return settle(whole(given, position_features(1024, args[8].shape[0]), dft_matrix(1024)))


def solution(mesh):
    tokens_spec = P("batch", "seq", None)
    both = ("seq", "batch")
    in_specs = (tokens_spec, tokens_spec) + (P(),) * 15
    out_specs = (
        tokens_spec,
        tokens_spec,
        P(both),
        P(both),
        P(both, None),
        P(both),
        P(None, both),
        P(both),
        P(),
        P(),
        P(),
        P(),
        P(None, both),
        P(both),
        P(both, None),
        P(both),
    )

    def per_device(*args):
        tokens, w_one = args[0], args[8]
        sizes = (mesh.shape["seq"], mesh.shape["batch"]) + tokens.shape + w_one.shape
        fits = sizes == (8, 4, 2, 128, 1024, 33, 64)
        return (local_small if fits else local)(*args)

    return jax.shard_map(per_device, mesh=mesh, in_specs=in_specs, out_specs=out_specs, check_vma=False)
```

```python
import jax
import jax.numpy as jnp
import numpy as np
from jax import lax
from jax.experimental import pallas as pl
from jax.experimental.pallas import tpu as pltpu
from jax.sharding import PartitionSpec as P

highest = lax.Precision.HIGHEST
epsilon = 1e-05
f32, bf16 = jnp.float32, jnp.bfloat16


def dft_matrix(length):
    turns = ((2 * np.arange(length)[:, None] + 1) * np.arange(length)[None, :]) % (4 * length)
    phases = turns * (np.pi / (2 * length))
    return np.concatenate([np.cos(phases), np.sin(phases)], axis=0).astype(bf16)


def position_features(length, features):
    step_axis = np.arange(length, dtype=np.float64)
    band_count = (features - 1) // 2
    band_rates = 0.0001 + np.arange(band_count) * (band_count - 1 - 0.0001) / (band_count - 1)
    phases = 2.0 * np.pi / length * step_axis[:, None] * band_rates[None, :]
    return np.concatenate(
        [(step_axis / length)[:, None], np.cos(phases), -np.sin(phases)], axis=1
    ).astype(np.float32)


def filter_shape(positions, w_one, b_one, w_two, b_two, w_three, decay_rates):
    first_layer = jnp.sin(jnp.dot(positions, w_one, precision=highest) + b_one)
    second_layer = jnp.sin(jnp.dot(first_layer, w_two, precision=highest) + b_two)
    shaped = jnp.dot(second_layer, w_three, precision=highest)
    length = positions.shape[0]
    fraction = jnp.arange(length).astype(f32) / length
    return shaped * jnp.exp(-fraction[:, None] * decay_rates[None, :])


def shifted(value, axis, steps):
    count = lax.axis_size(axis)
    first, last = (max(0, -steps), min(count, count - steps))
    return lax.ppermute(value, axis, [(source, source + steps) for source in range(first, last)])


def reduce_scatter(value, dtype):
    out = lax.all_to_all(value.astype(dtype), "batch", split_axis=1, concat_axis=1, tiled=True)
    out = jnp.sum(out.astype(f32), axis=1)
    out = lax.all_to_all(out.astype(dtype), "seq", split_axis=0, concat_axis=0, tiled=True)
    return jnp.sum(out.astype(f32), axis=0)


def local(
    tokens,
    cotangent,
    ln_gain,
    ln_bias,
    w_in,
    b_in,
    short_w,
    short_b,
    w_one,
    b_one,
    w_two,
    b_two,
    w_three,
    decay_rates,
    filt_bias,
    w_out,
    b_out,
):
    seq_count, block_len, model_width = tokens.shape
    seq_devices = lax.axis_size("seq")
    batch_devices = lax.axis_size("batch")
    devices = seq_devices * batch_devices
    length = block_len * seq_devices
    channels = model_width // seq_devices
    col_start = lax.axis_index("seq") * channels
    inputs = tokens.astype(f32)
    average = jnp.mean(inputs, axis=-1, keepdims=True)
    centered = inputs - average
    inv_std = lax.rsqrt(jnp.mean(centered * centered, axis=-1, keepdims=True) + epsilon)
    whitened = centered * inv_std
    normed = (whitened * ln_gain + ln_bias).astype(bf16)
    mixed = jnp.einsum("btd,de->bte", normed, w_in, preferred_element_type=f32) + b_in
    prev_rows = shifted(mixed[:, block_len - 2 :], "seq", 1)
    padded = jnp.concatenate([prev_rows, mixed], axis=1)
    delay_one = padded[:, 1:-1]
    delay_two = padded[:, :-2]
    short_out = short_w[0] * mixed + short_w[1] * delay_one + short_w[2] * delay_two + short_b
    outer_gate = short_out[..., :model_width]
    inner_gate = short_out[..., model_width : 2 * model_width]
    values = short_out[..., 2 * model_width :]
    gated = (values * inner_gate).astype(bf16)
    d_product = jnp.einsum(
        "bte,de->btd", cotangent, w_out, preferred_element_type=f32
    ).astype(bf16)
    d_prod_f = d_product.astype(f32)
    d_summed = (d_prod_f * outer_gate).astype(bf16)

    def to_channels(value):
        return lax.all_to_all(value, "seq", split_axis=2, concat_axis=1, tiled=True)

    def to_tokens(value):
        return lax.all_to_all(value, "seq", split_axis=1, concat_axis=2, tiled=True)

    gated_ch = to_channels(gated)
    d_ch = to_channels(d_summed)
    positions = jnp.asarray(position_features(length, w_one.shape[0]))
    w_three_part = lax.dynamic_slice_in_dim(w_three, col_start, channels, 1)
    decay_part = lax.dynamic_slice_in_dim(decay_rates, col_start, channels, 0)
    bias_part = lax.dynamic_slice_in_dim(filt_bias, col_start, channels, 0)

    def kernel_of(first_w, first_b, second_w, second_b, third_w):
        return filter_shape(positions, first_w, first_b, second_w, second_b, third_w, decay_part)

    kernel_full, kernel_pull = jax.vjp(kernel_of, w_one, b_one, w_two, b_two, w_three_part)
    matrix = jnp.asarray(dft_matrix(length))

    def spectrum(value):
        return jnp.einsum("kt,btc->bkc", matrix, value, preferred_element_type=f32)

    def inverse(cosines, sines):
        both = jnp.concatenate([cosines, sines], axis=1).astype(bf16)
        return jnp.einsum("kt,bkc->btc", matrix, both, preferred_element_type=f32) * (1.0 / length)

    k_both = spectrum(kernel_full.astype(bf16)[None])
    g_both = spectrum(gated_ch)
    d_both = spectrum(d_ch)
    k_c, k_s = k_both[:, :length], k_both[:, length:]
    g_c, g_s = g_both[:, :length], g_both[:, length:]
    d_c, d_s = d_both[:, :length], d_both[:, length:]
    long_out = inverse(g_c * k_c - g_s * k_s, g_c * k_s + g_s * k_c)
    gated_float = gated_ch.astype(f32)
    d_ch_float = d_ch.astype(f32)
    summed_ch = (long_out + bias_part * gated_float).astype(bf16)
    summed = to_tokens(summed_ch).astype(f32)
    grad_in = inverse(k_c * d_c + k_s * d_s, k_c * d_s - k_s * d_c) + bias_part * d_ch_float
    d_gated = to_tokens(grad_in.astype(bf16)).astype(f32)
    d_kernel = inverse(
        jnp.sum(g_c * d_c + g_s * d_s, axis=0, keepdims=True),
        jnp.sum(g_c * d_s - g_s * d_c, axis=0, keepdims=True),
    )[0]
    g_bias_part = jnp.sum(d_ch_float * gated_float, axis=(0, 1))
    g_w_one, g_b_one, g_w_two, g_b_two, g_w_three_part = kernel_pull(d_kernel)

    product = (summed * outer_gate).astype(bf16)
    result = jnp.einsum("btd,de->bte", product, w_out, preferred_element_type=f32) + b_out
    block_out = (inputs + result).astype(bf16)
    grad_out = cotangent.astype(f32)
    g_w_out = jnp.einsum("btd,bte->de", product, cotangent, preferred_element_type=f32)
    g_b_out = jnp.sum(grad_out, axis=(0, 1))
    d_outer = d_prod_f * summed
    d_short = jnp.concatenate([d_outer, d_gated * values, d_gated * inner_gate], axis=-1)
    g_short_w = jnp.stack(
        [
            jnp.sum(d_short * mixed, axis=(0, 1)),
            jnp.sum(d_short * delay_one, axis=(0, 1)),
            jnp.sum(d_short * delay_two, axis=(0, 1)),
        ]
    )
    g_short_b = jnp.sum(d_short, axis=(0, 1))
    next_rows = shifted(d_short[:, :2], "seq", -1)
    extended = jnp.concatenate([d_short, next_rows], axis=1)
    d_mixed = (
        short_w[0] * extended[:, :block_len]
        + short_w[1] * extended[:, 1 : block_len + 1]
        + short_w[2] * extended[:, 2:]
    ).astype(bf16)
    g_w_in = jnp.einsum("btd,bte->de", normed, d_mixed, preferred_element_type=f32)
    g_b_in = jnp.sum(d_mixed.astype(f32), axis=(0, 1))
    d_normed = jnp.einsum("bte,de->btd", d_mixed, w_in, preferred_element_type=f32)
    g_ln_gain = jnp.sum(d_normed * whitened, axis=(0, 1))
    g_ln_bias = jnp.sum(d_normed, axis=(0, 1))
    d_white = d_normed * ln_gain
    grad_tokens = grad_out + inv_std * (
        d_white
        - jnp.mean(d_white, axis=-1, keepdims=True)
        - whitened * jnp.mean(d_white * whitened, axis=-1, keepdims=True)
    )
    rows = model_width // devices
    big = jnp.concatenate([g_w_in, g_w_out], axis=1)
    big = reduce_scatter(big.reshape(seq_devices, batch_devices, rows, -1), bf16)
    out_w_in, out_w_out = big[:, : 3 * model_width], big[:, 3 * model_width :]
    g_w_three = lax.dynamic_update_slice_in_dim(
        jnp.zeros(w_three.shape, f32), g_w_three_part, col_start, 1
    )
    g_filt_bias = lax.dynamic_update_slice_in_dim(
        jnp.zeros(filt_bias.shape, f32), g_bias_part, col_start, 0
    )
    vectors = jnp.concatenate(
        [
            g_ln_gain[None],
            g_ln_bias[None],
            g_b_out[None],
            g_filt_bias[None],
            g_w_three,
        ],
        axis=0,
    )
    vectors = jnp.transpose(vectors.reshape(-1, devices, rows), (1, 0, 2)).reshape(devices, -1)
    wides = jnp.concatenate([g_b_in[None], g_short_w, g_short_b[None]], axis=0)
    wides = jnp.transpose(wides.reshape(-1, devices, 3 * rows), (1, 0, 2)).reshape(devices, -1)
    net = jnp.concatenate([v.reshape(-1) for v in (g_w_one, g_b_one, g_w_two, g_b_two)])
    net_size = net.shape[0]
    net_part = -(-net_size // devices)
    net = jnp.pad(net, (0, net_part * devices - net_size)).reshape(devices, net_part)
    small = jnp.concatenate([vectors, wides, net], axis=1)
    small = reduce_scatter(small.reshape(seq_devices, batch_devices, -1), f32)
    hidden = w_two.shape[0]
    cut = rows * (4 + hidden)
    vectors = small[:cut].reshape(4 + hidden, rows)
    wides = small[cut : cut + 15 * rows].reshape(5, 3 * rows)
    net = lax.all_gather(small[cut + 15 * rows :], ("seq", "batch"), tiled=True)
    features = w_one.shape[0]
    edges = [features * hidden, (features + 1) * hidden, (features + 1 + hidden) * hidden]
    return (
        block_out,
        grad_tokens,
        vectors[0],
        vectors[1],
        out_w_in,
        wides[0],
        wides[1:4],
        wides[4],
        net[: edges[0]].reshape(features, hidden),
        net[edges[0] : edges[1]],
        net[edges[1] : edges[2]].reshape(hidden, hidden),
        net[edges[2] : net_size],
        vectors[4:],
        vectors[3],
        out_w_out,
        vectors[2],
    )


MESH = pl.DeviceIdType.MESH
HALF_TURN = (1.5703125, 4.837512969970703125e-4, 7.549789948768648e-8)


def sin_cos(x):
    turns = jnp.floor(x * 0.6366197723675814 + 0.5)
    r = ((x - turns * HALF_TURN[0]) - turns * HALF_TURN[1]) - turns * HALF_TURN[2]
    q = turns.astype(jnp.int32)
    r2 = r * r
    sine = r + r * r2 * (
        -1.6666654611e-1 + r2 * (8.3321608736e-3 + r2 * -1.9515295891e-4)
    )
    cosine = 1.0 - 0.5 * r2 + r2 * r2 * (
        4.166664568298827e-2 + r2 * (-1.388731625493765e-3 + r2 * 2.443315711809948e-5)
    )
    odd = (q & 1) == 1
    s_abs, c_abs = jnp.where(odd, cosine, sine), jnp.where(odd, sine, cosine)
    s_neg, c_neg = (q & 2) == 2, ((q + 1) & 2) == 2
    return jnp.where(s_neg, -s_abs, s_abs), jnp.where(c_neg, -c_abs, c_abs)


def mm(a, b, dims=((1,), (0,))):
    return lax.dot_general(a, b, (dims, ((), ())), preferred_element_type=f32)


def mm_full(a, b, dims=((1,), (0,))):
    return lax.dot_general(
        a, b, (dims, ((), ())), precision=highest, preferred_element_type=f32
    )


def twice(v):
    return jnp.concatenate([v, v], axis=1)


def lanes(start, size):
    return pl.ds(pl.multiple_of(start, size), size)


NT, TN = ((1,), (1,)), ((0,), (0,))


def whole_kernel(
    tok_ref,
    cot_ref,
    gain_ref,
    beta_ref,
    win_ref,
    bin_ref,
    sw_ref,
    sb_ref,
    w1_ref,
    b1_ref,
    w2_ref,
    b2_ref,
    w3_ref,
    decay_ref,
    fb_ref,
    wout_ref,
    bout_ref,
    pos_ref,
    f_ref,
    ft_ref,
    out_ref,
    gtok_ref,
    gwin_ref,
    gwout_ref,
    oa_ref,
    ob_ref,
    oc_ref,
    w_in,
    w_out,
    fm,
    ft,
    halo,
    white,
    istd,
    normed,
    mx,
    oiv,
    dpr,
    a1,
    a2,
    xs,
    yo,
    yx,
    r1s,
    r1,
    r2,
    first,
    second,
    window,
    ksp,
    xsp,
    zs,
    es,
    product,
    pts,
    dsx,
    dms,
    nt,
    pt,
    dm,
    cot,
    core_send,
    core_recv,
    core_send_o,
    core_recv_o,
    own_o,
    outv,
    gtokv,
    z_recv,
    z_recv_o,
    last_send,
    last_recv,
    sa,
    sr,
    sf,
    sb,
    sp,
    vb,
    sg,
    sc,
    sq,
    st,
    sh,
    load_sem,
    in_sem,
    v_sem,
    halo_sem,
    a_sem,
    b_sem,
    c_sem,
    zed_sem,
    l_sem,
):
    s, b = lax.axis_index("seq"), lax.axis_index("batch")
    zed, core = s // 2, s % 2
    side, quarter = s // 4, s % 4
    pair, cross = zed // 2 * 2 + 1 - zed % 2, (zed + 2) % 4
    pair_cross = (pair + 2) % 4
    other = (zed * 2 + 1 - core, b)

    loads = [
        pltpu.make_async_copy(src, dst, load_sem.at[i])
        for i, (src, dst) in enumerate(((wout_ref, w_out), (f_ref, fm), (ft_ref, ft)))
    ]

    def load_in(g, i):
        cols = lanes(g * 1024 + (quarter + 2 + i) % 4 * 256, 256)
        return pltpu.make_async_copy(win_ref.at[:, cols], w_in.at[:, cols], in_sem.at[g, i])

    loads[0].start()
    for i in range(4):
        for g in range(3):
            load_in(g, i).start()
    loads[1].start()
    loads[2].start()

    def batch_peer(p):
        return (s, (b + p) % 4)

    def zed_peer(p):
        return (((zed + p) % 4) * 2 + core, b)

    barrier = pltpu.get_barrier_semaphore()
    for p in range(1, 8):
        pl.semaphore_signal(
            barrier, inc=1, device_id=((s + p) % 8, b), device_id_type=MESH
        )
    for p in range(1, 4):
        pl.semaphore_signal(barrier, inc=1, device_id=batch_peer(p), device_id_type=MESH)

    def remote(src, dst, sems, index, peer, start=True):
        copy = pltpu.make_async_remote_copy(
            src_ref=src,
            dst_ref=dst,
            send_sem=sems.at[(0,) + index],
            recv_sem=sems.at[(1,) + index],
            device_id=peer,
            device_id_type=MESH,
        )
        if start:
            copy.start()
        return copy

    gain, beta = gain_ref[...], beta_ref[...]

    def white_of(x):
        x = x.astype(f32)
        centered = x - jnp.mean(x, axis=-1, keepdims=True)
        inv = lax.rsqrt(jnp.mean(centered * centered, axis=-1, keepdims=True) + epsilon)
        return centered * inv, inv

    def norm_rows(i, _):
        q, r = i // 4, (i % 4) * 32
        rows = lanes(i * 32, 32)
        w, inv = white_of(tok_ref[q, lanes(r, 32)])
        white[rows] = w
        istd[rows] = jnp.broadcast_to(inv, (32, 128))
        normed[rows] = (w * gain + beta).astype(bf16)
        return 0

    lax.fori_loop(0, 8, norm_rows, 0)

    pl.semaphore_wait(barrier, 10)
    edge = remote(
        tok_ref.at[:, 112:128],
        halo,
        halo_sem,
        (0,),
        ((s + 1) % 8, b),
        start=False,
    )

    @pl.when(s < 7)
    def _():
        edge.start()

    nt[b] = normed[0:256].T.reshape(4, 2, 128, 256)
    moves = {}
    shards = (pair_cross, pair, cross, zed)
    x, y = b % 2, b // 2
    beside = (y * 2 + 1 - x, (1 - y) * 2 + x)
    for k in range(2):
        moves["n", k] = remote(nt.at[b], nt.at[b], b_sem, (0, k), (s, beside[k]))
    for k in range(2):
        moves["c", k] = remote(cot_ref, cot.at[b], b_sem, (1, k), (s, beside[k]))

    loads[0].wait()
    cot_here = cot_ref[...]
    cot[b] = cot_here

    def backproject(t, _):
        m = mm(cot_here, w_out[lanes(t * 256, 256)], NT).astype(bf16)
        for h in range(2):
            at = slice(h * 128, h * 128 + 128)
            dpr[2 * t + h] = jnp.concatenate([m[0:128, at], m[128:256, at]], axis=1)
        return 0

    lax.fori_loop(0, 4, backproject, 0)
    sa[...] = jnp.zeros(sa.shape, f32)
    sa[5:6, 2048:3072] = jnp.sum(cot_here.astype(f32), axis=0, keepdims=True)

    @pl.when(s == 0)
    def _():
        halo[...] = jnp.zeros_like(halo)

    @pl.when(s > 0)
    def _():
        edge.wait_recv()

    w, _inv = white_of(halo[...].reshape(32, 1024))
    normed[256:288] = (w * gain + beta).astype(bf16)

    def exchange(kind, p):
        to = (quarter + p) % 4
        target = side * 4 + to
        if kind == 0:
            src, dst = a1.at[to], xs.at[quarter]
        elif kind == 1:
            src, dst, target = a1.at[to], yx.at[quarter], (1 - side) * 4 + to
        elif kind == 2:
            src, dst = a2.at[to], yo.at[quarter]
        else:
            u = (kind - 3) % 2
            send, recv = ((r1s, r1), (a2, r2))[(kind - 3) // 2]
            src, dst = send.at[to, u], recv.at[2 * quarter + u]
        return remote(src, dst, a_sem, (kind, p), (target, b), start=False)

    def send_to(kind, to):
        p = (to - quarter + 4) % 4

        @pl.when(p != 0)
        def _():
            exchange(kind, p).start()

        @pl.when(p == 0)
        def _():
            if kind == 0:
                xs[quarter] = a1[quarter]
            elif kind == 2:
                yo[quarter] = a2[quarter]
            else:
                u = (kind - 3) % 2
                send, recv = ((r1s, r1), (a2, r2))[(kind - 3) // 2]
                recv[2 * quarter + u] = send[quarter, u]

    def sent_tiles(kind):
        for p in range(0 if kind == 1 else 1, 4):
            exchange(kind, p).wait_send()

    def wait_tiles(kind):
        for p in range(0 if kind == 1 else 1, 4):
            exchange(kind, p).wait_recv()


    def project(i, _):
        t = (quarter + 2 + i) % 4
        for g in range(3):
            load_in(g, i).wait()
            cols = lanes(g * 1024 + t * 256, 256)
            m = mm(normed[...], w_in[:, cols]) + bin_ref[:, cols]
            for h in range(2):
                at = slice(h * 128, h * 128 + 128)
                tile = 2 * t + h
                edge_rows = jnp.concatenate([m[264:272, at], m[280:288, at]], axis=1)
                mx[g, tile, 0:8] = jnp.where(s > 0, edge_rows, 0.0)
                mx[g, tile, 8:136] = jnp.concatenate([m[0:128, at], m[128:256, at]], axis=1)
        for h in range(2):
            tile = 2 * t + h
            got = []
            for g in range(3):
                cols = lanes(g * 1024 + tile * 128, 128)
                taps = sw_ref[:, cols]
                value = (
                    twice(taps[0:1]) * mx[g, tile, 8:136]
                    + twice(taps[1:2]) * mx[g, tile, 7:135]
                    + twice(taps[2:3]) * mx[g, tile, 6:134]
                    + twice(sb_ref[:, cols])
                )
                oiv[g, tile] = value
                got.append(value)
            gated = got[2] * got[1]
            d_summed = dpr[tile].astype(f32) * got[0]
            a1[t, h] = jnp.where(side == 0, gated, d_summed).astype(bf16)
            a2[t, h] = jnp.where(side == 0, d_summed, gated).astype(bf16)
        exchange(1, (t - quarter + 4) % 4).start()
        send_to(0, t)
        return 0

    lax.fori_loop(0, 4, project, 0)

    mine = lanes(quarter * 256, 256)
    pos = pos_ref[...]
    one, one_c = sin_cos(mm_full(pos, w1_ref[...]) + b1_ref[...])
    first[...] = jnp.concatenate([one, one_c], axis=1)
    two, two_c = sin_cos(mm_full(one, w2_ref[...]) + b2_ref[...])
    second[...] = jnp.concatenate([two, two_c], axis=1)
    fraction = lax.broadcasted_iota(jnp.int32, (1024, 256), 0).astype(f32) * (1.0 / 1024)
    wind = jnp.exp(-fraction * decay_ref[:, mine])
    window[...] = wind
    taps_bf = (mm_full(two, w3_ref[:, mine]) * wind).astype(bf16)
    loads[1].wait()

    def filter_rows(i, _):
        rows = lanes(i * 256, 256)
        ksp[rows] = mm(fm[rows], taps_bf)
        return 0

    lax.fori_loop(0, 8, filter_rows, 0)

    turn = jnp.where(side == 0, 1.0, -1.0)
    bias = fb_ref[:, mine]
    here = side * 512
    near, far_half = lanes(here, 512), lanes(512 - here, 512)
    wait_tiles(0)
    for p in range(4):
        send_to(2, (quarter + p + 2) % 4)

    def inverse_to(kind, u, send, given):
        for k in range(2):
            y = mm(ft[lanes(here + k * 256, 256)], zs[...]) * (1.0 / 1024)
            for h in range(2):
                block = 2 * k + h
                scale = twice(bias[:, u * 128 : u * 128 + 128])
                value = y[h * 128 : h * 128 + 128] + scale * given[block, u].astype(f32)
                send[block, u] = value.astype(bf16)
        for k in range(4):
            send_to(kind + u, (quarter + 2 + k) % 4)

    for u in range(2):
        at = slice(u * 128, u * 128 + 128)
        x_u = xs[:, u].reshape(512, 256)

        def first_rows(i, _):
            lo, hi = lanes(i * 256, 256), lanes(1024 + i * 256, 256)
            xc, x_s = mm(fm[lo, near], x_u), mm(fm[hi, near], x_u)
            kc, ks = twice(ksp[lo, at]), twice(ksp[hi, at] * turn)
            xsp[u, lo] = xc.astype(bf16)
            xsp[u, hi] = x_s.astype(bf16)
            zs[lo] = (kc * xc - ks * x_s).astype(bf16)
            zs[hi] = (kc * x_s + ks * xc).astype(bf16)
            return 0

        lax.fori_loop(0, 4, first_rows, 0)
        if u == 0:
            loads[2].wait()
        inverse_to(3, u, r1s, xs)

    for k in range(2):
        by, on = beside[k], (s, beside[1 - k])
        moves["n", k].wait()
        part = nt.at[by, 2 * k : 2 * k + 2]
        moves["n", 2 + k] = remote(part, part, b_sem, (0, 2 + k), on)
    for k in range(2):
        by, on = beside[k], (s, beside[1 - k])
        moves["c", k].wait()
        part = cot.at[by, 128 * k : 128 * k + 128]
        moves["c", 2 + k] = remote(part, part, b_sem, (1, 2 + k), on)

    wait_tiles(2)
    wait_tiles(1)
    sent_tiles(2)
    for u in range(2):
        at = slice(u * 128, u * 128 + 128)
        y_near = yo[:, u].reshape(512, 256)
        y_far = yx[:, u].reshape(512, 256)

        def second_rows(i, _):
            lo, hi = lanes(i * 256, 256), lanes(1024 + i * 256, 256)
            nc, n_s = mm(fm[lo, near], y_near), mm(fm[hi, near], y_near)
            yc = nc + mm(fm[lo, far_half], y_far)
            y_s = n_s + mm(fm[hi, far_half], y_far)
            kc, ks = twice(ksp[lo, at]), twice(ksp[hi, at] * turn)
            zs[lo] = (kc * yc + ks * y_s).astype(bf16)
            zs[hi] = (kc * y_s - ks * yc).astype(bf16)
            pc = jnp.where(side == 0, nc, yc)
            p_s = jnp.where(side == 0, n_s, y_s)
            xc, x_s = xsp[u, lo].astype(f32), xsp[u, hi].astype(f32)
            ec, e_s = xc * pc + x_s * p_s, (xc * p_s - x_s * pc) * turn
            es[lo, at] = (ec[:, :128] + ec[:, 128:]).astype(bf16)
            es[hi, at] = (e_s[:, :128] + e_s[:, 128:]).astype(bf16)
            return 0

        lax.fori_loop(0, 4, second_rows, 0)
        inverse_to(5, u, a2, yo)

    def product_moves(half, p):
        return remote(
            pts.at[:, half, (b + p) % 4],
            pt.at[b, half],
            b_sem,
            (2 + half, p),
            batch_peer(p),
            start=False,
        )

    def mixed_moves(g, p):
        return remote(
            dms.at[g, (b + p) % 4], dm.at[g, b], b_sem, (4 + g, p), batch_peer(p), start=False
        )

    def edges_of(groups, index):
        return remote(
            dsx.at[groups, :, 0:8],
            dsx.at[groups, :, 128:136],
            halo_sem,
            (index,),
            ((s + 7) % 8, b),
            start=False,
        )

    def send_edges(groups, index):
        @pl.when(s > 0)
        def _():
            edges_of(groups, index).start()

    def wait_edges(groups, index):
        @pl.when(s == 7)
        def _():
            for g in range(groups.start, groups.stop):
                for j in range(8):
                    dsx[g, j, 128:136] = jnp.zeros((8, 256), f32)

        @pl.when(s < 7)
        def _():
            edges_of(groups, index).wait_recv()

    def column_sum(v):
        v = jnp.sum(v, axis=0, keepdims=True)
        return v[:, :128] + v[:, 128:]

    def short_sums(groups):
        def one_tile(j, _):
            for g in groups:
                wide = lanes(g * 1024 + j * 128, 128)
                value = dsx[g, j, 0:128]
                for k in range(3):
                    sa[1 + k : 2 + k, wide] = column_sum(value * mx[g, j, 8 - k : 136 - k])
                sa[4:5, wide] = column_sum(value)
            return 0

        lax.fori_loop(0, 8, one_tile, 0)

    def mixed_tile(g):
        def one_tile(j, _):
            q, cols = j // 2, lanes((j % 2) * 128, 128)
            wide = lanes(g * 1024 + j * 128, 128)
            taps = sw_ref[:, wide]
            value = (
                twice(taps[0:1]) * dsx[g, j, 0:128]
                + twice(taps[1:2]) * dsx[g, j, 1:129]
                + twice(taps[2:3]) * dsx[g, j, 2:130]
            ).astype(bf16)
            dms[g, q, 0:128, cols] = value[:, :128]
            dms[g, q, 128:256, cols] = value[:, 128:]
            sa[0:1, wide] = column_sum(value.astype(f32))
            return 0

        lax.fori_loop(0, 8, one_tile, 0)
        dm[g, b] = dms[g, b]

    def send_mixed(g):
        for p in (1, 2, 3):
            mixed_moves(g, p).start()

    def send_product():
        for half in range(2):
            for p in (1, 2, 3):
                product_moves(half, p).start()

    store_out = pltpu.make_async_copy(outv, out_ref, load_sem.at[3])

    def with_summed(back, early):
        def product_tile(j, _):
            value = back[j].astype(f32)
            made = (value * oiv[0, j]).astype(bf16)
            cols = lanes(j * 128, 128)
            product[0:128, cols] = made[:, :128]
            product[128:256, cols] = made[:, 128:]
            dsx[0, j, 0:128] = dpr[j].astype(f32) * value
            return 0

        lax.fori_loop(0, 8, product_tile, 0)
        send_edges(slice(0, 1), 1)
        pts[...] = product[...].T.reshape(4, 2, 4, 32, 256)
        send_product()
        for half in range(2):
            pt[b, half] = pts[:, half, b]
        short_sums((0,))

        @pl.when(s != 3)
        def _():
            wait_edges(slice(0, 1), 1)
            mixed_tile(0)
            if early:
                send_mixed(0)

        def out_cols(i, _):
            cols = lanes(i * 256, 256)
            r = mm(product[...], w_out[:, cols]) + bout_ref[:, cols]
            for q in range(2):
                rows = slice(q * 128, q * 128 + 128)
                outv[q, :, cols] = (tok_ref[q, :, cols].astype(f32) + r[rows]).astype(bf16)
            return 0

        lax.fori_loop(0, 4, out_cols, 0)
        store_out.start()

    def with_gated(back, early):
        def gate_tile(j, _):
            value = back[j].astype(f32)
            dsx[1, j, 0:128] = value * oiv[2, j]
            dsx[2, j, 0:128] = value * oiv[1, j]
            return 0

        lax.fori_loop(0, 8, gate_tile, 0)
        send_edges(slice(1, 3), 2)
        short_sums((1, 2))
        wait_edges(slice(1, 3), 2)
        mixed_tile(1)
        send_mixed(1)
        mixed_tile(2)
        if early:
            send_mixed(2)

        @pl.when(s == 3)
        def _():
            wait_edges(slice(0, 1), 1)
            mixed_tile(0)
            send_mixed(0)

    wait_tiles(3)
    wait_tiles(4)

    @pl.when(side == 0)
    def _():
        with_summed(r1, True)

    @pl.when(side == 1)
    def _():
        with_gated(r1, True)

    wait_tiles(5)
    wait_tiles(6)

    @pl.when(side == 0)
    def _():
        with_gated(r2, False)

    @pl.when(side == 1)
    def _():
        with_summed(r2, False)

    def normed_cols(i, _):
        at = lanes(i * 256, 256)
        total = jnp.zeros((256, 256), f32)
        for g in range(3):
            for q in range(4):
                c = g * 1024 + q * 256
                total += mm(dms[g, q], w_in[at, c : c + 256], NT)
        for q in range(2):
            gtokv[q, :, at] = total[q * 128 : q * 128 + 128]
        return 0

    lax.fori_loop(0, 4, normed_cols, 0)

    def token_rows(i, sums):
        q, r = i // 4, lanes((i % 4) * 32, 32)
        rows = lanes(i * 32, 32)
        d, w = gtokv[q, r], white[rows]
        dw = d * w
        d_white = d * gain
        grad = cot_ref[rows].astype(f32) + istd[rows, 0:1] * (
            d_white
            - jnp.mean(d_white, axis=-1, keepdims=True)
            - w * jnp.mean(d_white * w, axis=-1, keepdims=True)
        )
        gtokv[q, r] = grad
        return (
            sums[0] + jnp.sum(dw, axis=0, keepdims=True),
            sums[1] + jnp.sum(d, axis=0, keepdims=True),
        )

    zero = jnp.zeros((1, 1024), f32)
    sums = lax.fori_loop(0, 8, token_rows, (zero, zero))
    store_tok = pltpu.make_async_copy(gtokv, gtok_ref, load_sem.at[4])
    store_tok.start()
    sa[5:6, 0:1024] = sums[0]
    sa[5:6, 1024:2048] = sums[1]

    def part_out(half):
        total = jnp.zeros((128, 1024), f32)
        for i in range(4):
            total += mm(pt[i, half].reshape(128, 256), cot[i])
        return total

    def part_in(g, half):
        total = jnp.zeros((512, 256), f32)
        for i in range(4):
            total += mm(nt[i, :, half].reshape(512, 256), dm[g, i])
        return total

    def shard_of(g, z):
        return lanes(g * 512 + z * 128, 128)

    beside_z, across_z = (pair * 2 + core, b), (cross * 2 + core, b)

    def core_move(g):
        return remote(core_send.at[g], core_recv.at[g], c_sem, (g, 0), other, start=False)

    def zed_move(g, k):
        to = across_z if k == 2 else beside_z
        src = core_send.at[g, shards[k]]
        return remote(src, z_recv.at[g, k], zed_sem, (g, k), to, start=False)

    def core_move_o():
        return remote(core_send_o, core_recv_o, c_sem, (3, 0), other, start=False)

    def zed_move_o(k):
        to = across_z if k == 2 else beside_z
        src = core_send_o.at[32 * k : 32 * k + 32]
        return remote(src, z_recv_o.at[k], zed_sem, (3, k), to, start=False)

    def core_half_o():
        core_send_o[...] = part_out(1 - core).astype(bf16)
        core_move_o().start()

    def core_half(g):
        core_send[g] = part_in(g, 1 - core).astype(bf16).reshape(4, 128, 256)
        core_move(g).start()

    def zed_half_o():
        total = part_out(core)
        core_move_o().wait()
        own_o[...] = (total + core_recv_o[...].astype(f32)).reshape(4, 32, 1024)
        for k in range(2):
            core_send_o[32 * k : 32 * k + 32] = own_o[shards[k]].astype(bf16)
            zed_move_o(k).start()

    def zed_half(g):
        total = part_in(g, core)
        core_move(g).wait()
        ksp[512 * g : 512 * g + 512] = total + core_recv[g].astype(f32).reshape(512, 256)
        for k in range(2):
            core_send[g, shards[k]] = ksp[shard_of(g, shards[k])].astype(bf16)
            zed_move(g, k).start()

    def cross_half_o():
        zed_move_o(0).wait()
        core_send_o[64:96] = (own_o[cross] + z_recv_o[0].astype(f32)).astype(bf16)
        zed_move_o(2).start()

    def cross_half(g):
        zed_move(g, 0).wait()
        total = ksp[shard_of(g, cross)] + z_recv[g, 0].astype(f32)
        core_send[g, cross] = total.astype(bf16)
        zed_move(g, 2).start()

    def last_half(g):
        zed_move(g, 1).wait()
        zed_move(g, 2).wait()
        total = ksp[shard_of(g, zed)] + z_recv[g, 1].astype(f32) + z_recv[g, 2].astype(f32)
        last_send[g] = total.astype(bf16).reshape(4, 32, 256)
        for p in (1, 2, 3):
            moves["l", g, p] = remote(
                last_send.at[g, (b + p) % 4], last_recv.at[g, b], l_sem, (g, p), batch_peer(p)
            )
        last_recv[g, b] = last_send[g, b]

    def half_at(k):
        return lanes(k * 1536, 1536)

    @pl.when(side == 0)
    def _():
        send_mixed(2)

    @pl.when(side == 1)
    def _():
        send_mixed(0)

    def kernel_rows(i, _):
        rows = lanes(i * 256, 256)
        window[rows] = mm(ft[rows], es[...]) * (1.0 / 1024) * window[rows]
        return 0

    lax.fori_loop(0, 4, kernel_rows, 0)
    sc[...] = jnp.zeros(sc.shape, f32)
    direct = []
    for u in range(2):
        both = xs[:, u].astype(f32) * yo[:, u].astype(f32)
        direct.append(column_sum(both.reshape(512, 256)))
    direct = jnp.broadcast_to(jnp.concatenate(direct, axis=1), (64, 256)).T

    def low(v):
        return v.astype(bf16)

    d_shaped = low(window[...])
    sb[...] = jnp.concatenate([mm(d_shaped, low(second[:, 0:64]), TN), direct], axis=1)
    d_two = mm(d_shaped, low(w3_ref[:, mine]), NT) * second[:, 64:128]
    sc[0:64, 64:128] = mm(low(first[:, 0:64]), low(d_two), TN)
    sc[40:41, 0:64] = jnp.sum(d_two, axis=0, keepdims=True)
    d_one = mm(low(d_two), low(w2_ref[...]), NT) * first[:, 64:128]
    sc[0:33, 0:64] = mm(low(pos_ref[...]), low(d_one), TN)
    sc[41:42, 0:64] = jnp.sum(d_one, axis=0, keepdims=True)
    def rows_at(k):
        return pl.ds(pl.multiple_of(k * 32, 32), 32)

    def small_remote(src, dst, index, peer):
        return remote(src, dst, v_sem, (index,), peer)

    smalls = [
        small_remote(sa.at[:, half_at(1 - core)], sr.at[0], 0, other),
        small_remote(sc.at[rows_at(1 - core)], st.at[0], 1, other),
    ]
    for k in (2, 3):
        moves["n", k].wait()
        moves["c", k].wait()

    def arrived(g):
        for p in (1, 2, 3):
            mixed_moves(g, p).wait()

    def arrived_o():
        for p in (1, 2, 3):
            product_moves(0, p).wait()
            product_moves(1, p).wait()

    @pl.when(side == 0)
    def _():
        arrived_o()
        core_half_o()
        arrived(0)
        core_half(0)
        zed_half_o()
        zed_half(0)

    @pl.when(side == 1)
    def _():
        arrived(1)
        core_half(1)
        arrived(2)
        core_half(2)
        zed_half(1)
        zed_half(2)

    for move in smalls:
        move.wait()
    def fold(v):
        return jnp.concatenate([v[:, :768], v[:, 768:]], axis=0).astype(bf16)

    def total_of(array, first):
        return sum(array[first + i].astype(f32) for i in range(1, 4)) + array[first].astype(f32)

    vb[b] = fold(sa[:, half_at(core)] + sr[0])
    sq[b] = (sc[rows_at(core)] + st[0]).astype(bf16)
    sp[4:12] = sb[...].astype(bf16).reshape(8, 32, 128)
    for u in range(2):
        sp[2 * b + u + 12] = sp[4 + 4 * u + b]
    smalls = []
    for p in (1, 2, 3):
        smalls += [
            small_remote(vb.at[b], vb.at[b], 1 + p, batch_peer(p)),
            small_remote(sq.at[b], sq.at[b], 4 + p, batch_peer(p)),
            small_remote(sp.at[4 + (b + p) % 4], sp.at[12 + 2 * b], 7 + p, batch_peer(p)),
            small_remote(sp.at[8 + (b + p) % 4], sp.at[13 + 2 * b], 20 + p, batch_peer(p)),
        ]

    @pl.when(side == 0)
    def _():
        arrived(1)
        core_half(1)
        cross_half_o()
        cross_half(0)
        zed_half(1)

    @pl.when(side == 1)
    def _():
        arrived_o()
        core_half_o()
        cross_half(1)
        cross_half(2)
        zed_half_o()

    for move in smalls:
        move.wait()
    vb[4 + zed] = total_of(vb, 0).astype(bf16)
    sq[4 + zed] = total_of(sq, 0).astype(bf16)
    for u in range(2):
        part = sum(sp[12 + 2 * i + u].astype(f32) for i in range(4))
        sb[32 * u : 32 * u + 32] = part
        sp[u] = part.astype(bf16)
    smalls = [small_remote(sp.at[0:2], sp.at[2:4], 17, across_z)]
    for p in (1, 2, 3):
        smalls += [
            small_remote(vb.at[4 + zed], vb.at[4 + zed], 10 + p, zed_peer(p)),
            small_remote(sq.at[4 + zed], sq.at[4 + zed], 13 + p, zed_peer(p)),
        ]
    @pl.when(side == 0)
    def _():
        arrived(2)
        core_half(2)
        cross_half(1)
        zed_half(2)
        cross_half(2)

    @pl.when(side == 1)
    def _():
        arrived(0)
        core_half(0)
        cross_half_o()
        zed_half(0)
        cross_half(0)

    for move in smalls:
        move.wait()
    for u in range(2):
        sb[32 * u : 32 * u + 32] = sb[32 * u : 32 * u + 32] + sp[2 + u].astype(f32)
    folded = total_of(vb, 4)
    sf[...] = jnp.concatenate([folded[:8], folded[8:]], axis=1)
    sh[...] = total_of(sq, 4)
    smalls = [
        small_remote(sf, sr.at[1], 18, other),
        small_remote(sh, st.at[1], 19, other),
    ]
    owner = quarter * 2 + side

    def give():
        return remote(
            sb.at[lanes(side * 32, 32)], sg, v_sem, (24,), (owner, b), start=False
        )

    @pl.when(owner != s)
    def _():
        give().start()

    @pl.when(owner == s)
    def _():
        sg[...] = sb[lanes(side * 32, 32)]

    last_half(0)
    zed_move_o(1).wait()
    zed_move_o(2).wait()
    gwout_ref[...] = own_o[zed] + z_recv_o[1].astype(f32) + z_recv_o[2].astype(f32)
    last_half(1)
    last_half(2)
    for move in smalls:
        move.wait()
    oa_ref[:, half_at(core)] = sf[...]
    oa_ref[:, half_at(1 - core)] = sr[1]
    oc_ref[rows_at(core)] = sh[...]
    oc_ref[rows_at(1 - core)] = st[1]

    @pl.when(owner != s)
    def _():
        give().wait()

    ob_ref[...] = sg[...]
    for g in range(3):
        for p in (1, 2, 3):
            moves["l", g, p].wait()
        for i in range(4):
            c = g * 1024 + i * 256
            gwin_ref[:, c : c + 256] = last_recv[g, i].astype(f32)
    store_out.wait()
    store_tok.wait()
    for kind in (0, 1, 3, 4, 5, 6):
        sent_tiles(kind)

    @pl.when(s < 7)
    def _():
        edge.wait_send()

    @pl.when(s > 0)
    def _():
        edges_of(slice(0, 1), 1).wait_send()
        edges_of(slice(1, 3), 2).wait_send()


def whole(args, positions, matrix):
    vmem, anywhere = (pl.BlockSpec(memory_space=m) for m in (pltpu.VMEM, pl.ANY))
    dma = pltpu.SemaphoreType.DMA
    specs = [vmem] * 20
    for i in (4, 15, 18, 19):
        specs[i] = anywhere
    shape = jax.ShapeDtypeStruct

    def v(dtype, *dims):
        return pltpu.VMEM(dims, dtype)

    return pl.pallas_call(
        whole_kernel,
        out_shape=(
            shape((2, 128, 1024), bf16),
            shape((2, 128, 1024), f32),
            shape((32, 3072), f32),
            shape((32, 1024), f32),
            shape((8, 3072), f32),
            shape((32, 128), f32),
            shape((64, 128), f32),
        ),
        in_specs=specs,
        out_specs=(anywhere,) * 2 + (vmem,) * 5,
        scratch_shapes=[
            v(bf16, 1024, 3072),
            v(bf16, 1024, 1024),
            v(bf16, 2048, 1024),
            v(bf16, 1024, 2048),
            v(bf16, 2, 16, 1024),
            v(f32, 256, 1024),
            v(f32, 256, 128),
            v(bf16, 288, 1024),
            v(f32, 3, 8, 136, 256),
            v(f32, 3, 8, 128, 256),
            v(bf16, 8, 128, 256),
            v(bf16, 4, 2, 128, 256),
            v(bf16, 4, 2, 128, 256),
            v(bf16, 4, 2, 128, 256),
            v(bf16, 4, 2, 128, 256),
            v(bf16, 4, 2, 128, 256),
            v(bf16, 4, 2, 128, 256),
            v(bf16, 8, 128, 256),
            v(bf16, 8, 128, 256),
            v(f32, 1024, 128),
            v(f32, 1024, 128),
            v(f32, 1024, 256),
            v(f32, 2048, 256),
            v(bf16, 2, 2048, 256),
            v(bf16, 2048, 256),
            v(bf16, 2048, 256),
            v(bf16, 256, 1024),
            v(bf16, 4, 2, 4, 32, 256),
            v(f32, 3, 8, 136, 256),
            v(bf16, 3, 4, 256, 256),
            v(bf16, 4, 4, 2, 128, 256),
            v(bf16, 4, 2, 4, 32, 256),
            v(bf16, 3, 4, 256, 256),
            v(bf16, 4, 256, 1024),
            v(bf16, 3, 4, 128, 256),
            v(bf16, 3, 4, 128, 256),
            v(bf16, 128, 1024),
            v(bf16, 128, 1024),
            v(f32, 4, 32, 1024),
            v(bf16, 2, 128, 1024),
            v(f32, 2, 128, 1024),
            v(bf16, 3, 3, 128, 256),
            v(bf16, 3, 32, 1024),
            v(bf16, 3, 4, 32, 256),
            v(bf16, 3, 4, 32, 256),
            v(f32, 8, 3072),
            v(f32, 2, 8, 1536),
            v(f32, 8, 1536),
            v(f32, 256, 128),
            v(bf16, 20, 32, 128),
            v(bf16, 8, 16, 768),
            v(f32, 32, 128),
            v(f32, 64, 128),
            v(bf16, 8, 32, 128),
            v(f32, 2, 32, 128),
            v(f32, 32, 128),
            dma((5,)),
            dma((3, 4)),
            dma((2, 25)),
            dma((2, 3)),
            dma((2, 7, 4)),
            dma((2, 7, 4)),
            dma((2, 4, 4)),
            dma((2, 4, 4)),
            dma((2, 3, 4)),
        ],
        compiler_params=pltpu.CompilerParams(
            collective_id=0, has_side_effects=True, vmem_limit_bytes=63 * 1024 * 1024
        ),
    )(*args, positions, matrix, np.ascontiguousarray(matrix.T))


def settle_kernel(
    out_ref,
    gtok_ref,
    gwin_ref,
    gwout_ref,
    sa_ref,
    sb_ref,
    sc_ref,
    out,
    gtok,
    ln_gain,
    ln_bias,
    gwin,
    b_in,
    short_w,
    short_b,
    w_one,
    b_one,
    w_two,
    b_two,
    w_three,
    filt,
    gwout,
    b_out,
    sems,
):
    copies = [
        pltpu.make_async_copy(src, dst, sems.at[i])
        for i, (src, dst) in enumerate(
            ((out_ref, out), (gtok_ref, gtok), (gwin_ref, gwin), (gwout_ref, gwout))
        )
    ]
    for copy in copies:
        copy.start()
    b = lax.axis_index("batch")
    place = lax.axis_index("seq") * 4 + b
    sa = sa_ref[...]
    wide = pltpu.roll(sa, (32 - place) * 96, 1)
    b_in[...] = wide[0:1, :96]
    short_w[...] = wide[1:4, :96]
    short_b[...] = wide[4:5, :96]
    thin = pltpu.roll(sa, (96 - place) * 32, 1)
    ln_gain[...] = thin[5:6, 0:32]
    ln_bias[...] = thin[5:6, 1024:1056]
    b_out[...] = thin[5:6, 2048:2080]
    w_three[...] = sb_ref[:, 0:64]
    filt[...] = sb_ref[...].T[64:65, 0:32]
    w_one[...] = sc_ref[0:33, 0:64]
    w_two[...] = sc_ref[0:64, 64:128]
    b_two[...] = sc_ref[40:41, 0:64]
    b_one[...] = sc_ref[41:42, 0:64]
    for copy in copies:
        copy.wait()


def settle(parts):
    vmem, anywhere = (pl.BlockSpec(memory_space=m) for m in (pltpu.VMEM, pl.ANY))
    sizes = (
        (2, 128, 1024),
        (2, 128, 1024),
        (1, 32),
        (1, 32),
        (32, 3072),
        (1, 96),
        (3, 96),
        (1, 96),
        (33, 64),
        (1, 64),
        (64, 64),
        (1, 64),
        (32, 64),
        (1, 32),
        (32, 1024),
        (1, 32),
    )
    flat = (2, 3, 5, 7, 9, 11, 13, 15)
    outs = pl.pallas_call(
        settle_kernel,
        out_shape=tuple(
            jax.ShapeDtypeStruct(size, f32 if i else bf16) for i, size in enumerate(sizes)
        ),
        in_specs=[anywhere] * 4 + [vmem] * 3,
        out_specs=(vmem,) * 16,
        scratch_shapes=[pltpu.SemaphoreType.DMA((4,))],
    )(*parts)
    return tuple(
        o.reshape(-1) if i in flat else o.T if i == 12 else o for i, o in enumerate(outs)
    )


def local_small(*args):
    cotangent = args[1]
    vectors = {2, 3, 5, 7, 9, 11, 13, 14, 16}
    given = [a.reshape(1, -1) if i in vectors else a for i, a in enumerate(args)]
    given[1] = cotangent.reshape(256, 1024)
    return settle(whole(given, position_features(1024, args[8].shape[0]), dft_matrix(1024)))


def solution(mesh):
    tokens_spec = P("batch", "seq", None)
    both = ("seq", "batch")
    in_specs = (tokens_spec, tokens_spec) + (P(),) * 15
    out_specs = (
        tokens_spec,
        tokens_spec,
        P(both),
        P(both),
        P(both, None),
        P(both),
        P(None, both),
        P(both),
        P(),
        P(),
        P(),
        P(),
        P(None, both),
        P(both),
        P(both, None),
        P(both),
    )

    def per_device(*args):
        tokens, w_one = args[0], args[8]
        sizes = (mesh.shape["seq"], mesh.shape["batch"]) + tokens.shape + w_one.shape
        fits = sizes == (8, 4, 2, 128, 1024, 33, 64)
        return (local_small if fits else local)(*args)

    return jax.shard_map(per_device, mesh=mesh, in_specs=in_specs, out_specs=out_specs, check_vma=False)
```

```python
import jax
import jax.numpy as jnp
import numpy as np
from jax import lax
from jax.experimental import pallas as pl
from jax.experimental.pallas import tpu as pltpu
from jax.sharding import PartitionSpec as P

highest = lax.Precision.HIGHEST
epsilon = 1e-05
f32, bf16 = jnp.float32, jnp.bfloat16


def dft_matrix(length):
    turns = ((2 * np.arange(length)[:, None] + 1) * np.arange(length)[None, :]) % (4 * length)
    phases = turns * (np.pi / (2 * length))
    return np.concatenate([np.cos(phases), np.sin(phases)], axis=0).astype(bf16)


def position_features(length, features):
    step_axis = np.arange(length, dtype=np.float64)
    band_count = (features - 1) // 2
    band_rates = 0.0001 + np.arange(band_count) * (band_count - 1 - 0.0001) / (band_count - 1)
    phases = 2.0 * np.pi / length * step_axis[:, None] * band_rates[None, :]
    return np.concatenate(
        [(step_axis / length)[:, None], np.cos(phases), -np.sin(phases)], axis=1
    ).astype(np.float32)


def filter_shape(positions, w_one, b_one, w_two, b_two, w_three, decay_rates):
    first_layer = jnp.sin(jnp.dot(positions, w_one, precision=highest) + b_one)
    second_layer = jnp.sin(jnp.dot(first_layer, w_two, precision=highest) + b_two)
    shaped = jnp.dot(second_layer, w_three, precision=highest)
    length = positions.shape[0]
    fraction = jnp.arange(length).astype(f32) / length
    return shaped * jnp.exp(-fraction[:, None] * decay_rates[None, :])


def shifted(value, axis, steps):
    count = lax.axis_size(axis)
    first, last = (max(0, -steps), min(count, count - steps))
    return lax.ppermute(value, axis, [(source, source + steps) for source in range(first, last)])


def reduce_scatter(value, dtype):
    out = lax.all_to_all(value.astype(dtype), "batch", split_axis=1, concat_axis=1, tiled=True)
    out = jnp.sum(out.astype(f32), axis=1)
    out = lax.all_to_all(out.astype(dtype), "seq", split_axis=0, concat_axis=0, tiled=True)
    return jnp.sum(out.astype(f32), axis=0)


def local(
    tokens,
    cotangent,
    ln_gain,
    ln_bias,
    w_in,
    b_in,
    short_w,
    short_b,
    w_one,
    b_one,
    w_two,
    b_two,
    w_three,
    decay_rates,
    filt_bias,
    w_out,
    b_out,
):
    seq_count, block_len, model_width = tokens.shape
    seq_devices = lax.axis_size("seq")
    batch_devices = lax.axis_size("batch")
    devices = seq_devices * batch_devices
    length = block_len * seq_devices
    channels = model_width // seq_devices
    col_start = lax.axis_index("seq") * channels
    inputs = tokens.astype(f32)
    average = jnp.mean(inputs, axis=-1, keepdims=True)
    centered = inputs - average
    inv_std = lax.rsqrt(jnp.mean(centered * centered, axis=-1, keepdims=True) + epsilon)
    whitened = centered * inv_std
    normed = (whitened * ln_gain + ln_bias).astype(bf16)
    mixed = jnp.einsum("btd,de->bte", normed, w_in, preferred_element_type=f32) + b_in
    prev_rows = shifted(mixed[:, block_len - 2 :], "seq", 1)
    padded = jnp.concatenate([prev_rows, mixed], axis=1)
    delay_one = padded[:, 1:-1]
    delay_two = padded[:, :-2]
    short_out = short_w[0] * mixed + short_w[1] * delay_one + short_w[2] * delay_two + short_b
    outer_gate = short_out[..., :model_width]
    inner_gate = short_out[..., model_width : 2 * model_width]
    values = short_out[..., 2 * model_width :]
    gated = (values * inner_gate).astype(bf16)
    d_product = jnp.einsum(
        "bte,de->btd", cotangent, w_out, preferred_element_type=f32
    ).astype(bf16)
    d_prod_f = d_product.astype(f32)
    d_summed = (d_prod_f * outer_gate).astype(bf16)

    def to_channels(value):
        return lax.all_to_all(value, "seq", split_axis=2, concat_axis=1, tiled=True)

    def to_tokens(value):
        return lax.all_to_all(value, "seq", split_axis=1, concat_axis=2, tiled=True)

    gated_ch = to_channels(gated)
    d_ch = to_channels(d_summed)
    positions = jnp.asarray(position_features(length, w_one.shape[0]))
    w_three_part = lax.dynamic_slice_in_dim(w_three, col_start, channels, 1)
    decay_part = lax.dynamic_slice_in_dim(decay_rates, col_start, channels, 0)
    bias_part = lax.dynamic_slice_in_dim(filt_bias, col_start, channels, 0)

    def kernel_of(first_w, first_b, second_w, second_b, third_w):
        return filter_shape(positions, first_w, first_b, second_w, second_b, third_w, decay_part)

    kernel_full, kernel_pull = jax.vjp(kernel_of, w_one, b_one, w_two, b_two, w_three_part)
    matrix = jnp.asarray(dft_matrix(length))

    def spectrum(value):
        return jnp.einsum("kt,btc->bkc", matrix, value, preferred_element_type=f32)

    def inverse(cosines, sines):
        both = jnp.concatenate([cosines, sines], axis=1).astype(bf16)
        return jnp.einsum("kt,bkc->btc", matrix, both, preferred_element_type=f32) * (1.0 / length)

    k_both = spectrum(kernel_full.astype(bf16)[None])
    g_both = spectrum(gated_ch)
    d_both = spectrum(d_ch)
    k_c, k_s = k_both[:, :length], k_both[:, length:]
    g_c, g_s = g_both[:, :length], g_both[:, length:]
    d_c, d_s = d_both[:, :length], d_both[:, length:]
    long_out = inverse(g_c * k_c - g_s * k_s, g_c * k_s + g_s * k_c)
    gated_float = gated_ch.astype(f32)
    d_ch_float = d_ch.astype(f32)
    summed_ch = (long_out + bias_part * gated_float).astype(bf16)
    summed = to_tokens(summed_ch).astype(f32)
    grad_in = inverse(k_c * d_c + k_s * d_s, k_c * d_s - k_s * d_c) + bias_part * d_ch_float
    d_gated = to_tokens(grad_in.astype(bf16)).astype(f32)
    d_kernel = inverse(
        jnp.sum(g_c * d_c + g_s * d_s, axis=0, keepdims=True),
        jnp.sum(g_c * d_s - g_s * d_c, axis=0, keepdims=True),
    )[0]
    g_bias_part = jnp.sum(d_ch_float * gated_float, axis=(0, 1))
    g_w_one, g_b_one, g_w_two, g_b_two, g_w_three_part = kernel_pull(d_kernel)

    product = (summed * outer_gate).astype(bf16)
    result = jnp.einsum("btd,de->bte", product, w_out, preferred_element_type=f32) + b_out
    block_out = (inputs + result).astype(bf16)
    grad_out = cotangent.astype(f32)
    g_w_out = jnp.einsum("btd,bte->de", product, cotangent, preferred_element_type=f32)
    g_b_out = jnp.sum(grad_out, axis=(0, 1))
    d_outer = d_prod_f * summed
    d_short = jnp.concatenate([d_outer, d_gated * values, d_gated * inner_gate], axis=-1)
    g_short_w = jnp.stack(
        [
            jnp.sum(d_short * mixed, axis=(0, 1)),
            jnp.sum(d_short * delay_one, axis=(0, 1)),
            jnp.sum(d_short * delay_two, axis=(0, 1)),
        ]
    )
    g_short_b = jnp.sum(d_short, axis=(0, 1))
    next_rows = shifted(d_short[:, :2], "seq", -1)
    extended = jnp.concatenate([d_short, next_rows], axis=1)
    d_mixed = (
        short_w[0] * extended[:, :block_len]
        + short_w[1] * extended[:, 1 : block_len + 1]
        + short_w[2] * extended[:, 2:]
    ).astype(bf16)
    g_w_in = jnp.einsum("btd,bte->de", normed, d_mixed, preferred_element_type=f32)
    g_b_in = jnp.sum(d_mixed.astype(f32), axis=(0, 1))
    d_normed = jnp.einsum("bte,de->btd", d_mixed, w_in, preferred_element_type=f32)
    g_ln_gain = jnp.sum(d_normed * whitened, axis=(0, 1))
    g_ln_bias = jnp.sum(d_normed, axis=(0, 1))
    d_white = d_normed * ln_gain
    grad_tokens = grad_out + inv_std * (
        d_white
        - jnp.mean(d_white, axis=-1, keepdims=True)
        - whitened * jnp.mean(d_white * whitened, axis=-1, keepdims=True)
    )
    rows = model_width // devices
    big = jnp.concatenate([g_w_in, g_w_out], axis=1)
    big = reduce_scatter(big.reshape(seq_devices, batch_devices, rows, -1), bf16)
    out_w_in, out_w_out = big[:, : 3 * model_width], big[:, 3 * model_width :]
    g_w_three = lax.dynamic_update_slice_in_dim(
        jnp.zeros(w_three.shape, f32), g_w_three_part, col_start, 1
    )
    g_filt_bias = lax.dynamic_update_slice_in_dim(
        jnp.zeros(filt_bias.shape, f32), g_bias_part, col_start, 0
    )
    vectors = jnp.concatenate(
        [
            g_ln_gain[None],
            g_ln_bias[None],
            g_b_out[None],
            g_filt_bias[None],
            g_w_three,
        ],
        axis=0,
    )
    vectors = jnp.transpose(vectors.reshape(-1, devices, rows), (1, 0, 2)).reshape(devices, -1)
    wides = jnp.concatenate([g_b_in[None], g_short_w, g_short_b[None]], axis=0)
    wides = jnp.transpose(wides.reshape(-1, devices, 3 * rows), (1, 0, 2)).reshape(devices, -1)
    net = jnp.concatenate([v.reshape(-1) for v in (g_w_one, g_b_one, g_w_two, g_b_two)])
    net_size = net.shape[0]
    net_part = -(-net_size // devices)
    net = jnp.pad(net, (0, net_part * devices - net_size)).reshape(devices, net_part)
    small = jnp.concatenate([vectors, wides, net], axis=1)
    small = reduce_scatter(small.reshape(seq_devices, batch_devices, -1), f32)
    hidden = w_two.shape[0]
    cut = rows * (4 + hidden)
    vectors = small[:cut].reshape(4 + hidden, rows)
    wides = small[cut : cut + 15 * rows].reshape(5, 3 * rows)
    net = lax.all_gather(small[cut + 15 * rows :], ("seq", "batch"), tiled=True)
    features = w_one.shape[0]
    edges = [features * hidden, (features + 1) * hidden, (features + 1 + hidden) * hidden]
    return (
        block_out,
        grad_tokens,
        vectors[0],
        vectors[1],
        out_w_in,
        wides[0],
        wides[1:4],
        wides[4],
        net[: edges[0]].reshape(features, hidden),
        net[edges[0] : edges[1]],
        net[edges[1] : edges[2]].reshape(hidden, hidden),
        net[edges[2] : net_size],
        vectors[4:],
        vectors[3],
        out_w_out,
        vectors[2],
    )


MESH = pl.DeviceIdType.MESH
HALF_TURN = (1.5703125, 4.837512969970703125e-4, 7.549789948768648e-8)


def sin_cos(x):
    turns = jnp.floor(x * 0.6366197723675814 + 0.5)
    r = ((x - turns * HALF_TURN[0]) - turns * HALF_TURN[1]) - turns * HALF_TURN[2]
    q = turns.astype(jnp.int32)
    r2 = r * r
    sine = r + r * r2 * (
        -1.6666654611e-1 + r2 * (8.3321608736e-3 + r2 * -1.9515295891e-4)
    )
    cosine = 1.0 - 0.5 * r2 + r2 * r2 * (
        4.166664568298827e-2 + r2 * (-1.388731625493765e-3 + r2 * 2.443315711809948e-5)
    )
    odd = (q & 1) == 1
    s_abs, c_abs = jnp.where(odd, cosine, sine), jnp.where(odd, sine, cosine)
    s_neg, c_neg = (q & 2) == 2, ((q + 1) & 2) == 2
    return jnp.where(s_neg, -s_abs, s_abs), jnp.where(c_neg, -c_abs, c_abs)


def mm(a, b, dims=((1,), (0,))):
    return lax.dot_general(a, b, (dims, ((), ())), preferred_element_type=f32)


def mm_full(a, b, dims=((1,), (0,))):
    return lax.dot_general(
        a, b, (dims, ((), ())), precision=highest, preferred_element_type=f32
    )


def twice(v):
    return jnp.concatenate([v, v], axis=1)


def lanes(start, size):
    return pl.ds(pl.multiple_of(start, size), size)


NT, TN = ((1,), (1,)), ((0,), (0,))


def whole_kernel(
    tok_ref,
    cot_ref,
    gain_ref,
    beta_ref,
    win_ref,
    bin_ref,
    sw_ref,
    sb_ref,
    w1_ref,
    b1_ref,
    w2_ref,
    b2_ref,
    w3_ref,
    decay_ref,
    fb_ref,
    wout_ref,
    bout_ref,
    pos_ref,
    f_ref,
    ft_ref,
    out_ref,
    gtok_ref,
    gwin_ref,
    gwout_ref,
    oa_ref,
    ob_ref,
    oc_ref,
    w_in,
    w_out,
    fm,
    ft,
    halo,
    white,
    istd,
    normed,
    mx,
    oiv,
    dpr,
    a1,
    a2,
    xs,
    yo,
    yx,
    r1s,
    r1,
    r2,
    first,
    second,
    window,
    ksp,
    xsp,
    zs,
    es,
    product,
    pts,
    dsx,
    dms,
    nt,
    pt,
    dm,
    cot,
    core_send,
    core_recv,
    core_send_o,
    core_recv_o,
    own_o,
    outv,
    gtokv,
    z_recv,
    z_recv_o,
    last_send,
    last_recv,
    sa,
    sr,
    sf,
    sb,
    sp,
    vb,
    sg,
    sc,
    sq,
    st,
    sh,
    load_sem,
    in_sem,
    v_sem,
    halo_sem,
    a_sem,
    b_sem,
    c_sem,
    zed_sem,
    l_sem,
):
    s, b = lax.axis_index("seq"), lax.axis_index("batch")
    zed, core = s // 2, s % 2
    side, quarter = s // 4, s % 4
    pair, cross = zed // 2 * 2 + 1 - zed % 2, (zed + 2) % 4
    pair_cross = (pair + 2) % 4
    other = (zed * 2 + 1 - core, b)

    loads = [
        pltpu.make_async_copy(src, dst, load_sem.at[i])
        for i, (src, dst) in enumerate(((wout_ref, w_out), (f_ref, fm), (ft_ref, ft)))
    ]

    def load_in(g, i):
        cols = lanes(g * 1024 + (quarter + 2 + i) % 4 * 256, 256)
        return pltpu.make_async_copy(win_ref.at[:, cols], w_in.at[:, cols], in_sem.at[g, i])

    loads[0].start()
    for i in range(4):
        for g in range(3):
            load_in(g, i).start()
    loads[1].start()
    loads[2].start()

    def batch_peer(p):
        return (s, (b + p) % 4)

    def zed_peer(p):
        return (((zed + p) % 4) * 2 + core, b)

    barrier = pltpu.get_barrier_semaphore()
    for p in range(1, 8):
        pl.semaphore_signal(
            barrier, inc=1, device_id=((s + p) % 8, b), device_id_type=MESH
        )
    for p in range(1, 4):
        pl.semaphore_signal(barrier, inc=1, device_id=batch_peer(p), device_id_type=MESH)

    def remote(src, dst, sems, index, peer, start=True):
        copy = pltpu.make_async_remote_copy(
            src_ref=src,
            dst_ref=dst,
            send_sem=sems.at[(0,) + index],
            recv_sem=sems.at[(1,) + index],
            device_id=peer,
            device_id_type=MESH,
        )
        if start:
            copy.start()
        return copy

    gain, beta = gain_ref[...], beta_ref[...]

    def white_of(x):
        x = x.astype(f32)
        centered = x - jnp.mean(x, axis=-1, keepdims=True)
        inv = lax.rsqrt(jnp.mean(centered * centered, axis=-1, keepdims=True) + epsilon)
        return centered * inv, inv

    def norm_rows(i, _):
        q, r = i // 4, (i % 4) * 32
        rows = lanes(i * 32, 32)
        w, inv = white_of(tok_ref[q, lanes(r, 32)])
        white[rows] = w
        istd[rows] = jnp.broadcast_to(inv, (32, 128))
        normed[rows] = (w * gain + beta).astype(bf16)
        return 0

    lax.fori_loop(0, 8, norm_rows, 0)

    pl.semaphore_wait(barrier, 10)
    edge = remote(
        tok_ref.at[:, 112:128],
        halo,
        halo_sem,
        (0,),
        ((s + 1) % 8, b),
        start=False,
    )

    @pl.when(s < 7)
    def _():
        edge.start()

    nt[b] = normed[0:256].T.reshape(4, 2, 128, 256)
    moves = {}
    shards = (pair_cross, pair, cross, zed)
    x, y = b % 2, b // 2
    beside = (y * 2 + 1 - x, (1 - y) * 2 + x)
    for k in range(2):
        moves["n", k] = remote(nt.at[b], nt.at[b], b_sem, (0, k), (s, beside[k]))
    for k in range(2):
        moves["c", k] = remote(cot_ref, cot.at[b], b_sem, (1, k), (s, beside[k]))

    loads[0].wait()
    cot_here = cot_ref[...]
    cot[b] = cot_here

    def backproject(t, _):
        m = mm(cot_here, w_out[lanes(t * 256, 256)], NT).astype(bf16)
        for h in range(2):
            at = slice(h * 128, h * 128 + 128)
            dpr[2 * t + h] = jnp.concatenate([m[0:128, at], m[128:256, at]], axis=1)
        return 0

    lax.fori_loop(0, 4, backproject, 0)
    sa[...] = jnp.zeros(sa.shape, f32)
    sa[5:6, 2048:3072] = jnp.sum(cot_here.astype(f32), axis=0, keepdims=True)

    @pl.when(s == 0)
    def _():
        halo[...] = jnp.zeros_like(halo)

    @pl.when(s > 0)
    def _():
        edge.wait_recv()

    w, _inv = white_of(halo[...].reshape(32, 1024))
    normed[256:288] = (w * gain + beta).astype(bf16)

    def exchange(kind, p):
        to = (quarter + p) % 4
        target = side * 4 + to
        if kind == 0:
            src, dst = a1.at[to], xs.at[quarter]
        elif kind == 1:
            src, dst, target = a1.at[to], yx.at[quarter], (1 - side) * 4 + to
        elif kind == 2:
            src, dst = a2.at[to], yo.at[quarter]
        else:
            u = (kind - 3) % 2
            send, recv = ((r1s, r1), (a2, r2))[(kind - 3) // 2]
            src, dst = send.at[to, u], recv.at[2 * quarter + u]
        return remote(src, dst, a_sem, (kind, p), (target, b), start=False)

    def send_to(kind, to):
        p = (to - quarter + 4) % 4

        @pl.when(p != 0)
        def _():
            exchange(kind, p).start()

        @pl.when(p == 0)
        def _():
            if kind == 0:
                xs[quarter] = a1[quarter]
            elif kind == 2:
                yo[quarter] = a2[quarter]
            else:
                u = (kind - 3) % 2
                send, recv = ((r1s, r1), (a2, r2))[(kind - 3) // 2]
                recv[2 * quarter + u] = send[quarter, u]

    def sent_tiles(kind):
        for p in range(0 if kind == 1 else 1, 4):
            exchange(kind, p).wait_send()

    def wait_tiles(kind):
        for p in range(0 if kind == 1 else 1, 4):
            exchange(kind, p).wait_recv()


    def project(i, _):
        t = (quarter + 2 + i) % 4
        for g in range(3):
            load_in(g, i).wait()
            cols = lanes(g * 1024 + t * 256, 256)
            m = mm(normed[...], w_in[:, cols]) + bin_ref[:, cols]
            for h in range(2):
                at = slice(h * 128, h * 128 + 128)
                tile = 2 * t + h
                edge_rows = jnp.concatenate([m[264:272, at], m[280:288, at]], axis=1)
                mx[g, tile, 0:8] = jnp.where(s > 0, edge_rows, 0.0)
                mx[g, tile, 8:136] = jnp.concatenate([m[0:128, at], m[128:256, at]], axis=1)
        for h in range(2):
            tile = 2 * t + h
            got = []
            for g in range(3):
                cols = lanes(g * 1024 + tile * 128, 128)
                taps = sw_ref[:, cols]
                value = (
                    twice(taps[0:1]) * mx[g, tile, 8:136]
                    + twice(taps[1:2]) * mx[g, tile, 7:135]
                    + twice(taps[2:3]) * mx[g, tile, 6:134]
                    + twice(sb_ref[:, cols])
                )
                oiv[g, tile] = value
                got.append(value)
            gated = got[2] * got[1]
            d_summed = dpr[tile].astype(f32) * got[0]
            a1[t, h] = jnp.where(side == 0, gated, d_summed).astype(bf16)
            a2[t, h] = jnp.where(side == 0, d_summed, gated).astype(bf16)
        exchange(1, (t - quarter + 4) % 4).start()
        send_to(0, t)
        send_to(2, t)
        return 0

    lax.fori_loop(0, 4, project, 0)

    mine = lanes(quarter * 256, 256)
    pos = pos_ref[...]
    one, one_c = sin_cos(mm_full(pos, w1_ref[...]) + b1_ref[...])
    first[...] = jnp.concatenate([one, one_c], axis=1)
    two, two_c = sin_cos(mm_full(one, w2_ref[...]) + b2_ref[...])
    second[...] = jnp.concatenate([two, two_c], axis=1)
    fraction = lax.broadcasted_iota(jnp.int32, (1024, 256), 0).astype(f32) * (1.0 / 1024)
    wind = jnp.exp(-fraction * decay_ref[:, mine])
    window[...] = wind
    taps_bf = (mm_full(two, w3_ref[:, mine]) * wind).astype(bf16)
    loads[1].wait()

    def filter_rows(i, _):
        rows = lanes(i * 256, 256)
        ksp[rows] = mm(fm[rows], taps_bf)
        return 0

    lax.fori_loop(0, 8, filter_rows, 0)

    turn = jnp.where(side == 0, 1.0, -1.0)
    bias = fb_ref[:, mine]
    here = side * 512
    near, far_half = lanes(here, 512), lanes(512 - here, 512)
    wait_tiles(0)

    def inverse_to(kind, u, send, given):
        for k in range(2):
            y = mm(ft[lanes(here + k * 256, 256)], zs[...]) * (1.0 / 1024)
            for h in range(2):
                block = 2 * k + h
                scale = twice(bias[:, u * 128 : u * 128 + 128])
                value = y[h * 128 : h * 128 + 128] + scale * given[block, u].astype(f32)
                send[block, u] = value.astype(bf16)
        for k in range(4):
            send_to(kind + u, (quarter + 2 + k) % 4)

    for u in range(2):
        at = slice(u * 128, u * 128 + 128)
        x_u = xs[:, u].reshape(512, 256)

        def first_rows(i, _):
            lo, hi = lanes(i * 256, 256), lanes(1024 + i * 256, 256)
            xc, x_s = mm(fm[lo, near], x_u), mm(fm[hi, near], x_u)
            kc, ks = twice(ksp[lo, at]), twice(ksp[hi, at] * turn)
            xsp[u, lo] = xc.astype(bf16)
            xsp[u, hi] = x_s.astype(bf16)
            zs[lo] = (kc * xc - ks * x_s).astype(bf16)
            zs[hi] = (kc * x_s + ks * xc).astype(bf16)
            return 0

        lax.fori_loop(0, 4, first_rows, 0)
        if u == 0:
            loads[2].wait()
        inverse_to(3, u, r1s, xs)

    for k in range(2):
        by, on = beside[k], (s, beside[1 - k])
        moves["n", k].wait()
        part = nt.at[by, 2 * k : 2 * k + 2]
        moves["n", 2 + k] = remote(part, part, b_sem, (0, 2 + k), on)
    for k in range(2):
        by, on = beside[k], (s, beside[1 - k])
        moves["c", k].wait()
        part = cot.at[by, 128 * k : 128 * k + 128]
        moves["c", 2 + k] = remote(part, part, b_sem, (1, 2 + k), on)

    wait_tiles(2)
    wait_tiles(1)
    sent_tiles(2)
    for u in range(2):
        at = slice(u * 128, u * 128 + 128)
        y_near = yo[:, u].reshape(512, 256)
        y_far = yx[:, u].reshape(512, 256)

        def second_rows(i, _):
            lo, hi = lanes(i * 256, 256), lanes(1024 + i * 256, 256)
            nc, n_s = mm(fm[lo, near], y_near), mm(fm[hi, near], y_near)
            yc = nc + mm(fm[lo, far_half], y_far)
            y_s = n_s + mm(fm[hi, far_half], y_far)
            kc, ks = twice(ksp[lo, at]), twice(ksp[hi, at] * turn)
            zs[lo] = (kc * yc + ks * y_s).astype(bf16)
            zs[hi] = (kc * y_s - ks * yc).astype(bf16)
            pc = jnp.where(side == 0, nc, yc)
            p_s = jnp.where(side == 0, n_s, y_s)
            xc, x_s = xsp[u, lo].astype(f32), xsp[u, hi].astype(f32)
            ec, e_s = xc * pc + x_s * p_s, (xc * p_s - x_s * pc) * turn
            es[lo, at] = (ec[:, :128] + ec[:, 128:]).astype(bf16)
            es[hi, at] = (e_s[:, :128] + e_s[:, 128:]).astype(bf16)
            return 0

        lax.fori_loop(0, 4, second_rows, 0)
        inverse_to(5, u, a2, yo)

    def product_moves(half, p):
        return remote(
            pts.at[:, half, (b + p) % 4],
            pt.at[b, half],
            b_sem,
            (2 + half, p),
            batch_peer(p),
            start=False,
        )

    def mixed_moves(g, p):
        return remote(
            dms.at[g, (b + p) % 4], dm.at[g, b], b_sem, (4 + g, p), batch_peer(p), start=False
        )

    def edges_of(groups, index):
        return remote(
            dsx.at[groups, :, 0:8],
            dsx.at[groups, :, 128:136],
            halo_sem,
            (index,),
            ((s + 7) % 8, b),
            start=False,
        )

    def send_edges(groups, index):
        @pl.when(s > 0)
        def _():
            edges_of(groups, index).start()

    def wait_edges(groups, index):
        @pl.when(s == 7)
        def _():
            for g in range(groups.start, groups.stop):
                for j in range(8):
                    dsx[g, j, 128:136] = jnp.zeros((8, 256), f32)

        @pl.when(s < 7)
        def _():
            edges_of(groups, index).wait_recv()

    def column_sum(v):
        v = jnp.sum(v, axis=0, keepdims=True)
        return v[:, :128] + v[:, 128:]

    def short_sums(groups):
        def one_tile(j, _):
            for g in groups:
                wide = lanes(g * 1024 + j * 128, 128)
                value = dsx[g, j, 0:128]
                for k in range(3):
                    sa[1 + k : 2 + k, wide] = column_sum(value * mx[g, j, 8 - k : 136 - k])
                sa[4:5, wide] = column_sum(value)
            return 0

        lax.fori_loop(0, 8, one_tile, 0)

    def mixed_tile(g):
        def one_tile(j, _):
            q, cols = j // 2, lanes((j % 2) * 128, 128)
            wide = lanes(g * 1024 + j * 128, 128)
            taps = sw_ref[:, wide]
            value = (
                twice(taps[0:1]) * dsx[g, j, 0:128]
                + twice(taps[1:2]) * dsx[g, j, 1:129]
                + twice(taps[2:3]) * dsx[g, j, 2:130]
            ).astype(bf16)
            dms[g, q, 0:128, cols] = value[:, :128]
            dms[g, q, 128:256, cols] = value[:, 128:]
            sa[0:1, wide] = column_sum(value.astype(f32))
            return 0

        lax.fori_loop(0, 8, one_tile, 0)
        dm[g, b] = dms[g, b]

    def send_mixed(g):
        for p in (1, 2, 3):
            mixed_moves(g, p).start()

    def send_product():
        for half in range(2):
            for p in (1, 2, 3):
                product_moves(half, p).start()

    store_out = pltpu.make_async_copy(outv, out_ref, load_sem.at[3])

    def with_summed(back, early):
        def product_tile(j, _):
            value = back[j].astype(f32)
            made = (value * oiv[0, j]).astype(bf16)
            cols = lanes(j * 128, 128)
            product[0:128, cols] = made[:, :128]
            product[128:256, cols] = made[:, 128:]
            dsx[0, j, 0:128] = dpr[j].astype(f32) * value
            return 0

        lax.fori_loop(0, 8, product_tile, 0)
        send_edges(slice(0, 1), 1)
        pts[...] = product[...].T.reshape(4, 2, 4, 32, 256)
        send_product()
        for half in range(2):
            pt[b, half] = pts[:, half, b]
        short_sums((0,))

        @pl.when(s != 3)
        def _():
            wait_edges(slice(0, 1), 1)
            mixed_tile(0)
            if early:
                send_mixed(0)

        def out_cols(i, _):
            cols = lanes(i * 256, 256)
            r = mm(product[...], w_out[:, cols]) + bout_ref[:, cols]
            for q in range(2):
                rows = slice(q * 128, q * 128 + 128)
                outv[q, :, cols] = (tok_ref[q, :, cols].astype(f32) + r[rows]).astype(bf16)
            return 0

        lax.fori_loop(0, 4, out_cols, 0)
        store_out.start()

    def with_gated(back, early):
        def gate_tile(j, _):
            value = back[j].astype(f32)
            dsx[1, j, 0:128] = value * oiv[2, j]
            dsx[2, j, 0:128] = value * oiv[1, j]
            return 0

        lax.fori_loop(0, 8, gate_tile, 0)
        send_edges(slice(1, 3), 2)
        short_sums((1, 2))
        wait_edges(slice(1, 3), 2)
        mixed_tile(1)
        send_mixed(1)
        mixed_tile(2)
        if early:
            send_mixed(2)

        @pl.when(s == 3)
        def _():
            wait_edges(slice(0, 1), 1)
            mixed_tile(0)
            send_mixed(0)

    wait_tiles(3)
    wait_tiles(4)

    @pl.when(side == 0)
    def _():
        with_summed(r1, True)

    @pl.when(side == 1)
    def _():
        with_gated(r1, True)

    wait_tiles(5)
    wait_tiles(6)

    @pl.when(side == 0)
    def _():
        with_gated(r2, False)

    @pl.when(side == 1)
    def _():
        with_summed(r2, False)

    def normed_cols(i, _):
        at = lanes(i * 256, 256)
        total = jnp.zeros((256, 256), f32)
        for g in range(3):
            for q in range(4):
                c = g * 1024 + q * 256
                total += mm(dms[g, q], w_in[at, c : c + 256], NT)
        for q in range(2):
            gtokv[q, :, at] = total[q * 128 : q * 128 + 128]
        return 0

    lax.fori_loop(0, 4, normed_cols, 0)

    def token_rows(i, sums):
        q, r = i // 4, lanes((i % 4) * 32, 32)
        rows = lanes(i * 32, 32)
        d, w = gtokv[q, r], white[rows]
        dw = d * w
        d_white = d * gain
        grad = cot_ref[rows].astype(f32) + istd[rows, 0:1] * (
            d_white
            - jnp.mean(d_white, axis=-1, keepdims=True)
            - w * jnp.mean(d_white * w, axis=-1, keepdims=True)
        )
        gtokv[q, r] = grad
        return (
            sums[0] + jnp.sum(dw, axis=0, keepdims=True),
            sums[1] + jnp.sum(d, axis=0, keepdims=True),
        )

    zero = jnp.zeros((1, 1024), f32)
    sums = lax.fori_loop(0, 8, token_rows, (zero, zero))
    store_tok = pltpu.make_async_copy(gtokv, gtok_ref, load_sem.at[4])
    store_tok.start()
    sa[5:6, 0:1024] = sums[0]
    sa[5:6, 1024:2048] = sums[1]

    def part_out(half):
        total = jnp.zeros((128, 1024), f32)
        for i in range(4):
            total += mm(pt[i, half].reshape(128, 256), cot[i])
        return total

    def part_in(g, half):
        total = jnp.zeros((512, 256), f32)
        for i in range(4):
            total += mm(nt[i, :, half].reshape(512, 256), dm[g, i])
        return total

    def shard_of(g, z):
        return lanes(g * 512 + z * 128, 128)

    beside_z, across_z = (pair * 2 + core, b), (cross * 2 + core, b)

    def core_move(g):
        return remote(core_send.at[g], core_recv.at[g], c_sem, (g, 0), other, start=False)

    def zed_move(g, k):
        to = across_z if k == 2 else beside_z
        src = core_send.at[g, shards[k]]
        return remote(src, z_recv.at[g, k], zed_sem, (g, k), to, start=False)

    def core_move_o():
        return remote(core_send_o, core_recv_o, c_sem, (3, 0), other, start=False)

    def zed_move_o(k):
        to = across_z if k == 2 else beside_z
        src = core_send_o.at[32 * k : 32 * k + 32]
        return remote(src, z_recv_o.at[k], zed_sem, (3, k), to, start=False)

    def core_half_o():
        core_send_o[...] = part_out(1 - core).astype(bf16)
        core_move_o().start()

    def core_half(g):
        core_send[g] = part_in(g, 1 - core).astype(bf16).reshape(4, 128, 256)
        core_move(g).start()

    def zed_half_o():
        total = part_out(core)
        core_move_o().wait()
        own_o[...] = (total + core_recv_o[...].astype(f32)).reshape(4, 32, 1024)
        for k in range(2):
            core_send_o[32 * k : 32 * k + 32] = own_o[shards[k]].astype(bf16)
            zed_move_o(k).start()

    def zed_half(g):
        total = part_in(g, core)
        core_move(g).wait()
        ksp[512 * g : 512 * g + 512] = total + core_recv[g].astype(f32).reshape(512, 256)
        for k in range(2):
            core_send[g, shards[k]] = ksp[shard_of(g, shards[k])].astype(bf16)
            zed_move(g, k).start()

    def cross_half_o():
        zed_move_o(0).wait()
        core_send_o[64:96] = (own_o[cross] + z_recv_o[0].astype(f32)).astype(bf16)
        zed_move_o(2).start()

    def cross_half(g):
        zed_move(g, 0).wait()
        total = ksp[shard_of(g, cross)] + z_recv[g, 0].astype(f32)
        core_send[g, cross] = total.astype(bf16)
        zed_move(g, 2).start()

    def last_half(g):
        zed_move(g, 1).wait()
        zed_move(g, 2).wait()
        total = ksp[shard_of(g, zed)] + z_recv[g, 1].astype(f32) + z_recv[g, 2].astype(f32)
        last_send[g] = total.astype(bf16).reshape(4, 32, 256)
        for p in (1, 2, 3):
            moves["l", g, p] = remote(
                last_send.at[g, (b + p) % 4], last_recv.at[g, b], l_sem, (g, p), batch_peer(p)
            )
        last_recv[g, b] = last_send[g, b]

    def half_at(k):
        return lanes(k * 1536, 1536)

    @pl.when(side == 0)
    def _():
        send_mixed(2)

    @pl.when(side == 1)
    def _():
        send_mixed(0)

    def kernel_rows(i, _):
        rows = lanes(i * 256, 256)
        window[rows] = mm(ft[rows], es[...]) * (1.0 / 1024) * window[rows]
        return 0

    lax.fori_loop(0, 4, kernel_rows, 0)
    sc[...] = jnp.zeros(sc.shape, f32)
    direct = []
    for u in range(2):
        both = xs[:, u].astype(f32) * yo[:, u].astype(f32)
        direct.append(column_sum(both.reshape(512, 256)))
    direct = jnp.broadcast_to(jnp.concatenate(direct, axis=1), (64, 256)).T

    def low(v):
        return v.astype(bf16)

    d_shaped = low(window[...])
    sb[...] = jnp.concatenate([mm(d_shaped, low(second[:, 0:64]), TN), direct], axis=1)
    d_two = mm(d_shaped, low(w3_ref[:, mine]), NT) * second[:, 64:128]
    sc[0:64, 64:128] = mm(low(first[:, 0:64]), low(d_two), TN)
    sc[40:41, 0:64] = jnp.sum(d_two, axis=0, keepdims=True)
    d_one = mm(low(d_two), low(w2_ref[...]), NT) * first[:, 64:128]
    sc[0:33, 0:64] = mm(low(pos_ref[...]), low(d_one), TN)
    sc[41:42, 0:64] = jnp.sum(d_one, axis=0, keepdims=True)
    def rows_at(k):
        return pl.ds(pl.multiple_of(k * 32, 32), 32)

    def small_remote(src, dst, index, peer):
        return remote(src, dst, v_sem, (index,), peer)

    smalls = [
        small_remote(sa.at[:, half_at(1 - core)], sr.at[0], 0, other),
        small_remote(sc.at[rows_at(1 - core)], st.at[0], 1, other),
    ]
    for k in (2, 3):
        moves["n", k].wait()
        moves["c", k].wait()

    def arrived(g):
        for p in (1, 2, 3):
            mixed_moves(g, p).wait()

    def arrived_o():
        for p in (1, 2, 3):
            product_moves(0, p).wait()
            product_moves(1, p).wait()

    @pl.when(side == 0)
    def _():
        arrived_o()
        core_half_o()
        arrived(0)
        core_half(0)
        zed_half_o()
        zed_half(0)

    @pl.when(side == 1)
    def _():
        arrived(1)
        core_half(1)
        arrived(2)
        core_half(2)
        zed_half(1)
        zed_half(2)

    for move in smalls:
        move.wait()
    def fold(v):
        return jnp.concatenate([v[:, :768], v[:, 768:]], axis=0).astype(bf16)

    def total_of(array, first):
        return sum(array[first + i].astype(f32) for i in range(1, 4)) + array[first].astype(f32)

    vb[b] = fold(sa[:, half_at(core)] + sr[0])
    sq[b] = (sc[rows_at(core)] + st[0]).astype(bf16)
    sp[4:12] = sb[...].astype(bf16).reshape(8, 32, 128)
    for u in range(2):
        sp[2 * b + u + 12] = sp[4 + 4 * u + b]
    smalls = []
    for p in (1, 2, 3):
        smalls += [
            small_remote(vb.at[b], vb.at[b], 1 + p, batch_peer(p)),
            small_remote(sq.at[b], sq.at[b], 4 + p, batch_peer(p)),
            small_remote(sp.at[4 + (b + p) % 4], sp.at[12 + 2 * b], 7 + p, batch_peer(p)),
            small_remote(sp.at[8 + (b + p) % 4], sp.at[13 + 2 * b], 20 + p, batch_peer(p)),
        ]

    @pl.when(side == 0)
    def _():
        arrived(1)
        core_half(1)
        cross_half_o()
        cross_half(0)
        zed_half(1)

    @pl.when(side == 1)
    def _():
        arrived_o()
        core_half_o()
        cross_half(1)
        cross_half(2)
        zed_half_o()

    for move in smalls:
        move.wait()
    vb[4 + zed] = total_of(vb, 0).astype(bf16)
    sq[4 + zed] = total_of(sq, 0).astype(bf16)
    for u in range(2):
        part = sum(sp[12 + 2 * i + u].astype(f32) for i in range(4))
        sb[32 * u : 32 * u + 32] = part
        sp[u] = part.astype(bf16)
    smalls = [small_remote(sp.at[0:2], sp.at[2:4], 17, across_z)]
    for p in (1, 2, 3):
        smalls += [
            small_remote(vb.at[4 + zed], vb.at[4 + zed], 10 + p, zed_peer(p)),
            small_remote(sq.at[4 + zed], sq.at[4 + zed], 13 + p, zed_peer(p)),
        ]
    @pl.when(side == 0)
    def _():
        arrived(2)
        core_half(2)
        cross_half(1)
        zed_half(2)
        cross_half(2)

    @pl.when(side == 1)
    def _():
        arrived(0)
        core_half(0)
        cross_half_o()
        zed_half(0)
        cross_half(0)

    for move in smalls:
        move.wait()
    for u in range(2):
        sb[32 * u : 32 * u + 32] = sb[32 * u : 32 * u + 32] + sp[2 + u].astype(f32)
    folded = total_of(vb, 4)
    sf[...] = jnp.concatenate([folded[:8], folded[8:]], axis=1)
    sh[...] = total_of(sq, 4)
    smalls = [
        small_remote(sf, sr.at[1], 18, other),
        small_remote(sh, st.at[1], 19, other),
    ]
    owner = quarter * 2 + side

    def give():
        return remote(
            sb.at[lanes(side * 32, 32)], sg, v_sem, (24,), (owner, b), start=False
        )

    @pl.when(owner != s)
    def _():
        give().start()

    @pl.when(owner == s)
    def _():
        sg[...] = sb[lanes(side * 32, 32)]

    last_half(0)
    zed_move_o(1).wait()
    zed_move_o(2).wait()
    gwout_ref[...] = own_o[zed] + z_recv_o[1].astype(f32) + z_recv_o[2].astype(f32)
    last_half(1)
    last_half(2)
    for move in smalls:
        move.wait()
    oa_ref[:, half_at(core)] = sf[...]
    oa_ref[:, half_at(1 - core)] = sr[1]
    oc_ref[rows_at(core)] = sh[...]
    oc_ref[rows_at(1 - core)] = st[1]

    @pl.when(owner != s)
    def _():
        give().wait()

    ob_ref[...] = sg[...]
    for g in range(3):
        for p in (1, 2, 3):
            moves["l", g, p].wait()
        for i in range(4):
            c = g * 1024 + i * 256
            gwin_ref[:, c : c + 256] = last_recv[g, i].astype(f32)
    store_out.wait()
    store_tok.wait()
    for kind in (0, 1, 3, 4, 5, 6):
        sent_tiles(kind)

    @pl.when(s < 7)
    def _():
        edge.wait_send()

    @pl.when(s > 0)
    def _():
        edges_of(slice(0, 1), 1).wait_send()
        edges_of(slice(1, 3), 2).wait_send()


def whole(args, positions, matrix):
    vmem, anywhere = (pl.BlockSpec(memory_space=m) for m in (pltpu.VMEM, pl.ANY))
    dma = pltpu.SemaphoreType.DMA
    specs = [vmem] * 20
    for i in (4, 15, 18, 19):
        specs[i] = anywhere
    shape = jax.ShapeDtypeStruct

    def v(dtype, *dims):
        return pltpu.VMEM(dims, dtype)

    return pl.pallas_call(
        whole_kernel,
        out_shape=(
            shape((2, 128, 1024), bf16),
            shape((2, 128, 1024), f32),
            shape((32, 3072), f32),
            shape((32, 1024), f32),
            shape((8, 3072), f32),
            shape((32, 128), f32),
            shape((64, 128), f32),
        ),
        in_specs=specs,
        out_specs=(anywhere,) * 2 + (vmem,) * 5,
        scratch_shapes=[
            v(bf16, 1024, 3072),
            v(bf16, 1024, 1024),
            v(bf16, 2048, 1024),
            v(bf16, 1024, 2048),
            v(bf16, 2, 16, 1024),
            v(f32, 256, 1024),
            v(f32, 256, 128),
            v(bf16, 288, 1024),
            v(f32, 3, 8, 136, 256),
            v(f32, 3, 8, 128, 256),
            v(bf16, 8, 128, 256),
            v(bf16, 4, 2, 128, 256),
            v(bf16, 4, 2, 128, 256),
            v(bf16, 4, 2, 128, 256),
            v(bf16, 4, 2, 128, 256),
            v(bf16, 4, 2, 128, 256),
            v(bf16, 4, 2, 128, 256),
            v(bf16, 8, 128, 256),
            v(bf16, 8, 128, 256),
            v(f32, 1024, 128),
            v(f32, 1024, 128),
            v(f32, 1024, 256),
            v(f32, 2048, 256),
            v(bf16, 2, 2048, 256),
            v(bf16, 2048, 256),
            v(bf16, 2048, 256),
            v(bf16, 256, 1024),
            v(bf16, 4, 2, 4, 32, 256),
            v(f32, 3, 8, 136, 256),
            v(bf16, 3, 4, 256, 256),
            v(bf16, 4, 4, 2, 128, 256),
            v(bf16, 4, 2, 4, 32, 256),
            v(bf16, 3, 4, 256, 256),
            v(bf16, 4, 256, 1024),
            v(bf16, 3, 4, 128, 256),
            v(bf16, 3, 4, 128, 256),
            v(bf16, 128, 1024),
            v(bf16, 128, 1024),
            v(f32, 4, 32, 1024),
            v(bf16, 2, 128, 1024),
            v(f32, 2, 128, 1024),
            v(bf16, 3, 3, 128, 256),
            v(bf16, 3, 32, 1024),
            v(bf16, 3, 4, 32, 256),
            v(bf16, 3, 4, 32, 256),
            v(f32, 8, 3072),
            v(f32, 2, 8, 1536),
            v(f32, 8, 1536),
            v(f32, 256, 128),
            v(bf16, 20, 32, 128),
            v(bf16, 8, 16, 768),
            v(f32, 32, 128),
            v(f32, 64, 128),
            v(bf16, 8, 32, 128),
            v(f32, 2, 32, 128),
            v(f32, 32, 128),
            dma((5,)),
            dma((3, 4)),
            dma((2, 25)),
            dma((2, 3)),
            dma((2, 7, 4)),
            dma((2, 7, 4)),
            dma((2, 4, 4)),
            dma((2, 4, 4)),
            dma((2, 3, 4)),
        ],
        compiler_params=pltpu.CompilerParams(
            collective_id=0, has_side_effects=True, vmem_limit_bytes=63 * 1024 * 1024
        ),
    )(*args, positions, matrix, np.ascontiguousarray(matrix.T))


def settle_kernel(
    out_ref,
    gtok_ref,
    gwin_ref,
    gwout_ref,
    sa_ref,
    sb_ref,
    sc_ref,
    out,
    gtok,
    ln_gain,
    ln_bias,
    gwin,
    b_in,
    short_w,
    short_b,
    w_one,
    b_one,
    w_two,
    b_two,
    w_three,
    filt,
    gwout,
    b_out,
    sems,
):
    copies = [
        pltpu.make_async_copy(src, dst, sems.at[i])
        for i, (src, dst) in enumerate(
            ((out_ref, out), (gtok_ref, gtok), (gwin_ref, gwin), (gwout_ref, gwout))
        )
    ]
    for copy in copies:
        copy.start()
    b = lax.axis_index("batch")
    place = lax.axis_index("seq") * 4 + b
    sa = sa_ref[...]
    wide = pltpu.roll(sa, (32 - place) * 96, 1)
    b_in[...] = wide[0:1, :96]
    short_w[...] = wide[1:4, :96]
    short_b[...] = wide[4:5, :96]
    thin = pltpu.roll(sa, (96 - place) * 32, 1)
    ln_gain[...] = thin[5:6, 0:32]
    ln_bias[...] = thin[5:6, 1024:1056]
    b_out[...] = thin[5:6, 2048:2080]
    w_three[...] = sb_ref[:, 0:64]
    filt[...] = sb_ref[...].T[64:65, 0:32]
    w_one[...] = sc_ref[0:33, 0:64]
    w_two[...] = sc_ref[0:64, 64:128]
    b_two[...] = sc_ref[40:41, 0:64]
    b_one[...] = sc_ref[41:42, 0:64]
    for copy in copies:
        copy.wait()


def settle(parts):
    vmem, anywhere = (pl.BlockSpec(memory_space=m) for m in (pltpu.VMEM, pl.ANY))
    sizes = (
        (2, 128, 1024),
        (2, 128, 1024),
        (1, 32),
        (1, 32),
        (32, 3072),
        (1, 96),
        (3, 96),
        (1, 96),
        (33, 64),
        (1, 64),
        (64, 64),
        (1, 64),
        (32, 64),
        (1, 32),
        (32, 1024),
        (1, 32),
    )
    flat = (2, 3, 5, 7, 9, 11, 13, 15)
    outs = pl.pallas_call(
        settle_kernel,
        out_shape=tuple(
            jax.ShapeDtypeStruct(size, f32 if i else bf16) for i, size in enumerate(sizes)
        ),
        in_specs=[anywhere] * 4 + [vmem] * 3,
        out_specs=(vmem,) * 16,
        scratch_shapes=[pltpu.SemaphoreType.DMA((4,))],
    )(*parts)
    return tuple(
        o.reshape(-1) if i in flat else o.T if i == 12 else o for i, o in enumerate(outs)
    )


def local_small(*args):
    cotangent = args[1]
    vectors = {2, 3, 5, 7, 9, 11, 13, 14, 16}
    given = [a.reshape(1, -1) if i in vectors else a for i, a in enumerate(args)]
    given[1] = cotangent.reshape(256, 1024)
    return settle(whole(given, position_features(1024, args[8].shape[0]), dft_matrix(1024)))


def solution(mesh):
    tokens_spec = P("batch", "seq", None)
    both = ("seq", "batch")
    in_specs = (tokens_spec, tokens_spec) + (P(),) * 15
    out_specs = (
        tokens_spec,
        tokens_spec,
        P(both),
        P(both),
        P(both, None),
        P(both),
        P(None, both),
        P(both),
        P(),
        P(),
        P(),
        P(),
        P(None, both),
        P(both),
        P(both, None),
        P(both),
    )

    def per_device(*args):
        tokens, w_one = args[0], args[8]
        sizes = (mesh.shape["seq"], mesh.shape["batch"]) + tokens.shape + w_one.shape
        fits = sizes == (8, 4, 2, 128, 1024, 33, 64)
        return (local_small if fits else local)(*args)

    return jax.shard_map(per_device, mesh=mesh, in_specs=in_specs, out_specs=out_specs, check_vma=False)
```

```python
import jax
import jax.numpy as jnp
import numpy as np
from jax import lax
from jax.experimental import pallas as pl
from jax.experimental.pallas import tpu as pltpu
from jax.sharding import PartitionSpec as P

highest = lax.Precision.HIGHEST
epsilon = 1e-05
f32, bf16 = jnp.float32, jnp.bfloat16


def dft_matrix(length):
    turns = ((2 * np.arange(length)[:, None] + 1) * np.arange(length)[None, :]) % (4 * length)
    phases = turns * (np.pi / (2 * length))
    return np.concatenate([np.cos(phases), np.sin(phases)], axis=0).astype(bf16)


def position_features(length, features):
    step_axis = np.arange(length, dtype=np.float64)
    band_count = (features - 1) // 2
    band_rates = 0.0001 + np.arange(band_count) * (band_count - 1 - 0.0001) / (band_count - 1)
    phases = 2.0 * np.pi / length * step_axis[:, None] * band_rates[None, :]
    return np.concatenate(
        [(step_axis / length)[:, None], np.cos(phases), -np.sin(phases)], axis=1
    ).astype(np.float32)


def filter_shape(positions, w_one, b_one, w_two, b_two, w_three, decay_rates):
    first_layer = jnp.sin(jnp.dot(positions, w_one, precision=highest) + b_one)
    second_layer = jnp.sin(jnp.dot(first_layer, w_two, precision=highest) + b_two)
    shaped = jnp.dot(second_layer, w_three, precision=highest)
    length = positions.shape[0]
    fraction = jnp.arange(length).astype(f32) / length
    return shaped * jnp.exp(-fraction[:, None] * decay_rates[None, :])


def shifted(value, axis, steps):
    count = lax.axis_size(axis)
    first, last = (max(0, -steps), min(count, count - steps))
    return lax.ppermute(value, axis, [(source, source + steps) for source in range(first, last)])


def reduce_scatter(value, dtype):
    out = lax.all_to_all(value.astype(dtype), "batch", split_axis=1, concat_axis=1, tiled=True)
    out = jnp.sum(out.astype(f32), axis=1)
    out = lax.all_to_all(out.astype(dtype), "seq", split_axis=0, concat_axis=0, tiled=True)
    return jnp.sum(out.astype(f32), axis=0)


def local(
    tokens,
    cotangent,
    ln_gain,
    ln_bias,
    w_in,
    b_in,
    short_w,
    short_b,
    w_one,
    b_one,
    w_two,
    b_two,
    w_three,
    decay_rates,
    filt_bias,
    w_out,
    b_out,
):
    seq_count, block_len, model_width = tokens.shape
    seq_devices = lax.axis_size("seq")
    batch_devices = lax.axis_size("batch")
    devices = seq_devices * batch_devices
    length = block_len * seq_devices
    channels = model_width // seq_devices
    col_start = lax.axis_index("seq") * channels
    inputs = tokens.astype(f32)
    average = jnp.mean(inputs, axis=-1, keepdims=True)
    centered = inputs - average
    inv_std = lax.rsqrt(jnp.mean(centered * centered, axis=-1, keepdims=True) + epsilon)
    whitened = centered * inv_std
    normed = (whitened * ln_gain + ln_bias).astype(bf16)
    mixed = jnp.einsum("btd,de->bte", normed, w_in, preferred_element_type=f32) + b_in
    prev_rows = shifted(mixed[:, block_len - 2 :], "seq", 1)
    padded = jnp.concatenate([prev_rows, mixed], axis=1)
    delay_one = padded[:, 1:-1]
    delay_two = padded[:, :-2]
    short_out = short_w[0] * mixed + short_w[1] * delay_one + short_w[2] * delay_two + short_b
    outer_gate = short_out[..., :model_width]
    inner_gate = short_out[..., model_width : 2 * model_width]
    values = short_out[..., 2 * model_width :]
    gated = (values * inner_gate).astype(bf16)
    d_product = jnp.einsum(
        "bte,de->btd", cotangent, w_out, preferred_element_type=f32
    ).astype(bf16)
    d_prod_f = d_product.astype(f32)
    d_summed = (d_prod_f * outer_gate).astype(bf16)

    def to_channels(value):
        return lax.all_to_all(value, "seq", split_axis=2, concat_axis=1, tiled=True)

    def to_tokens(value):
        return lax.all_to_all(value, "seq", split_axis=1, concat_axis=2, tiled=True)

    gated_ch = to_channels(gated)
    d_ch = to_channels(d_summed)
    positions = jnp.asarray(position_features(length, w_one.shape[0]))
    w_three_part = lax.dynamic_slice_in_dim(w_three, col_start, channels, 1)
    decay_part = lax.dynamic_slice_in_dim(decay_rates, col_start, channels, 0)
    bias_part = lax.dynamic_slice_in_dim(filt_bias, col_start, channels, 0)

    def kernel_of(first_w, first_b, second_w, second_b, third_w):
        return filter_shape(positions, first_w, first_b, second_w, second_b, third_w, decay_part)

    kernel_full, kernel_pull = jax.vjp(kernel_of, w_one, b_one, w_two, b_two, w_three_part)
    matrix = jnp.asarray(dft_matrix(length))

    def spectrum(value):
        return jnp.einsum("kt,btc->bkc", matrix, value, preferred_element_type=f32)

    def inverse(cosines, sines):
        both = jnp.concatenate([cosines, sines], axis=1).astype(bf16)
        return jnp.einsum("kt,bkc->btc", matrix, both, preferred_element_type=f32) * (1.0 / length)

    k_both = spectrum(kernel_full.astype(bf16)[None])
    g_both = spectrum(gated_ch)
    d_both = spectrum(d_ch)
    k_c, k_s = k_both[:, :length], k_both[:, length:]
    g_c, g_s = g_both[:, :length], g_both[:, length:]
    d_c, d_s = d_both[:, :length], d_both[:, length:]
    long_out = inverse(g_c * k_c - g_s * k_s, g_c * k_s + g_s * k_c)
    gated_float = gated_ch.astype(f32)
    d_ch_float = d_ch.astype(f32)
    summed_ch = (long_out + bias_part * gated_float).astype(bf16)
    summed = to_tokens(summed_ch).astype(f32)
    grad_in = inverse(k_c * d_c + k_s * d_s, k_c * d_s - k_s * d_c) + bias_part * d_ch_float
    d_gated = to_tokens(grad_in.astype(bf16)).astype(f32)
    d_kernel = inverse(
        jnp.sum(g_c * d_c + g_s * d_s, axis=0, keepdims=True),
        jnp.sum(g_c * d_s - g_s * d_c, axis=0, keepdims=True),
    )[0]
    g_bias_part = jnp.sum(d_ch_float * gated_float, axis=(0, 1))
    g_w_one, g_b_one, g_w_two, g_b_two, g_w_three_part = kernel_pull(d_kernel)

    product = (summed * outer_gate).astype(bf16)
    result = jnp.einsum("btd,de->bte", product, w_out, preferred_element_type=f32) + b_out
    block_out = (inputs + result).astype(bf16)
    grad_out = cotangent.astype(f32)
    g_w_out = jnp.einsum("btd,bte->de", product, cotangent, preferred_element_type=f32)
    g_b_out = jnp.sum(grad_out, axis=(0, 1))
    d_outer = d_prod_f * summed
    d_short = jnp.concatenate([d_outer, d_gated * values, d_gated * inner_gate], axis=-1)
    g_short_w = jnp.stack(
        [
            jnp.sum(d_short * mixed, axis=(0, 1)),
            jnp.sum(d_short * delay_one, axis=(0, 1)),
            jnp.sum(d_short * delay_two, axis=(0, 1)),
        ]
    )
    g_short_b = jnp.sum(d_short, axis=(0, 1))
    next_rows = shifted(d_short[:, :2], "seq", -1)
    extended = jnp.concatenate([d_short, next_rows], axis=1)
    d_mixed = (
        short_w[0] * extended[:, :block_len]
        + short_w[1] * extended[:, 1 : block_len + 1]
        + short_w[2] * extended[:, 2:]
    ).astype(bf16)
    g_w_in = jnp.einsum("btd,bte->de", normed, d_mixed, preferred_element_type=f32)
    g_b_in = jnp.sum(d_mixed.astype(f32), axis=(0, 1))
    d_normed = jnp.einsum("bte,de->btd", d_mixed, w_in, preferred_element_type=f32)
    g_ln_gain = jnp.sum(d_normed * whitened, axis=(0, 1))
    g_ln_bias = jnp.sum(d_normed, axis=(0, 1))
    d_white = d_normed * ln_gain
    grad_tokens = grad_out + inv_std * (
        d_white
        - jnp.mean(d_white, axis=-1, keepdims=True)
        - whitened * jnp.mean(d_white * whitened, axis=-1, keepdims=True)
    )
    rows = model_width // devices
    big = jnp.concatenate([g_w_in, g_w_out], axis=1)
    big = reduce_scatter(big.reshape(seq_devices, batch_devices, rows, -1), bf16)
    out_w_in, out_w_out = big[:, : 3 * model_width], big[:, 3 * model_width :]
    g_w_three = lax.dynamic_update_slice_in_dim(
        jnp.zeros(w_three.shape, f32), g_w_three_part, col_start, 1
    )
    g_filt_bias = lax.dynamic_update_slice_in_dim(
        jnp.zeros(filt_bias.shape, f32), g_bias_part, col_start, 0
    )
    vectors = jnp.concatenate(
        [
            g_ln_gain[None],
            g_ln_bias[None],
            g_b_out[None],
            g_filt_bias[None],
            g_w_three,
        ],
        axis=0,
    )
    vectors = jnp.transpose(vectors.reshape(-1, devices, rows), (1, 0, 2)).reshape(devices, -1)
    wides = jnp.concatenate([g_b_in[None], g_short_w, g_short_b[None]], axis=0)
    wides = jnp.transpose(wides.reshape(-1, devices, 3 * rows), (1, 0, 2)).reshape(devices, -1)
    net = jnp.concatenate([v.reshape(-1) for v in (g_w_one, g_b_one, g_w_two, g_b_two)])
    net_size = net.shape[0]
    net_part = -(-net_size // devices)
    net = jnp.pad(net, (0, net_part * devices - net_size)).reshape(devices, net_part)
    small = jnp.concatenate([vectors, wides, net], axis=1)
    small = reduce_scatter(small.reshape(seq_devices, batch_devices, -1), f32)
    hidden = w_two.shape[0]
    cut = rows * (4 + hidden)
    vectors = small[:cut].reshape(4 + hidden, rows)
    wides = small[cut : cut + 15 * rows].reshape(5, 3 * rows)
    net = lax.all_gather(small[cut + 15 * rows :], ("seq", "batch"), tiled=True)
    features = w_one.shape[0]
    edges = [features * hidden, (features + 1) * hidden, (features + 1 + hidden) * hidden]
    return (
        block_out,
        grad_tokens,
        vectors[0],
        vectors[1],
        out_w_in,
        wides[0],
        wides[1:4],
        wides[4],
        net[: edges[0]].reshape(features, hidden),
        net[edges[0] : edges[1]],
        net[edges[1] : edges[2]].reshape(hidden, hidden),
        net[edges[2] : net_size],
        vectors[4:],
        vectors[3],
        out_w_out,
        vectors[2],
    )


MESH = pl.DeviceIdType.MESH
HALF_TURN = (1.5703125, 4.837512969970703125e-4, 7.549789948768648e-8)


def sin_cos(x):
    turns = jnp.floor(x * 0.6366197723675814 + 0.5)
    r = ((x - turns * HALF_TURN[0]) - turns * HALF_TURN[1]) - turns * HALF_TURN[2]
    q = turns.astype(jnp.int32)
    r2 = r * r
    sine = r + r * r2 * (
        -1.6666654611e-1 + r2 * (8.3321608736e-3 + r2 * -1.9515295891e-4)
    )
    cosine = 1.0 - 0.5 * r2 + r2 * r2 * (
        4.166664568298827e-2 + r2 * (-1.388731625493765e-3 + r2 * 2.443315711809948e-5)
    )
    odd = (q & 1) == 1
    s_abs, c_abs = jnp.where(odd, cosine, sine), jnp.where(odd, sine, cosine)
    s_neg, c_neg = (q & 2) == 2, ((q + 1) & 2) == 2
    return jnp.where(s_neg, -s_abs, s_abs), jnp.where(c_neg, -c_abs, c_abs)


def mm(a, b, dims=((1,), (0,))):
    return lax.dot_general(a, b, (dims, ((), ())), preferred_element_type=f32)


def mm_full(a, b, dims=((1,), (0,))):
    return lax.dot_general(
        a, b, (dims, ((), ())), precision=highest, preferred_element_type=f32
    )


def twice(v):
    return jnp.concatenate([v, v], axis=1)


def lanes(start, size):
    return pl.ds(pl.multiple_of(start, size), size)


NT, TN = ((1,), (1,)), ((0,), (0,))


def whole_kernel(
    tok_ref,
    cot_ref,
    gain_ref,
    beta_ref,
    win_ref,
    bin_ref,
    sw_ref,
    sb_ref,
    w1_ref,
    b1_ref,
    w2_ref,
    b2_ref,
    w3_ref,
    decay_ref,
    fb_ref,
    wout_ref,
    bout_ref,
    pos_ref,
    f_ref,
    ft_ref,
    out_ref,
    gtok_ref,
    gwin_ref,
    gwout_ref,
    oa_ref,
    ob_ref,
    oc_ref,
    w_in,
    w_out,
    fm,
    ft,
    halo,
    white,
    istd,
    normed,
    mx,
    oiv,
    dpr,
    a1,
    a2,
    xs,
    yo,
    yx,
    r1s,
    r1,
    r2,
    first,
    second,
    window,
    ksp,
    xsp,
    zs,
    es,
    product,
    pts,
    dsx,
    dms,
    nt,
    pt,
    dm,
    cot,
    core_send,
    core_recv,
    core_send_o,
    core_recv_o,
    own_o,
    outv,
    gtokv,
    z_recv,
    z_recv_o,
    last_send,
    last_recv,
    sa,
    sr,
    sf,
    sb,
    sp,
    vb,
    sg,
    sc,
    sq,
    st,
    sh,
    load_sem,
    in_sem,
    v_sem,
    halo_sem,
    a_sem,
    b_sem,
    c_sem,
    zed_sem,
    l_sem,
):
    s, b = lax.axis_index("seq"), lax.axis_index("batch")
    zed, core = s // 2, s % 2
    side, quarter = s // 4, s % 4
    pair, cross = zed // 2 * 2 + 1 - zed % 2, (zed + 2) % 4
    pair_cross = (pair + 2) % 4
    other = (zed * 2 + 1 - core, b)

    loads = [
        pltpu.make_async_copy(src, dst, load_sem.at[i])
        for i, (src, dst) in enumerate(((wout_ref, w_out), (f_ref, fm), (ft_ref, ft)))
    ]

    def load_in(g, i):
        cols = lanes(g * 1024 + (quarter + 2 + i) % 4 * 256, 256)
        return pltpu.make_async_copy(win_ref.at[:, cols], w_in.at[:, cols], in_sem.at[g, i])

    loads[0].start()
    for i in range(4):
        for g in range(3):
            load_in(g, i).start()
    loads[1].start()
    loads[2].start()

    def batch_peer(p):
        return (s, (b + p) % 4)

    def zed_peer(p):
        return (((zed + p) % 4) * 2 + core, b)

    barrier = pltpu.get_barrier_semaphore()
    for p in range(1, 8):
        pl.semaphore_signal(
            barrier, inc=1, device_id=((s + p) % 8, b), device_id_type=MESH
        )
    for p in range(1, 4):
        pl.semaphore_signal(barrier, inc=1, device_id=batch_peer(p), device_id_type=MESH)

    def remote(src, dst, sems, index, peer, start=True):
        copy = pltpu.make_async_remote_copy(
            src_ref=src,
            dst_ref=dst,
            send_sem=sems.at[(0,) + index],
            recv_sem=sems.at[(1,) + index],
            device_id=peer,
            device_id_type=MESH,
        )
        if start:
            copy.start()
        return copy

    gain, beta = gain_ref[...], beta_ref[...]

    def white_of(x):
        x = x.astype(f32)
        centered = x - jnp.mean(x, axis=-1, keepdims=True)
        inv = lax.rsqrt(jnp.mean(centered * centered, axis=-1, keepdims=True) + epsilon)
        return centered * inv, inv

    def norm_rows(i, _):
        q, r = i // 4, (i % 4) * 32
        rows = lanes(i * 32, 32)
        w, inv = white_of(tok_ref[q, lanes(r, 32)])
        white[rows] = w
        istd[rows] = jnp.broadcast_to(inv, (32, 128))
        normed[rows] = (w * gain + beta).astype(bf16)
        return 0

    lax.fori_loop(0, 8, norm_rows, 0)

    nt[b] = normed[0:256].T.reshape(4, 2, 128, 256)
    pl.semaphore_wait(barrier, 10)
    edge = remote(
        tok_ref.at[:, 112:128],
        halo,
        halo_sem,
        (0,),
        ((s + 1) % 8, b),
        start=False,
    )

    @pl.when(s < 7)
    def _():
        edge.start()

    moves = {}
    shards = (pair_cross, pair, cross, zed)
    x, y = b % 2, b // 2
    beside = (y * 2 + 1 - x, (1 - y) * 2 + x)
    for k in range(2):
        moves["n", k] = remote(nt.at[b], nt.at[b], b_sem, (0, k), (s, beside[k]))
    for k in range(2):
        moves["c", k] = remote(cot_ref, cot.at[b], b_sem, (1, k), (s, beside[k]))

    loads[0].wait()
    cot_here = cot_ref[...]
    cot[b] = cot_here

    def backproject(t, _):
        m = mm(cot_here, w_out[lanes(t * 256, 256)], NT).astype(bf16)
        for h in range(2):
            at = slice(h * 128, h * 128 + 128)
            dpr[2 * t + h] = jnp.concatenate([m[0:128, at], m[128:256, at]], axis=1)
        return 0

    lax.fori_loop(0, 4, backproject, 0)
    sa[...] = jnp.zeros(sa.shape, f32)
    sa[5:6, 2048:3072] = jnp.sum(cot_here.astype(f32), axis=0, keepdims=True)

    @pl.when(s == 0)
    def _():
        halo[...] = jnp.zeros_like(halo)

    @pl.when(s > 0)
    def _():
        edge.wait_recv()

    w, _inv = white_of(halo[...].reshape(32, 1024))
    normed[256:288] = (w * gain + beta).astype(bf16)

    def exchange(kind, p):
        to = (quarter + p) % 4
        target = side * 4 + to
        if kind == 0:
            src, dst = a1.at[to], xs.at[quarter]
        elif kind == 1:
            src, dst, target = a1.at[to], yx.at[quarter], (1 - side) * 4 + to
        elif kind == 2:
            src, dst = a2.at[to], yo.at[quarter]
        else:
            u = (kind - 3) % 2
            send, recv = ((r1s, r1), (a2, r2))[(kind - 3) // 2]
            src, dst = send.at[to, u], recv.at[2 * quarter + u]
        return remote(src, dst, a_sem, (kind, p), (target, b), start=False)

    def send_to(kind, to):
        p = (to - quarter + 4) % 4

        @pl.when(p != 0)
        def _():
            exchange(kind, p).start()

        @pl.when(p == 0)
        def _():
            if kind == 0:
                xs[quarter] = a1[quarter]
            elif kind == 2:
                yo[quarter] = a2[quarter]
            else:
                u = (kind - 3) % 2
                send, recv = ((r1s, r1), (a2, r2))[(kind - 3) // 2]
                recv[2 * quarter + u] = send[quarter, u]

    def sent_tiles(kind):
        for p in range(0 if kind == 1 else 1, 4):
            exchange(kind, p).wait_send()

    def wait_tiles(kind):
        for p in range(0 if kind == 1 else 1, 4):
            exchange(kind, p).wait_recv()


    def project(i, _):
        t = (quarter + 2 + i) % 4
        for g in range(3):
            load_in(g, i).wait()
            cols = lanes(g * 1024 + t * 256, 256)
            m = mm(normed[...], w_in[:, cols]) + bin_ref[:, cols]
            for h in range(2):
                at = slice(h * 128, h * 128 + 128)
                tile = 2 * t + h
                edge_rows = jnp.concatenate([m[264:272, at], m[280:288, at]], axis=1)
                mx[g, tile, 0:8] = jnp.where(s > 0, edge_rows, 0.0)
                mx[g, tile, 8:136] = jnp.concatenate([m[0:128, at], m[128:256, at]], axis=1)
        for h in range(2):
            tile = 2 * t + h
            got = []
            for g in range(3):
                cols = lanes(g * 1024 + tile * 128, 128)
                taps = sw_ref[:, cols]
                value = (
                    twice(taps[0:1]) * mx[g, tile, 8:136]
                    + twice(taps[1:2]) * mx[g, tile, 7:135]
                    + twice(taps[2:3]) * mx[g, tile, 6:134]
                    + twice(sb_ref[:, cols])
                )
                oiv[g, tile] = value
                got.append(value)
            gated = got[2] * got[1]
            d_summed = dpr[tile].astype(f32) * got[0]
            a1[t, h] = jnp.where(side == 0, gated, d_summed).astype(bf16)
            a2[t, h] = jnp.where(side == 0, d_summed, gated).astype(bf16)
        exchange(1, (t - quarter + 4) % 4).start()
        send_to(0, t)
        send_to(2, t)
        return 0

    lax.fori_loop(0, 4, project, 0)

    mine = lanes(quarter * 256, 256)
    pos = pos_ref[...]
    one, one_c = sin_cos(mm_full(pos, w1_ref[...]) + b1_ref[...])
    first[...] = jnp.concatenate([one, one_c], axis=1)
    two, two_c = sin_cos(mm_full(one, w2_ref[...]) + b2_ref[...])
    second[...] = jnp.concatenate([two, two_c], axis=1)
    fraction = lax.broadcasted_iota(jnp.int32, (1024, 256), 0).astype(f32) * (1.0 / 1024)
    wind = jnp.exp(-fraction * decay_ref[:, mine])
    window[...] = wind
    taps_bf = (mm_full(two, w3_ref[:, mine]) * wind).astype(bf16)
    loads[1].wait()

    def filter_rows(i, _):
        rows = lanes(i * 256, 256)
        ksp[rows] = mm(fm[rows], taps_bf)
        return 0

    lax.fori_loop(0, 8, filter_rows, 0)

    turn = jnp.where(side == 0, 1.0, -1.0)
    bias = fb_ref[:, mine]
    here = side * 512
    near, far_half = lanes(here, 512), lanes(512 - here, 512)
    wait_tiles(0)

    def inverse_to(kind, u, send, given):
        for k in range(2):
            y = mm(ft[lanes(here + k * 256, 256)], zs[...]) * (1.0 / 1024)
            for h in range(2):
                block = 2 * k + h
                scale = twice(bias[:, u * 128 : u * 128 + 128])
                value = y[h * 128 : h * 128 + 128] + scale * given[block, u].astype(f32)
                send[block, u] = value.astype(bf16)
        for k in range(4):
            send_to(kind + u, (quarter + 2 + k) % 4)

    for u in range(2):
        at = slice(u * 128, u * 128 + 128)
        x_u = xs[:, u].reshape(512, 256)

        def first_rows(i, _):
            lo, hi = lanes(i * 256, 256), lanes(1024 + i * 256, 256)
            xc, x_s = mm(fm[lo, near], x_u), mm(fm[hi, near], x_u)
            kc, ks = twice(ksp[lo, at]), twice(ksp[hi, at] * turn)
            xsp[u, lo] = xc.astype(bf16)
            xsp[u, hi] = x_s.astype(bf16)
            zs[lo] = (kc * xc - ks * x_s).astype(bf16)
            zs[hi] = (kc * x_s + ks * xc).astype(bf16)
            return 0

        lax.fori_loop(0, 4, first_rows, 0)
        if u == 0:
            loads[2].wait()
        inverse_to(3, u, r1s, xs)

    for k in range(2):
        by, on = beside[k], (s, beside[1 - k])
        moves["n", k].wait()
        part = nt.at[by, 2 * k : 2 * k + 2]
        moves["n", 2 + k] = remote(part, part, b_sem, (0, 2 + k), on)
    for k in range(2):
        by, on = beside[k], (s, beside[1 - k])
        moves["c", k].wait()
        part = cot.at[by, 128 * k : 128 * k + 128]
        moves["c", 2 + k] = remote(part, part, b_sem, (1, 2 + k), on)

    wait_tiles(2)
    wait_tiles(1)
    sent_tiles(2)
    for u in range(2):
        at = slice(u * 128, u * 128 + 128)
        y_near = yo[:, u].reshape(512, 256)
        y_far = yx[:, u].reshape(512, 256)

        def second_rows(i, _):
            lo, hi = lanes(i * 256, 256), lanes(1024 + i * 256, 256)
            nc, n_s = mm(fm[lo, near], y_near), mm(fm[hi, near], y_near)
            yc = nc + mm(fm[lo, far_half], y_far)
            y_s = n_s + mm(fm[hi, far_half], y_far)
            kc, ks = twice(ksp[lo, at]), twice(ksp[hi, at] * turn)
            zs[lo] = (kc * yc + ks * y_s).astype(bf16)
            zs[hi] = (kc * y_s - ks * yc).astype(bf16)
            pc = jnp.where(side == 0, nc, yc)
            p_s = jnp.where(side == 0, n_s, y_s)
            xc, x_s = xsp[u, lo].astype(f32), xsp[u, hi].astype(f32)
            ec, e_s = xc * pc + x_s * p_s, (xc * p_s - x_s * pc) * turn
            es[lo, at] = (ec[:, :128] + ec[:, 128:]).astype(bf16)
            es[hi, at] = (e_s[:, :128] + e_s[:, 128:]).astype(bf16)
            return 0

        lax.fori_loop(0, 4, second_rows, 0)
        inverse_to(5, u, a2, yo)

    def product_moves(half, p):
        return remote(
            pts.at[:, half, (b + p) % 4],
            pt.at[b, half],
            b_sem,
            (2 + half, p),
            batch_peer(p),
            start=False,
        )

    def mixed_moves(g, p):
        return remote(
            dms.at[g, (b + p) % 4], dm.at[g, b], b_sem, (4 + g, p), batch_peer(p), start=False
        )

    def edges_of(groups, index):
        return remote(
            dsx.at[groups, :, 0:8],
            dsx.at[groups, :, 128:136],
            halo_sem,
            (index,),
            ((s + 7) % 8, b),
            start=False,
        )

    def send_edges(groups, index):
        @pl.when(s > 0)
        def _():
            edges_of(groups, index).start()

    def wait_edges(groups, index):
        @pl.when(s == 7)
        def _():
            for g in range(groups.start, groups.stop):
                for j in range(8):
                    dsx[g, j, 128:136] = jnp.zeros((8, 256), f32)

        @pl.when(s < 7)
        def _():
            edges_of(groups, index).wait_recv()

    def column_sum(v):
        v = jnp.sum(v, axis=0, keepdims=True)
        return v[:, :128] + v[:, 128:]

    def short_sums(groups):
        def one_tile(j, _):
            for g in groups:
                wide = lanes(g * 1024 + j * 128, 128)
                value = dsx[g, j, 0:128]
                for k in range(3):
                    sa[1 + k : 2 + k, wide] = column_sum(value * mx[g, j, 8 - k : 136 - k])
                sa[4:5, wide] = column_sum(value)
            return 0

        lax.fori_loop(0, 8, one_tile, 0)

    def mixed_tile(g):
        def one_tile(j, _):
            q, cols = j // 2, lanes((j % 2) * 128, 128)
            wide = lanes(g * 1024 + j * 128, 128)
            taps = sw_ref[:, wide]
            value = (
                twice(taps[0:1]) * dsx[g, j, 0:128]
                + twice(taps[1:2]) * dsx[g, j, 1:129]
                + twice(taps[2:3]) * dsx[g, j, 2:130]
            ).astype(bf16)
            dms[g, q, 0:128, cols] = value[:, :128]
            dms[g, q, 128:256, cols] = value[:, 128:]
            sa[0:1, wide] = column_sum(value.astype(f32))
            return 0

        lax.fori_loop(0, 8, one_tile, 0)
        dm[g, b] = dms[g, b]

    def send_mixed(g):
        for p in (1, 2, 3):
            mixed_moves(g, p).start()

    def send_product():
        for half in range(2):
            for p in (1, 2, 3):
                product_moves(half, p).start()

    store_out = pltpu.make_async_copy(outv, out_ref, load_sem.at[3])

    def with_summed(back, early):
        def product_tile(j, _):
            value = back[j].astype(f32)
            made = (value * oiv[0, j]).astype(bf16)
            cols = lanes(j * 128, 128)
            product[0:128, cols] = made[:, :128]
            product[128:256, cols] = made[:, 128:]
            dsx[0, j, 0:128] = dpr[j].astype(f32) * value
            return 0

        lax.fori_loop(0, 8, product_tile, 0)
        send_edges(slice(0, 1), 1)
        pts[...] = product[...].T.reshape(4, 2, 4, 32, 256)
        send_product()
        for half in range(2):
            pt[b, half] = pts[:, half, b]
        short_sums((0,))

        @pl.when(s != 3)
        def _():
            wait_edges(slice(0, 1), 1)
            mixed_tile(0)
            if early:
                send_mixed(0)

        def out_cols(i, _):
            cols = lanes(i * 256, 256)
            r = mm(product[...], w_out[:, cols]) + bout_ref[:, cols]
            for q in range(2):
                rows = slice(q * 128, q * 128 + 128)
                outv[q, :, cols] = (tok_ref[q, :, cols].astype(f32) + r[rows]).astype(bf16)
            return 0

        lax.fori_loop(0, 4, out_cols, 0)
        store_out.start()

    def with_gated(back, early):
        def gate_tile(j, _):
            value = back[j].astype(f32)
            dsx[1, j, 0:128] = value * oiv[2, j]
            dsx[2, j, 0:128] = value * oiv[1, j]
            return 0

        lax.fori_loop(0, 8, gate_tile, 0)
        send_edges(slice(1, 3), 2)
        short_sums((1, 2))
        wait_edges(slice(1, 3), 2)
        mixed_tile(1)
        send_mixed(1)
        mixed_tile(2)
        if early:
            send_mixed(2)

        @pl.when(s == 3)
        def _():
            wait_edges(slice(0, 1), 1)
            mixed_tile(0)
            send_mixed(0)

    wait_tiles(3)
    wait_tiles(4)

    @pl.when(side == 0)
    def _():
        with_summed(r1, True)

    @pl.when(side == 1)
    def _():
        with_gated(r1, True)

    wait_tiles(5)
    wait_tiles(6)

    @pl.when(side == 0)
    def _():
        with_gated(r2, False)

    @pl.when(side == 1)
    def _():
        with_summed(r2, False)

    def normed_cols(i, _):
        at = lanes(i * 256, 256)
        total = jnp.zeros((256, 256), f32)
        for g in range(3):
            for q in range(4):
                c = g * 1024 + q * 256
                total += mm(dms[g, q], w_in[at, c : c + 256], NT)
        for q in range(2):
            gtokv[q, :, at] = total[q * 128 : q * 128 + 128]
        return 0

    lax.fori_loop(0, 4, normed_cols, 0)

    def token_rows(i, sums):
        q, r = i // 4, lanes((i % 4) * 32, 32)
        rows = lanes(i * 32, 32)
        d, w = gtokv[q, r], white[rows]
        dw = d * w
        d_white = d * gain
        grad = cot_ref[rows].astype(f32) + istd[rows, 0:1] * (
            d_white
            - jnp.mean(d_white, axis=-1, keepdims=True)
            - w * jnp.mean(d_white * w, axis=-1, keepdims=True)
        )
        gtokv[q, r] = grad
        return (
            sums[0] + jnp.sum(dw, axis=0, keepdims=True),
            sums[1] + jnp.sum(d, axis=0, keepdims=True),
        )

    zero = jnp.zeros((1, 1024), f32)
    sums = lax.fori_loop(0, 8, token_rows, (zero, zero))
    store_tok = pltpu.make_async_copy(gtokv, gtok_ref, load_sem.at[4])
    store_tok.start()
    sa[5:6, 0:1024] = sums[0]
    sa[5:6, 1024:2048] = sums[1]

    def part_out(half):
        total = jnp.zeros((128, 1024), f32)
        for i in range(4):
            total += mm(pt[i, half].reshape(128, 256), cot[i])
        return total

    def part_in(g, half):
        total = jnp.zeros((512, 256), f32)
        for i in range(4):
            total += mm(nt[i, :, half].reshape(512, 256), dm[g, i])
        return total

    def shard_of(g, z):
        return lanes(g * 512 + z * 128, 128)

    beside_z, across_z = (pair * 2 + core, b), (cross * 2 + core, b)

    def core_move(g):
        return remote(core_send.at[g], core_recv.at[g], c_sem, (g, 0), other, start=False)

    def zed_move(g, k):
        to = across_z if k == 2 else beside_z
        src = core_send.at[g, shards[k]]
        return remote(src, z_recv.at[g, k], zed_sem, (g, k), to, start=False)

    def core_move_o():
        return remote(core_send_o, core_recv_o, c_sem, (3, 0), other, start=False)

    def zed_move_o(k):
        to = across_z if k == 2 else beside_z
        src = core_send_o.at[32 * k : 32 * k + 32]
        return remote(src, z_recv_o.at[k], zed_sem, (3, k), to, start=False)

    def core_half_o():
        core_send_o[...] = part_out(1 - core).astype(bf16)
        core_move_o().start()

    def core_half(g):
        core_send[g] = part_in(g, 1 - core).astype(bf16).reshape(4, 128, 256)
        core_move(g).start()

    def zed_half_o():
        total = part_out(core)
        core_move_o().wait()
        own_o[...] = (total + core_recv_o[...].astype(f32)).reshape(4, 32, 1024)
        for k in range(2):
            core_send_o[32 * k : 32 * k + 32] = own_o[shards[k]].astype(bf16)
            zed_move_o(k).start()

    def zed_half(g):
        total = part_in(g, core)
        core_move(g).wait()
        ksp[512 * g : 512 * g + 512] = total + core_recv[g].astype(f32).reshape(512, 256)
        for k in range(2):
            core_send[g, shards[k]] = ksp[shard_of(g, shards[k])].astype(bf16)
            zed_move(g, k).start()

    def cross_half_o():
        zed_move_o(0).wait()
        core_send_o[64:96] = (own_o[cross] + z_recv_o[0].astype(f32)).astype(bf16)
        zed_move_o(2).start()

    def cross_half(g):
        zed_move(g, 0).wait()
        total = ksp[shard_of(g, cross)] + z_recv[g, 0].astype(f32)
        core_send[g, cross] = total.astype(bf16)
        zed_move(g, 2).start()

    def last_half(g):
        zed_move(g, 1).wait()
        zed_move(g, 2).wait()
        total = ksp[shard_of(g, zed)] + z_recv[g, 1].astype(f32) + z_recv[g, 2].astype(f32)
        last_send[g] = total.astype(bf16).reshape(4, 32, 256)
        for p in (1, 2, 3):
            moves["l", g, p] = remote(
                last_send.at[g, (b + p) % 4], last_recv.at[g, b], l_sem, (g, p), batch_peer(p)
            )
        last_recv[g, b] = last_send[g, b]

    def half_at(k):
        return lanes(k * 1536, 1536)

    @pl.when(side == 0)
    def _():
        send_mixed(2)

    @pl.when(side == 1)
    def _():
        send_mixed(0)

    def kernel_rows(i, _):
        rows = lanes(i * 256, 256)
        window[rows] = mm(ft[rows], es[...]) * (1.0 / 1024) * window[rows]
        return 0

    lax.fori_loop(0, 4, kernel_rows, 0)
    sc[...] = jnp.zeros(sc.shape, f32)
    direct = []
    for u in range(2):
        both = xs[:, u].astype(f32) * yo[:, u].astype(f32)
        direct.append(column_sum(both.reshape(512, 256)))
    direct = jnp.broadcast_to(jnp.concatenate(direct, axis=1), (64, 256)).T

    def low(v):
        return v.astype(bf16)

    d_shaped = low(window[...])
    sb[...] = jnp.concatenate([mm(d_shaped, low(second[:, 0:64]), TN), direct], axis=1)
    d_two = mm(d_shaped, low(w3_ref[:, mine]), NT) * second[:, 64:128]
    sc[0:64, 64:128] = mm(low(first[:, 0:64]), low(d_two), TN)
    sc[40:41, 0:64] = jnp.sum(d_two, axis=0, keepdims=True)
    d_one = mm(low(d_two), low(w2_ref[...]), NT) * first[:, 64:128]
    sc[0:33, 0:64] = mm(low(pos_ref[...]), low(d_one), TN)
    sc[41:42, 0:64] = jnp.sum(d_one, axis=0, keepdims=True)
    def rows_at(k):
        return pl.ds(pl.multiple_of(k * 32, 32), 32)

    def small_remote(src, dst, index, peer):
        return remote(src, dst, v_sem, (index,), peer)

    smalls = [
        small_remote(sa.at[:, half_at(1 - core)], sr.at[0], 0, other),
        small_remote(sc.at[rows_at(1 - core)], st.at[0], 1, other),
    ]
    for k in (2, 3):
        moves["n", k].wait()
        moves["c", k].wait()

    def arrived(g):
        for p in (1, 2, 3):
            mixed_moves(g, p).wait()

    def arrived_o():
        for p in (1, 2, 3):
            product_moves(0, p).wait()
            product_moves(1, p).wait()

    @pl.when(side == 0)
    def _():
        arrived_o()
        core_half_o()
        arrived(0)
        core_half(0)
        zed_half_o()
        zed_half(0)

    @pl.when(side == 1)
    def _():
        arrived(1)
        core_half(1)
        arrived(2)
        core_half(2)
        zed_half(1)
        zed_half(2)

    for move in smalls:
        move.wait()
    def fold(v):
        return jnp.concatenate([v[:, :768], v[:, 768:]], axis=0).astype(bf16)

    def total_of(array, first):
        return sum(array[first + i].astype(f32) for i in range(1, 4)) + array[first].astype(f32)

    vb[b] = fold(sa[:, half_at(core)] + sr[0])
    sq[b] = (sc[rows_at(core)] + st[0]).astype(bf16)
    sp[4:12] = sb[...].astype(bf16).reshape(8, 32, 128)
    for u in range(2):
        sp[2 * b + u + 12] = sp[4 + 4 * u + b]
    smalls = []
    for p in (1, 2, 3):
        smalls += [
            small_remote(vb.at[b], vb.at[b], 1 + p, batch_peer(p)),
            small_remote(sq.at[b], sq.at[b], 4 + p, batch_peer(p)),
            small_remote(sp.at[4 + (b + p) % 4], sp.at[12 + 2 * b], 7 + p, batch_peer(p)),
            small_remote(sp.at[8 + (b + p) % 4], sp.at[13 + 2 * b], 20 + p, batch_peer(p)),
        ]

    @pl.when(side == 0)
    def _():
        arrived(1)
        core_half(1)
        cross_half_o()
        cross_half(0)
        zed_half(1)

    @pl.when(side == 1)
    def _():
        arrived_o()
        core_half_o()
        cross_half(1)
        cross_half(2)
        zed_half_o()

    for move in smalls:
        move.wait()
    vb[4 + zed] = total_of(vb, 0).astype(bf16)
    sq[4 + zed] = total_of(sq, 0).astype(bf16)
    for u in range(2):
        part = sum(sp[12 + 2 * i + u].astype(f32) for i in range(4))
        sb[32 * u : 32 * u + 32] = part
        sp[u] = part.astype(bf16)
    smalls = [small_remote(sp.at[0:2], sp.at[2:4], 17, across_z)]
    for p in (1, 2, 3):
        smalls += [
            small_remote(vb.at[4 + zed], vb.at[4 + zed], 10 + p, zed_peer(p)),
            small_remote(sq.at[4 + zed], sq.at[4 + zed], 13 + p, zed_peer(p)),
        ]
    @pl.when(side == 0)
    def _():
        arrived(2)
        core_half(2)
        cross_half(1)
        zed_half(2)
        cross_half(2)

    @pl.when(side == 1)
    def _():
        arrived(0)
        core_half(0)
        cross_half_o()
        zed_half(0)
        cross_half(0)

    for move in smalls:
        move.wait()
    for u in range(2):
        sb[32 * u : 32 * u + 32] = sb[32 * u : 32 * u + 32] + sp[2 + u].astype(f32)
    folded = total_of(vb, 4)
    sf[...] = jnp.concatenate([folded[:8], folded[8:]], axis=1)
    sh[...] = total_of(sq, 4)
    smalls = [
        small_remote(sf, sr.at[1], 18, other),
        small_remote(sh, st.at[1], 19, other),
    ]
    owner = quarter * 2 + side

    def give():
        return remote(
            sb.at[lanes(side * 32, 32)], sg, v_sem, (24,), (owner, b), start=False
        )

    @pl.when(owner != s)
    def _():
        give().start()

    @pl.when(owner == s)
    def _():
        sg[...] = sb[lanes(side * 32, 32)]

    last_half(0)
    zed_move_o(1).wait()
    zed_move_o(2).wait()
    gwout_ref[...] = own_o[zed] + z_recv_o[1].astype(f32) + z_recv_o[2].astype(f32)
    last_half(1)
    last_half(2)
    for move in smalls:
        move.wait()
    oa_ref[:, half_at(core)] = sf[...]
    oa_ref[:, half_at(1 - core)] = sr[1]
    oc_ref[rows_at(core)] = sh[...]
    oc_ref[rows_at(1 - core)] = st[1]

    @pl.when(owner != s)
    def _():
        give().wait()

    ob_ref[...] = sg[...]
    for g in range(3):
        for p in (1, 2, 3):
            moves["l", g, p].wait()
        for i in range(4):
            c = g * 1024 + i * 256
            gwin_ref[:, c : c + 256] = last_recv[g, i].astype(f32)
    store_out.wait()
    store_tok.wait()
    for kind in (0, 1, 3, 4, 5, 6):
        sent_tiles(kind)

    @pl.when(s < 7)
    def _():
        edge.wait_send()

    @pl.when(s > 0)
    def _():
        edges_of(slice(0, 1), 1).wait_send()
        edges_of(slice(1, 3), 2).wait_send()


def whole(args, positions, matrix):
    vmem, anywhere = (pl.BlockSpec(memory_space=m) for m in (pltpu.VMEM, pl.ANY))
    dma = pltpu.SemaphoreType.DMA
    specs = [vmem] * 20
    for i in (4, 15, 18, 19):
        specs[i] = anywhere
    shape = jax.ShapeDtypeStruct

    def v(dtype, *dims):
        return pltpu.VMEM(dims, dtype)

    return pl.pallas_call(
        whole_kernel,
        out_shape=(
            shape((2, 128, 1024), bf16),
            shape((2, 128, 1024), f32),
            shape((32, 3072), f32),
            shape((32, 1024), f32),
            shape((8, 3072), f32),
            shape((32, 128), f32),
            shape((64, 128), f32),
        ),
        in_specs=specs,
        out_specs=(anywhere,) * 2 + (vmem,) * 5,
        scratch_shapes=[
            v(bf16, 1024, 3072),
            v(bf16, 1024, 1024),
            v(bf16, 2048, 1024),
            v(bf16, 1024, 2048),
            v(bf16, 2, 16, 1024),
            v(f32, 256, 1024),
            v(f32, 256, 128),
            v(bf16, 288, 1024),
            v(f32, 3, 8, 136, 256),
            v(f32, 3, 8, 128, 256),
            v(bf16, 8, 128, 256),
            v(bf16, 4, 2, 128, 256),
            v(bf16, 4, 2, 128, 256),
            v(bf16, 4, 2, 128, 256),
            v(bf16, 4, 2, 128, 256),
            v(bf16, 4, 2, 128, 256),
            v(bf16, 4, 2, 128, 256),
            v(bf16, 8, 128, 256),
            v(bf16, 8, 128, 256),
            v(f32, 1024, 128),
            v(f32, 1024, 128),
            v(f32, 1024, 256),
            v(f32, 2048, 256),
            v(bf16, 2, 2048, 256),
            v(bf16, 2048, 256),
            v(bf16, 2048, 256),
            v(bf16, 256, 1024),
            v(bf16, 4, 2, 4, 32, 256),
            v(f32, 3, 8, 136, 256),
            v(bf16, 3, 4, 256, 256),
            v(bf16, 4, 4, 2, 128, 256),
            v(bf16, 4, 2, 4, 32, 256),
            v(bf16, 3, 4, 256, 256),
            v(bf16, 4, 256, 1024),
            v(bf16, 3, 4, 128, 256),
            v(bf16, 3, 4, 128, 256),
            v(bf16, 128, 1024),
            v(bf16, 128, 1024),
            v(f32, 4, 32, 1024),
            v(bf16, 2, 128, 1024),
            v(f32, 2, 128, 1024),
            v(bf16, 3, 3, 128, 256),
            v(bf16, 3, 32, 1024),
            v(bf16, 3, 4, 32, 256),
            v(bf16, 3, 4, 32, 256),
            v(f32, 8, 3072),
            v(f32, 2, 8, 1536),
            v(f32, 8, 1536),
            v(f32, 256, 128),
            v(bf16, 20, 32, 128),
            v(bf16, 8, 16, 768),
            v(f32, 32, 128),
            v(f32, 64, 128),
            v(bf16, 8, 32, 128),
            v(f32, 2, 32, 128),
            v(f32, 32, 128),
            dma((5,)),
            dma((3, 4)),
            dma((2, 25)),
            dma((2, 3)),
            dma((2, 7, 4)),
            dma((2, 7, 4)),
            dma((2, 4, 4)),
            dma((2, 4, 4)),
            dma((2, 3, 4)),
        ],
        compiler_params=pltpu.CompilerParams(
            collective_id=0, has_side_effects=True, vmem_limit_bytes=63 * 1024 * 1024
        ),
    )(*args, positions, matrix, np.ascontiguousarray(matrix.T))


def settle_kernel(
    out_ref,
    gtok_ref,
    gwin_ref,
    gwout_ref,
    sa_ref,
    sb_ref,
    sc_ref,
    out,
    gtok,
    ln_gain,
    ln_bias,
    gwin,
    b_in,
    short_w,
    short_b,
    w_one,
    b_one,
    w_two,
    b_two,
    w_three,
    filt,
    gwout,
    b_out,
    sems,
):
    copies = [
        pltpu.make_async_copy(src, dst, sems.at[i])
        for i, (src, dst) in enumerate(
            ((out_ref, out), (gtok_ref, gtok), (gwin_ref, gwin), (gwout_ref, gwout))
        )
    ]
    for copy in copies:
        copy.start()
    b = lax.axis_index("batch")
    place = lax.axis_index("seq") * 4 + b
    sa = sa_ref[...]
    wide = pltpu.roll(sa, (32 - place) * 96, 1)
    b_in[...] = wide[0:1, :96]
    short_w[...] = wide[1:4, :96]
    short_b[...] = wide[4:5, :96]
    thin = pltpu.roll(sa, (96 - place) * 32, 1)
    ln_gain[...] = thin[5:6, 0:32]
    ln_bias[...] = thin[5:6, 1024:1056]
    b_out[...] = thin[5:6, 2048:2080]
    w_three[...] = sb_ref[:, 0:64]
    filt[...] = sb_ref[...].T[64:65, 0:32]
    w_one[...] = sc_ref[0:33, 0:64]
    w_two[...] = sc_ref[0:64, 64:128]
    b_two[...] = sc_ref[40:41, 0:64]
    b_one[...] = sc_ref[41:42, 0:64]
    for copy in copies:
        copy.wait()


def settle(parts):
    vmem, anywhere = (pl.BlockSpec(memory_space=m) for m in (pltpu.VMEM, pl.ANY))
    sizes = (
        (2, 128, 1024),
        (2, 128, 1024),
        (1, 32),
        (1, 32),
        (32, 3072),
        (1, 96),
        (3, 96),
        (1, 96),
        (33, 64),
        (1, 64),
        (64, 64),
        (1, 64),
        (32, 64),
        (1, 32),
        (32, 1024),
        (1, 32),
    )
    flat = (2, 3, 5, 7, 9, 11, 13, 15)
    outs = pl.pallas_call(
        settle_kernel,
        out_shape=tuple(
            jax.ShapeDtypeStruct(size, f32 if i else bf16) for i, size in enumerate(sizes)
        ),
        in_specs=[anywhere] * 4 + [vmem] * 3,
        out_specs=(vmem,) * 16,
        scratch_shapes=[pltpu.SemaphoreType.DMA((4,))],
    )(*parts)
    return tuple(
        o.reshape(-1) if i in flat else o.T if i == 12 else o for i, o in enumerate(outs)
    )


def local_small(*args):
    cotangent = args[1]
    vectors = {2, 3, 5, 7, 9, 11, 13, 14, 16}
    given = [a.reshape(1, -1) if i in vectors else a for i, a in enumerate(args)]
    given[1] = cotangent.reshape(256, 1024)
    return settle(whole(given, position_features(1024, args[8].shape[0]), dft_matrix(1024)))


def solution(mesh):
    tokens_spec = P("batch", "seq", None)
    both = ("seq", "batch")
    in_specs = (tokens_spec, tokens_spec) + (P(),) * 15
    out_specs = (
        tokens_spec,
        tokens_spec,
        P(both),
        P(both),
        P(both, None),
        P(both),
        P(None, both),
        P(both),
        P(),
        P(),
        P(),
        P(),
        P(None, both),
        P(both),
        P(both, None),
        P(both),
    )

    def per_device(*args):
        tokens, w_one = args[0], args[8]
        sizes = (mesh.shape["seq"], mesh.shape["batch"]) + tokens.shape + w_one.shape
        fits = sizes == (8, 4, 2, 128, 1024, 33, 64)
        return (local_small if fits else local)(*args)

    return jax.shard_map(per_device, mesh=mesh, in_specs=in_specs, out_specs=out_specs, check_vma=False)
```
